32 devices in a mesh: tower: 2 (over x), batch: 16 (over z, y, core).
Axes of the slice: x: 2, y: 2, z: 4, core: 2. Of those that a mesh axis runs over, the one named last changes fastest.
Arguments:
- tokens: bfloat16 [2, 64, 256, 768], P('tower', 'batch'), may hold values from -6 to 6
- lengths: int32 [2, 64], P('tower', 'batch'), may hold values from 8 to 256, as said below
- positives: int32 [64], P('batch'), may hold values from 0 to 63, each once
- datasets: int32 [64], P('batch'), may hold values from 0 to 3
- w_qkv: bfloat16 [2, 768, 2304], P('tower'), may hold values from -0.21875 to 0.21875
- w_attn_out: bfloat16 [2, 768, 768], P('tower'), may hold values from -0.625 to 0.625
- w_ffn_in: bfloat16 [2, 768, 3072], P('tower'), may hold values from -0.21875 to 0.21875
- w_ffn_out: bfloat16 [2, 3072, 768], P('tower'), may hold values from -0.109375 to 0.109375
- b_ffn_in: float32 [2, 3072], P('tower'), may hold values from -1.2 to 1.2
- biases: float32 [2, 6, 768], P('tower'), may hold values from -1.2 to 1.2
- gains: float32 [2, 2, 768], P('tower'), may hold values from 0.5 to 1.5
Outputs:
- pooled_vectors: float32 [2, 64, 768], P('tower', 'batch')
- grad_tokens: float32 [2, 64, 256, 768], P('tower', 'batch')
- grad_w_qkv: float32 [2, 768, 2304], P('tower', 'batch')
- grad_w_attn_out: float32 [2, 768, 768], P('tower', 'batch')
- grad_w_ffn_in: float32 [2, 768, 3072], P('tower', 'batch')
- grad_w_ffn_out: float32 [2, 3072, 768], P('tower', 'batch')
- grad_b_ffn_in: float32 [2, 3072], P('tower', 'batch')
- grad_biases: float32 [2, 6, 768], P('tower', None, 'batch')
- grad_gains: float32 [2, 2, 768], P('tower', None, 'batch')
The draws below stay inside these ranges and needn't reach their ends.
Inputs may be any that keep to these rules, and one draw needn't show every extreme that they name: Row 0 holds question lengths, at most 64 and one exactly 64; row 1 holds passage lengths, one exactly 256.
All inputs are finite; a program needn't handle non-finite values.
Results may differ from the reference program's by a relative error of at most 0.02.
Values may be sent and summed in bfloat16 or wider, within the bound.
A program may use at most 192 MiB of HBM per device.

```python
import jax
import jax.numpy as jnp
from jax import lax

D = 768
HEADS = 12
HEAD = 64
FF = 3072
LEN = 256
QLEN = 64
SEQS = 64


def draw_lengths(key, part):
    key = jax.random.fold_in(key, 11)
    key_short, key_long, key_qtop, key_ptop = jax.random.split(key, 4)
    short_rows = jax.random.randint(key_short, (SEQS,), max(1, QLEN // 8), QLEN + 1)
    long_rows = jax.random.randint(key_long, (SEQS,), max(1, LEN // 8), LEN + 1)
    short_top = jax.random.randint(key_qtop, (), 0, SEQS)
    long_top = jax.random.randint(key_ptop, (), 0, SEQS)
    places = jnp.arange(SEQS)
    short_rows = jnp.where(places == short_top, QLEN, short_rows)
    long_rows = jnp.where(places == long_top, LEN, long_rows)
    return jnp.stack([short_rows, long_rows]).astype(jnp.int32)


def place_ends(result, own_key, smallest, high):
    shape = result.shape
    spot = [jax.random.randint(jax.random.fold_in(own_key, axis), (), 0, shape[axis]) for axis in range(len(shape))]
    result = result.at[tuple(spot)].set(smallest)
    longest = shape.index(max(shape))
    spot[longest] = (spot[longest] + 1) % shape[longest]
    return result.at[tuple(spot)].set(high)


def steps_of(rng, extent, cuts, least, top_value):
    def one(position, shards_of):
        heights = jax.random.uniform(jax.random.fold_in(jax.random.fold_in(rng, 6), position), (shards_of,), jnp.float32, least / len(cuts), top_value / len(cuts))
        return jnp.repeat(jnp.exp(heights), extent[position] // shards_of).reshape((-1,) + (1,) * (len(extent) - position - 1))

    level = one(*cuts[0])
    for cut in cuts[1:]:
        level = level * one(*cut)
    return level


def bell_draw(key, dims, deviation, bound, cuts=(), held_as=jnp.bfloat16):
    entries = deviation * jax.random.normal(key, dims, jnp.float32)
    if cuts:
        entries = entries * steps_of(key, dims, cuts, -0.22, 0.18)
    return jnp.clip(entries, -bound, bound).astype(held_as)


def setup_inputs(seed: int = 0) -> dict:
    streams_of = jax.random.split(jax.random.key(seed), 12)
    return {
        "tokens": bell_draw(streams_of[0], (2, SEQS, LEN, D), 1.0, 6.0, ((0, 2), (1, 16))),
        "lengths": draw_lengths(jax.random.fold_in(streams_of[11], 71), 0),
        "positives": jax.random.permutation(streams_of[2], SEQS).astype(jnp.int32),
        "datasets": place_ends(jax.random.randint(streams_of[3], (SEQS,), 0, 4), jax.random.fold_in(streams_of[3], 1), 0, 3).astype(jnp.int32),
        "w_qkv": bell_draw(streams_of[4], (2, D, 3 * D), D ** -0.5, 0.21875, ((0, 2),)),
        "w_attn_out": bell_draw(streams_of[5], (2, D, D), (D // 8) ** -0.5, 0.625, ((0, 2),)),
        "w_ffn_in": bell_draw(streams_of[6], (2, D, FF), D ** -0.5, 0.21875, ((0, 2),)),
        "w_ffn_out": bell_draw(streams_of[7], (2, FF, D), FF ** -0.5, 0.109375, ((0, 2),)),
        "b_ffn_in": bell_draw(streams_of[8], (2, FF), 0.2, 1.2, ((0, 2),), jnp.float32),
        "biases": bell_draw(streams_of[9], (2, 6, D), 0.2, 1.2, ((0, 2),), jnp.float32),
        "gains": jnp.clip(1.0 + 0.1 * jax.random.normal(streams_of[10], (2, 2, D), jnp.float32), 0.5, 1.5),
    }


@jax.custom_vjp
def low(v):
    return lax.optimization_barrier(v.astype(jnp.bfloat16)).astype(jnp.float32)

@jax.custom_vjp
def low_back(v):
    return v

def low_keep(v):
    return (low(v), None)

def low_pass(kept, grad):
    return (grad,)

def back_keep(v):
    return (v, None)

def back_low(kept, grad):
    return (low(grad),)
low.defvjp(low_keep, low_pass)
low_back.defvjp(back_keep, back_low)
EPS = 1e-12
SCALE = 4.0
HIGH = lax.Precision.HIGHEST

def rounded(value):
    return low_back(low(value))

def matmul(left, right):
    return jnp.einsum('bld,de->ble', left, right, precision=HIGH)

def layer_norm(total, gain, shift):
    mean = lax.optimization_barrier(jnp.mean(total, axis=-1, keepdims=True))
    centered = total - mean
    inverse = lax.rsqrt(lax.optimization_barrier(jnp.mean(centered * centered, axis=-1, keepdims=True)) + EPS)
    return centered * inverse * gain + shift

def encode(inputs, lens, weight_qkv, weight_attn, weight_in, weight_out, bias_in, vectors, scales):
    batch_rows = inputs.shape[0]
    keep = lax.broadcasted_iota(jnp.int32, (batch_rows, LEN), 1) < lens[:, None]
    projected = matmul(low(inputs), weight_qkv)
    shape_heads = (batch_rows, LEN, HEADS, HEAD)
    query = rounded(projected[..., :D] + vectors[0]).reshape(shape_heads)
    key_rows = rounded(projected[..., D:2 * D]).reshape(shape_heads)
    value = rounded(projected[..., 2 * D:] + vectors[1]).reshape(shape_heads)
    scores = low_back(jnp.einsum('bqhe,bkhe->bhqk', query, key_rows, precision=HIGH) * 0.125)
    scores = jnp.where(keep[:, None, None, :], scores, -1000000000.0)
    probs = jnp.exp(scores - jax.nn.logsumexp(scores, axis=-1, keepdims=True))
    context = jnp.einsum('bhqk,bkhe->bqhe', low(probs), value, precision=HIGH)
    context = rounded(context.reshape(batch_rows, LEN, D))
    attended = low_back(matmul(context, weight_attn) + vectors[2])
    first_norm = layer_norm(inputs + attended, scales[0], vectors[3])
    hidden_pre = low_back(matmul(low(first_norm), weight_in) + bias_in)
    hidden = low(jax.nn.gelu(hidden_pre, approximate=False))
    branch = low_back(matmul(hidden, weight_out) + vectors[4])
    output = layer_norm(first_norm + branch, scales[1], vectors[5])
    keep_float = keep.astype(jnp.float32)
    return lax.optimization_barrier(jnp.sum(output * keep_float[..., None], axis=1)) / lens.astype(jnp.float32)[:, None]

def reference(tokens, lengths, positives, datasets, w_qkv, w_attn_out, w_ffn_in, w_ffn_out, b_ffn_in, biases, gains):
    floats = tuple((item.astype(jnp.float32) for item in (tokens, w_qkv, w_attn_out, w_ffn_in, w_ffn_out, b_ffn_in, biases, gains)))
    blocks_of = 16 if SEQS % 16 == 0 else SEQS

    def tower_pool(tower, every_token, weight_qkv, weight_attn, weight_in, weight_out, bias_in, vectors, scales):
        inputs = every_token[tower].reshape(SEQS // blocks_of, blocks_of, LEN, D)
        lens = lengths[tower].reshape(SEQS // blocks_of, blocks_of)

        def one_block(packed):
            return encode(packed[0], packed[1], weight_qkv[tower], weight_attn[tower], weight_in[tower], weight_out[tower], bias_in[tower], vectors[tower], scales[tower])
        return lax.map(jax.checkpoint(one_block), (inputs, lens)).reshape(SEQS, D)

    def forward(*items):
        pooled_question = tower_pool(0, *items)
        pooled_passage = tower_pool(1, *items)
        question_low = rounded(pooled_question)
        passage_low = low(pooled_passage)
        logits = jnp.dot(question_low, passage_low.T, precision=HIGH) * SCALE
        query_set = datasets[positives]
        allowed = datasets[None, :] == query_set[:, None]
        masked = jnp.where(allowed, logits, -1000000000.0)
        total = jax.nn.logsumexp(masked, axis=1)
        picked = jnp.take_along_axis(masked, positives[:, None], axis=1)[:, 0]
        return (jnp.sum(total - picked), jnp.stack([pooled_question, pooled_passage]))
    loss, pullback, pooled = jax.vjp(forward, *floats, has_aux=True)
    grads = pullback(jnp.ones((), jnp.float32))
    return (pooled, grads[0], grads[1], grads[2], grads[3], grads[4], grads[5], grads[6], grads[7])
```

```python
from functools import partial

import jax
import jax.numpy as jnp
from jax import lax
from jax.experimental import pallas as pl
from jax.experimental.pallas import tpu as pltpu
from jax.sharding import PartitionSpec as P

HEADS = 12
EPS = 1e-12
SCALE = 4.0
HIGH = lax.Precision.HIGHEST
MESH = pl.DeviceIdType.MESH
NEG = -1000000000.0
PIECES = 3
CHUNK = 1536


def product(left, right):
    return jnp.dot(left, right, preferred_element_type=jnp.float32)


def transposed_left(left, right):
    return lax.dot_general(
        left, right, (((0,), (0,)), ((), ())), preferred_element_type=jnp.float32
    )


def transposed_right(left, right):
    return lax.dot_general(
        left, right, (((1,), (1,)), ((), ())), preferred_element_type=jnp.float32
    )


def norm_forward(total, gain, shift):
    mean = jnp.mean(total, axis=-1, keepdims=True)
    centered = total - mean
    inverse = lax.rsqrt(jnp.mean(centered * centered, axis=-1, keepdims=True) + EPS)
    normed = centered * inverse
    return (normed * gain + shift, normed, inverse)


def norm_backward(grad, normed, inverse, gain):
    scaled = grad * gain
    first_mean = jnp.mean(scaled, axis=-1, keepdims=True)
    second_mean = jnp.mean(scaled * normed, axis=-1, keepdims=True)
    d_total = inverse * (scaled - first_mean - normed * second_mean)
    return (d_total, jnp.sum(grad * normed, axis=0), jnp.sum(grad, axis=0))


def scores_of(query_heads, key_heads, keep):
    raw = (
        jnp.einsum("sqhe,skhe->shqk", query_heads, key_heads, preferred_element_type=jnp.float32)
        * 0.125
    )
    return jnp.where(keep[:, None, None, :], raw, NEG)


def select(condition):
    return jnp.where(condition, 1.0, 0.0)


def loss_kernel(n, pooled_ref, extra_ref, out_ref, mine, everyone, send_sem, recv_sem):
    tower, me = lax.axis_index("tower"), lax.axis_index("batch")
    flat = tower * n + me
    total = 2 * n

    barrier = pltpu.get_barrier_semaphore()

    @pl.loop(1, total)
    def _(step):
        other = lax.rem(flat + step, total)
        pl.semaphore_signal(
            barrier, inc=1, device_id=(other // n, lax.rem(other, n)), device_id_type=MESH
        )

    pooled = pooled_ref[...]
    block = jnp.concatenate(
        [pooled[:, 0:256], pooled[:, 256:512], pooled[:, 512:768], extra_ref[...]], axis=0
    ).astype(jnp.bfloat16)
    mine[...] = block
    everyone[flat] = block
    pl.semaphore_wait(barrier, total - 1)

    def copy_to(step):
        other = lax.rem(flat + step, total)
        return pltpu.make_async_remote_copy(
            src_ref=mine,
            dst_ref=everyone.at[flat],
            send_sem=send_sem.at[step],
            recv_sem=recv_sem.at[step],
            device_id=(other // n, lax.rem(other, n)),
            device_id_type=MESH,
        )

    @pl.loop(1, total)
    def _(step):
        copy_to(step).start()

    @pl.loop(1, total)
    def _(step):
        copy_to(step).wait()

    seqs = 4 * n
    packed = everyone[...]
    questions = packed[:n].reshape(16 * n, 256)
    passages = packed[n:].reshape(16 * n, 256)
    rows = lax.broadcasted_iota(jnp.int32, (seqs, 16 * n), 0)
    places = lax.broadcasted_iota(jnp.int32, (seqs, 16 * n), 1)
    owner, lane = rows // 4, lax.rem(rows, 4)

    def picked(values, row):
        return product(select(places == owner * 16 + row).astype(jnp.bfloat16), values)

    def whole(values):
        parts = [
            product(select(places == owner * 16 + 4 * part + lane).astype(jnp.bfloat16), values)
            for part in range(3)
        ]
        return jnp.concatenate(parts, axis=1)

    column_lane = lax.broadcasted_iota(jnp.int32, (seqs, 256), 1)
    column_want = lax.rem(lax.broadcasted_iota(jnp.int32, (seqs, 256), 0), 4)

    def column(row):
        return jnp.sum(
            jnp.where(column_lane == column_want, picked(passages, row), 0.0), axis=1, keepdims=True
        )

    question_float, passage_float = whole(questions), whole(passages)
    question_low = question_float.astype(jnp.bfloat16)
    passage_low = passage_float.astype(jnp.bfloat16)
    positives, sets = column(12), column(13)
    first = lax.broadcasted_iota(jnp.int32, (seqs, seqs), 0)
    second = lax.broadcasted_iota(jnp.int32, (seqs, seqs), 1)
    set_row = jnp.sum(jnp.where(first == second, sets, 0.0), axis=0, keepdims=True)
    chosen = second == positives.astype(jnp.int32)
    query_set = jnp.sum(jnp.where(chosen, set_row, 0.0), axis=1, keepdims=True)
    logits = transposed_right(question_low, passage_low) * SCALE
    masked = jnp.where(set_row == query_set, logits, NEG)
    top = jnp.max(masked, axis=1, keepdims=True)
    weights = jnp.exp(masked - top)
    softmax = weights / jnp.sum(weights, axis=1, keepdims=True)
    d_logits = (softmax - select(chosen)) * SCALE

    mine_row = lax.broadcasted_iota(jnp.int32, (8, seqs), 0)
    mine_column = lax.broadcasted_iota(jnp.int32, (8, seqs), 1)
    own = select((mine_column == me * 4 + mine_row) & (mine_row < 4))

    @pl.when(tower == 0)
    def _():
        terms = jnp.dot(own, d_logits, precision=HIGH, preferred_element_type=jnp.float32)
        grad = jnp.dot(terms, passage_float, precision=HIGH, preferred_element_type=jnp.float32)
        out_ref[...] = grad.astype(jnp.bfloat16).astype(jnp.float32)

    @pl.when(tower == 1)
    def _():
        terms = lax.dot_general(
            own, d_logits, (((1,), (1,)), ((), ())), precision=HIGH, preferred_element_type=jnp.float32
        )
        out_ref[...] = jnp.dot(terms, question_float, precision=HIGH, preferred_element_type=jnp.float32)


def loss_gradient(pooled, positives, datasets, n):
    extra = jnp.stack([positives.astype(jnp.float32), datasets.astype(jnp.float32)])
    extra = jnp.pad(extra, ((0, 2), (0, 252)))
    grad = pl.pallas_call(
        partial(loss_kernel, n),
        out_shape=jax.ShapeDtypeStruct((8, pooled.shape[1]), jnp.float32),
        in_specs=[pl.BlockSpec(memory_space=pltpu.VMEM)] * 2,
        out_specs=pl.BlockSpec(memory_space=pltpu.VMEM),
        scratch_shapes=[
            pltpu.VMEM((16, 256), jnp.bfloat16),
            pltpu.VMEM((2 * n, 16, 256), jnp.bfloat16),
            pltpu.SemaphoreType.DMA((2 * n,)),
            pltpu.SemaphoreType.DMA((2 * n,)),
        ],
        compiler_params=pltpu.CompilerParams(collective_id=0, has_side_effects=True),
        name="loss",
    )(pooled, extra)
    return grad[:4]


def ring_place(chip, chips):
    half, y = chip // 2, lax.rem(chip, 2)
    return jnp.where(y == 0, half, chips - 1 - half)


def ring_chip(place, chips):
    return jnp.where(place < chips // 2, place * 2, (chips - 1 - place) * 2 + 1)


def sum_kernel(
    n, grads, small_ref, out_out, out_in, out_attn, out_qkv, out_small,
    sibling_got, sending, ring_got, small_got,
    pair_send, pair_recv, ring_send, ring_recv, small_send, small_recv,
):
    chips = n // 2
    tower, me = lax.axis_index("tower"), lax.axis_index("batch")
    chip, core = me // 2, lax.rem(me, 2)
    place = ring_place(chip, chips)
    sibling = (tower, me + 1 - 2 * core)
    right = (tower, ring_chip(lax.rem(place + 1, chips), chips) * 2 + core)
    left = (tower, ring_chip(lax.rem(place + chips - 1, chips), chips) * 2 + core)

    barrier = pltpu.get_barrier_semaphore()

    @pl.loop(1, n)
    def _(step):
        pl.semaphore_signal(
            barrier, inc=1, device_id=(tower, lax.rem(me + step, n)), device_id_type=MESH
        )

    pl.semaphore_wait(barrier, n - 1)

    def small_copy(step):
        other = lax.rem(me + step, n)
        return pltpu.make_async_remote_copy(
            src_ref=small_ref.at[other], dst_ref=small_got.at[step],
            send_sem=small_send.at[step], recv_sem=small_recv.at[step],
            device_id=(tower, other), device_id_type=MESH,
        )

    def pair_copy(piece, step, way):
        target = ring_chip(target_place(step, way), chips)
        return pltpu.make_async_remote_copy(
            src_ref=grads.at[piece, target, 1 - core, way],
            dst_ref=sibling_got.at[piece, step, way],
            send_sem=pair_send.at[piece, step, way], recv_sem=pair_recv.at[piece, step, way],
            device_id=sibling, device_id_type=MESH,
        )

    def target_place(step, way):
        return lax.rem(place + chips - 1 - step, chips) if way == 0 else lax.rem(place + 1 + step, chips)

    def ring_copy(piece, step, way):
        return pltpu.make_async_remote_copy(
            src_ref=sending.at[piece, step, way], dst_ref=ring_got.at[piece, step, way],
            send_sem=ring_send.at[piece, step, way], recv_sem=ring_recv.at[piece, step, way],
            device_id=right if way == 0 else left, device_id_type=MESH,
        )

    @pl.loop(0, chips)
    def _(step):
        for piece in range(PIECES):
            for way in range(2):
                pair_copy(piece, step, way).start()

    @pl.loop(1, n)
    def _(step):
        small_copy(step).start()

    def local(piece, step, way):
        pair_copy(piece, step, way).wait_recv()
        target = ring_chip(target_place(step, way), chips)
        return (
            grads[piece, target, core, way].astype(jnp.float32)
            + sibling_got[piece, step, way].astype(jnp.float32)
        )

    for piece in range(PIECES):
        for way in range(2):
            sending[piece, 0, way] = local(piece, 0, way).astype(jnp.bfloat16)
            ring_copy(piece, 0, way).start()

    @pl.loop(1, chips - 1)
    def _(step):
        for piece in range(PIECES):
            for way in range(2):
                base = local(piece, step, way)
                ring_copy(piece, step - 1, way).wait_recv()
                sending[piece, step, way] = (
                    base + ring_got[piece, step - 1, way].astype(jnp.float32)
                ).astype(jnp.bfloat16)
                ring_copy(piece, step, way).start()

    for piece in range(PIECES):
        for way in range(2):
            total = local(piece, chips - 1, way)
            ring_copy(piece, chips - 2, way).wait_recv()
            total = total + ring_got[piece, chips - 2, way].astype(jnp.float32)
            if piece == 0:
                for part in range(4):
                    out_out[48 * part:48 * (part + 1), 384 * way:384 * (way + 1)] = total[
                        :, 384 * part:384 * (part + 1)]
            elif piece == 1:
                out_in[:, CHUNK * way:CHUNK * (way + 1)] = total
            else:
                out_attn[:, 384 * way:384 * (way + 1)] = total[:, :384]
                out_qkv[:, 1152 * way:1152 * (way + 1)] = total[:, 384:]

    out_small[...] = small_ref[me]

    @pl.loop(1, n)
    def _(step):
        small_copy(step).wait()
        out_small[...] += small_got[step]

    @pl.loop(0, chips)
    def _(step):
        for piece in range(PIECES):
            for way in range(2):
                pair_copy(piece, step, way).wait_send()

    @pl.loop(0, chips - 1)
    def _(step):
        for piece in range(PIECES):
            for way in range(2):
                ring_copy(piece, step, way).wait_send()


def summed_over_batch(packed, small, n):
    chips = n // 2
    block = (48, CHUNK)
    f32 = jnp.float32
    return pl.pallas_call(
        partial(sum_kernel, n),
        out_shape=[
            jax.ShapeDtypeStruct((192, 768), f32),
            jax.ShapeDtypeStruct((48, 3072), f32),
            jax.ShapeDtypeStruct((48, 768), f32),
            jax.ShapeDtypeStruct((48, 2304), f32),
            jax.ShapeDtypeStruct((8, 128), f32),
        ],
        in_specs=[pl.BlockSpec(memory_space=pltpu.VMEM)] * 2,
        out_specs=[pl.BlockSpec(memory_space=pltpu.VMEM)] * 5,
        scratch_shapes=[
            pltpu.VMEM((PIECES, chips, 2) + block, jnp.bfloat16),
            pltpu.VMEM((PIECES, chips - 1, 2) + block, jnp.bfloat16),
            pltpu.VMEM((PIECES, chips - 1, 2) + block, jnp.bfloat16),
            pltpu.VMEM((n, 8, 128), f32),
            pltpu.SemaphoreType.DMA((PIECES, chips, 2)),
            pltpu.SemaphoreType.DMA((PIECES, chips, 2)),
            pltpu.SemaphoreType.DMA((PIECES, chips - 1, 2)),
            pltpu.SemaphoreType.DMA((PIECES, chips - 1, 2)),
            pltpu.SemaphoreType.DMA((n,)),
            pltpu.SemaphoreType.DMA((n,)),
        ],
        compiler_params=pltpu.CompilerParams(
            collective_id=1, has_side_effects=True, vmem_limit_bytes=56 * 2**20
        ),
        name="gradient_sum",
    )(packed, small)


def packed_of(g_out, g_in, g_attn, g_qkv, n):
    low = jnp.bfloat16
    rows = 768 // n
    piece_out = g_out.astype(low).reshape(n, 4, rows, 2, 384).transpose(0, 3, 2, 1, 4).reshape(n, 2, rows, CHUNK)
    piece_in = g_in.astype(low).reshape(n, rows, 2, CHUNK).transpose(0, 2, 1, 3)
    piece_rest = jnp.concatenate(
        [g_attn.astype(low).reshape(n, rows, 2, 384), g_qkv.astype(low).reshape(n, rows, 2, 1152)], axis=3
    ).transpose(0, 2, 1, 3)
    return jnp.stack([piece_out, piece_in, piece_rest]).reshape(PIECES, n // 2, 2, 2, rows, CHUNK)


def small_of(g_bias_in, g_vectors, g_scales, n):
    parts = [
        g_bias_in.reshape(n, -1),
        g_vectors.reshape(6, n, -1).transpose(1, 0, 2).reshape(n, -1),
        g_scales.reshape(2, n, -1).transpose(1, 0, 2).reshape(n, -1),
    ]
    small = jnp.concatenate(parts, axis=1)
    return jnp.pad(small, ((0, 0), (0, 1024 - small.shape[1]))).reshape(n, 8, 128)


def from_behind(value, axis, steps):
    count = lax.axis_size(axis)
    leading, last = (max(0, -steps), min(count, count - steps))
    return lax.ppermute(value, axis, [(source, source + steps) for source in range(leading, last)])


def loss_gradient_plain(pooled, positives, datasets):
    seq_count = pooled.shape[0]
    mine = pooled.astype(jnp.bfloat16)
    questions = from_behind(mine, "tower", 1)
    everyone, every_set = (
        lax.all_gather(mine, "batch", axis=0, tiled=True),
        lax.all_gather(datasets.astype(jnp.bfloat16), "batch", axis=0, tiled=True),
    )
    total_seqs = everyone.shape[0]
    columns = lax.broadcasted_iota(jnp.int32, (seq_count, total_seqs), 1)
    chosen = columns == positives[:, None]
    set_row = every_set.astype(jnp.float32)[None, :]
    query_set = jnp.sum(jnp.where(chosen, set_row, 0.0), axis=1, keepdims=True)
    allowed = set_row == query_set
    question_float = questions.astype(jnp.float32)
    everyone_float = everyone.astype(jnp.float32)
    logits = jnp.dot(question_float, everyone_float.T, precision=HIGH) * SCALE
    masked = jnp.where(allowed, logits, NEG)
    softmax_rows = jnp.exp(masked - jax.nn.logsumexp(masked, axis=1, keepdims=True))
    d_logits = (softmax_rows - chosen.astype(jnp.float32)) * SCALE
    d_questions = jnp.dot(d_logits, everyone_float, precision=HIGH).astype(jnp.bfloat16)
    passage_terms = jnp.dot(d_logits.T, question_float, precision=HIGH)
    d_passages = lax.psum_scatter(passage_terms, "batch", scatter_dimension=0, tiled=True)
    returned = from_behind(d_questions, "tower", -1)
    is_passage = lax.axis_index("tower") == 1
    return jnp.where(is_passage, d_passages, returned.astype(jnp.float32))


def per_device(
    n, direct,
    tokens, lengths, positives, datasets, w_qkv, w_attn_out, w_ffn_in, w_ffn_out, b_ffn_in, biases, gains,
):
    seq_count, seq_len, width = (tokens.shape[1], tokens.shape[2], tokens.shape[3])
    head_size = width // HEADS
    rows = seq_count * seq_len
    inputs = tokens[0].reshape(rows, width)
    lens = lengths[0]
    weight_qkv = w_qkv[0]
    weight_attn = w_attn_out[0]
    weight_in = w_ffn_in[0]
    weight_out = w_ffn_out[0]
    bias_in = b_ffn_in[0]
    vectors = biases[0]
    scales = gains[0]
    positions = lax.broadcasted_iota(jnp.int32, (seq_count, seq_len), 1)
    keep = positions < lens[:, None]
    keep_float = keep.astype(jnp.float32)
    lens_float = lens.astype(jnp.float32)[:, None]
    shape_heads = (seq_count, seq_len, HEADS, head_size)
    projected = product(inputs, weight_qkv)
    query = (projected[:, :width] + vectors[0]).astype(jnp.bfloat16)
    key_rows = projected[:, width : 2 * width].astype(jnp.bfloat16)
    value = (projected[:, 2 * width :] + vectors[1]).astype(jnp.bfloat16)
    query_heads = query.reshape(shape_heads)
    key_heads = key_rows.reshape(shape_heads)
    value_heads = value.reshape(shape_heads)
    scores = scores_of(query_heads, key_heads, keep)
    log_total = jax.nn.logsumexp(scores, axis=-1, keepdims=True)
    probs_low = jnp.exp(scores - log_total).astype(jnp.bfloat16)
    context = jnp.einsum(
        "shqk,skhe->sqhe", probs_low, value_heads, preferred_element_type=jnp.float32
    )
    context = context.reshape(rows, width).astype(jnp.bfloat16)
    attended = product(context, weight_attn) + vectors[2]
    first_norm, normed_one, inverse_one = norm_forward(
        inputs.astype(jnp.float32) + attended, scales[0], vectors[3]
    )
    first_low = first_norm.astype(jnp.bfloat16)
    hidden_pre = product(first_low, weight_in) + bias_in
    hidden = jax.nn.gelu(hidden_pre, approximate=False).astype(jnp.bfloat16)
    branch = product(hidden, weight_out) + vectors[4]
    output, normed_two, inverse_two = norm_forward(first_norm + branch, scales[1], vectors[5])
    pooled = (
        jnp.sum(output.reshape(seq_count, seq_len, width) * keep_float[:, :, None], axis=1)
        / lens_float
    )
    if direct:
        d_pooled = loss_gradient(pooled, positives, datasets, n)
    else:
        d_pooled = loss_gradient_plain(pooled, positives, datasets)
    d_output = ((d_pooled / lens_float)[:, None, :] * keep_float[:, :, None]).reshape(rows, width)
    d_second, d_gain_two, d_shift_two = norm_backward(d_output, normed_two, inverse_two, scales[1])
    d_branch = d_second.astype(jnp.bfloat16)
    g_weight_out = transposed_left(hidden, d_branch)
    g_bias_out = jnp.sum(d_branch.astype(jnp.float32), axis=0)
    d_hidden = transposed_right(d_branch, weight_out)
    gelu_pull = jax.vjp(partial(jax.nn.gelu, approximate=False), hidden_pre)[1]
    d_pre = gelu_pull(d_hidden)[0].astype(jnp.bfloat16)
    g_weight_in = transposed_left(first_low, d_pre)
    g_bias_in = jnp.sum(d_pre.astype(jnp.float32), axis=0)
    d_first = d_second + transposed_right(d_pre, weight_in)
    d_sum_one, d_gain_one, d_shift_one = norm_backward(d_first, normed_one, inverse_one, scales[0])
    d_attended = d_sum_one.astype(jnp.bfloat16)
    g_weight_attn = transposed_left(context, d_attended)
    g_bias_attn = jnp.sum(d_attended.astype(jnp.float32), axis=0)
    d_context = transposed_right(d_attended, weight_attn).astype(jnp.bfloat16).reshape(shape_heads)
    again = scores_of(query_heads, key_heads, keep)
    probs = jnp.exp(again - log_total)
    d_value = jnp.einsum(
        "shqk,sqhe->skhe", probs.astype(jnp.bfloat16), d_context, preferred_element_type=jnp.float32
    )
    d_probs = jnp.einsum(
        "sqhe,skhe->shqk", d_context, value_heads, preferred_element_type=jnp.float32
    )
    d_scores = (probs * (d_probs - jnp.sum(d_probs * probs, axis=-1, keepdims=True))).astype(
        jnp.bfloat16
    )
    d_query = (
        jnp.einsum("shqk,skhe->sqhe", d_scores, key_heads, preferred_element_type=jnp.float32)
        * 0.125
    )
    d_key = (
        jnp.einsum("shqk,sqhe->skhe", d_scores, query_heads, preferred_element_type=jnp.float32)
        * 0.125
    )
    d_query_low = d_query.reshape(rows, width).astype(jnp.bfloat16)
    d_key_low = d_key.reshape(rows, width).astype(jnp.bfloat16)
    d_value_low = d_value.reshape(rows, width).astype(jnp.bfloat16)
    d_projected = jnp.concatenate([d_query_low, d_key_low, d_value_low], axis=1)
    g_weight_qkv = transposed_left(inputs, d_projected)
    g_bias_query = jnp.sum(d_query_low.astype(jnp.float32), axis=0)
    g_bias_value = jnp.sum(d_value_low.astype(jnp.float32), axis=0)
    d_inputs = d_sum_one + transposed_right(d_projected, weight_qkv)
    g_vectors = jnp.stack(
        [g_bias_query, g_bias_value, g_bias_attn, d_shift_one, g_bias_out, d_shift_two]
    )
    g_scales = jnp.stack([d_gain_one, d_gain_two])
    if direct:
        packed = packed_of(g_weight_out, g_weight_in, g_weight_attn, g_weight_qkv, n)
        small = small_of(g_bias_in, g_vectors, g_scales, n)
        summed_out, summed_in, summed_attn, summed_qkv, small = summed_over_batch(packed, small, n)
        small = small.reshape(1024)
        part = width // n
        summed_bias_in = small[: 4 * part]
        summed_vectors = small[4 * part : 10 * part].reshape(6, part)
        summed_scales = small[10 * part : 12 * part].reshape(2, part)
    else:
        def scatter(value, dimension):
            return lax.psum_scatter(value, "batch", scatter_dimension=dimension, tiled=True)

        summed_qkv, summed_attn, summed_in, summed_out = (
            scatter(g_weight_qkv, 0), scatter(g_weight_attn, 0), scatter(g_weight_in, 0), scatter(g_weight_out, 0)
        )
        summed_bias_in, summed_vectors, summed_scales = (
            scatter(g_bias_in, 0), scatter(g_vectors, 1), scatter(g_scales, 1)
        )
    return (
        pooled[None],
        d_inputs.reshape(1, seq_count, seq_len, width),
        summed_qkv[None],
        summed_attn[None],
        summed_in[None],
        summed_out[None],
        summed_bias_in[None],
        summed_vectors[None],
        summed_scales[None],
    )


def solution(mesh):
    n = mesh.shape["batch"]
    direct = n == 16
    in_specs = (
        P("tower", "batch", None, None),
        P("tower", "batch"),
        P("batch"),
        P("batch"),
        P("tower", None, None),
        P("tower", None, None),
        P("tower", None, None),
        P("tower", None, None),
        P("tower", None),
        P("tower", None, None),
        P("tower", None, None),
    )
    out_specs = (
        P("tower", "batch", None),
        P("tower", "batch", None, None),
        P("tower", "batch", None),
        P("tower", "batch", None),
        P("tower", "batch", None),
        P("tower", "batch", None),
        P("tower", "batch"),
        P("tower", None, "batch"),
        P("tower", None, "batch"),
    )
    return jax.shard_map(
        partial(per_device, n, direct), mesh=mesh, in_specs=in_specs, out_specs=out_specs, check_vma=False
    )
```

```python
from functools import partial

import jax
import jax.numpy as jnp
from jax import lax
from jax.experimental import pallas as pl
from jax.experimental.pallas import tpu as pltpu
from jax.sharding import PartitionSpec as P

HEADS = 12
EPS = 1e-12
SCALE = 4.0
HIGH = lax.Precision.HIGHEST
MESH = pl.DeviceIdType.MESH
NEG = -1000000000.0
LOW = jnp.bfloat16
F32 = jnp.float32
CHUNK = 1536
SUBS = 3
MIB = 2**20


def product(left, right):
    return jnp.dot(left, right, preferred_element_type=jnp.float32)


def transposed_left(left, right):
    return lax.dot_general(
        left, right, (((0,), (0,)), ((), ())), preferred_element_type=jnp.float32
    )


def transposed_right(left, right):
    return lax.dot_general(
        left, right, (((1,), (1,)), ((), ())), preferred_element_type=jnp.float32
    )


def norm_forward(total, gain, shift):
    mean = jnp.mean(total, axis=-1, keepdims=True)
    centered = total - mean
    inverse = lax.rsqrt(jnp.mean(centered * centered, axis=-1, keepdims=True) + EPS)
    normed = centered * inverse
    return (normed * gain + shift, normed, inverse)


def norm_backward(grad, normed, inverse, gain):
    scaled = grad * gain
    first_mean = jnp.mean(scaled, axis=-1, keepdims=True)
    second_mean = jnp.mean(scaled * normed, axis=-1, keepdims=True)
    d_total = inverse * (scaled - first_mean - normed * second_mean)
    return (d_total, jnp.sum(grad * normed, axis=0), jnp.sum(grad, axis=0))


def scores_of(query_heads, key_heads, keep):
    raw = (
        jnp.einsum("sqhe,skhe->shqk", query_heads, key_heads, preferred_element_type=jnp.float32)
        * 0.125
    )
    return jnp.where(keep[:, None, None, :], raw, NEG)


def select(condition):
    return jnp.where(condition, 1.0, 0.0)


def loss_kernel(n, pooled_ref, extra_ref, out_ref, mine, everyone, send_sem, recv_sem):
    tower, me = lax.axis_index("tower"), lax.axis_index("batch")
    flat = tower * n + me
    total = 2 * n

    barrier = pltpu.get_barrier_semaphore()

    @pl.loop(1, total)
    def _(step):
        other = lax.rem(flat + step, total)
        pl.semaphore_signal(
            barrier, inc=1, device_id=(other // n, lax.rem(other, n)), device_id_type=MESH
        )

    pooled = pooled_ref[...]
    block = jnp.concatenate(
        [pooled[:, 0:256], pooled[:, 256:512], pooled[:, 512:768], extra_ref[...]], axis=0
    ).astype(jnp.bfloat16)
    mine[...] = block
    everyone[flat] = block
    pl.semaphore_wait(barrier, total - 1)

    def copy_to(step):
        other = lax.rem(flat + step, total)
        return pltpu.make_async_remote_copy(
            src_ref=mine,
            dst_ref=everyone.at[flat],
            send_sem=send_sem.at[step],
            recv_sem=recv_sem.at[step],
            device_id=(other // n, lax.rem(other, n)),
            device_id_type=MESH,
        )

    @pl.loop(1, total)
    def _(step):
        copy_to(step).start()

    @pl.loop(1, total)
    def _(step):
        copy_to(step).wait()

    seqs = 4 * n
    packed = everyone[...]
    questions = packed[:n].reshape(16 * n, 256)
    passages = packed[n:].reshape(16 * n, 256)
    rows = lax.broadcasted_iota(jnp.int32, (seqs, 16 * n), 0)
    places = lax.broadcasted_iota(jnp.int32, (seqs, 16 * n), 1)
    owner, lane = rows // 4, lax.rem(rows, 4)

    def picked(values, row):
        return product(select(places == owner * 16 + row).astype(jnp.bfloat16), values)

    def whole(values):
        parts = [
            product(select(places == owner * 16 + 4 * part + lane).astype(jnp.bfloat16), values)
            for part in range(3)
        ]
        return jnp.concatenate(parts, axis=1)

    column_lane = lax.broadcasted_iota(jnp.int32, (seqs, 256), 1)
    column_want = lax.rem(lax.broadcasted_iota(jnp.int32, (seqs, 256), 0), 4)

    def column(row):
        return jnp.sum(
            jnp.where(column_lane == column_want, picked(passages, row), 0.0), axis=1, keepdims=True
        )

    question_float, passage_float = whole(questions), whole(passages)
    question_low = question_float.astype(jnp.bfloat16)
    passage_low = passage_float.astype(jnp.bfloat16)
    positives, sets = column(12), column(13)
    first = lax.broadcasted_iota(jnp.int32, (seqs, seqs), 0)
    second = lax.broadcasted_iota(jnp.int32, (seqs, seqs), 1)
    set_row = jnp.sum(jnp.where(first == second, sets, 0.0), axis=0, keepdims=True)
    chosen = second == positives.astype(jnp.int32)
    query_set = jnp.sum(jnp.where(chosen, set_row, 0.0), axis=1, keepdims=True)
    logits = transposed_right(question_low, passage_low) * SCALE
    masked = jnp.where(set_row == query_set, logits, NEG)
    top = jnp.max(masked, axis=1, keepdims=True)
    weights = jnp.exp(masked - top)
    softmax = weights / jnp.sum(weights, axis=1, keepdims=True)
    d_logits = (softmax - select(chosen)) * SCALE

    mine_row = lax.broadcasted_iota(jnp.int32, (8, seqs), 0)
    mine_column = lax.broadcasted_iota(jnp.int32, (8, seqs), 1)
    own = select((mine_column == me * 4 + mine_row) & (mine_row < 4))

    @pl.when(tower == 0)
    def _():
        terms = jnp.dot(own, d_logits, precision=HIGH, preferred_element_type=jnp.float32)
        grad = jnp.dot(terms, passage_float, precision=HIGH, preferred_element_type=jnp.float32)
        out_ref[...] = grad.astype(jnp.bfloat16).astype(jnp.float32)

    @pl.when(tower == 1)
    def _():
        terms = lax.dot_general(
            own, d_logits, (((1,), (1,)), ((), ())), precision=HIGH, preferred_element_type=jnp.float32
        )
        out_ref[...] = jnp.dot(terms, question_float, precision=HIGH, preferred_element_type=jnp.float32)


def loss_gradient(pooled, positives, datasets, n):
    extra = jnp.stack([positives.astype(jnp.float32), datasets.astype(jnp.float32)])
    extra = jnp.pad(extra, ((0, 2), (0, 252)))
    grad = pl.pallas_call(
        partial(loss_kernel, n),
        out_shape=jax.ShapeDtypeStruct((8, pooled.shape[1]), jnp.float32),
        in_specs=[pl.BlockSpec(memory_space=pltpu.VMEM)] * 2,
        out_specs=pl.BlockSpec(memory_space=pltpu.VMEM),
        scratch_shapes=[
            pltpu.VMEM((16, 256), jnp.bfloat16),
            pltpu.VMEM((2 * n, 16, 256), jnp.bfloat16),
            pltpu.SemaphoreType.DMA((2 * n,)),
            pltpu.SemaphoreType.DMA((2 * n,)),
        ],
        compiler_params=pltpu.CompilerParams(collective_id=0, has_side_effects=True),
        name="loss",
    )(pooled, extra)
    return grad


def gelu_parts(z):
    t = 1.0 / (1.0 + jnp.abs(z) * (0.3275911 * 0.7071067811865476))
    bell = jnp.exp(z * z * -0.5)
    tail = t * bell * (
        0.127414796 + t * (-0.142248368 + t * (0.7107068705 + t * (-0.7265760135 + t * 0.5307027145)))
    )
    below = jnp.where(z < 0.0, tail, 1.0 - tail)
    return z * below, below + z * bell * 0.3989422804014327


def normed(total):
    mean = jnp.mean(total, axis=-1, keepdims=True)
    centered = total - mean
    inverse = lax.rsqrt(jnp.mean(centered * centered, axis=-1, keepdims=True) + EPS)
    return centered * inverse, inverse


def encoder_kernel(
    lens, x_ref, wqkv_hbm, wattn_hbm, win_hbm, wout_hbm, bin_ref, vec_ref, gain_ref,
    pooled_ref, query_ref, key_t_ref, value_ref, probs_ref, context_t_ref, low_t_ref, x_t_ref,
    n1_ref, n2_ref, inv_ref, hidden_ref, slope_ref,
    wqkv, wattn, win, wout, sems,
):
    step = pl.program_id(0)
    loads = [
        pltpu.make_async_copy(source.at[0], target, sems.at[place])
        for place, (source, target) in enumerate(
            [(wqkv_hbm, wqkv), (wattn_hbm, wattn), (win_hbm, win), (wout_hbm, wout)]
        )
    ]

    @pl.when(step == 0)
    def _():
        for load in loads:
            load.start()
        loads[0].wait()

    length = lens[step]
    x = x_ref[...]
    rows = x.shape[0]
    query = (product(x, wqkv[:, :768]) + vec_ref[0, 0:1]).astype(LOW) * 0.125
    key = product(x, wqkv[:, 768:1536]).astype(LOW)
    value = (product(x, wqkv[:, 1536:]) + vec_ref[0, 1:2]).astype(LOW)
    query_ref[...] = query
    value_ref[...] = value
    key_t_ref[...] = key.T
    x_t_ref[...] = x.T
    value_t = value.T
    blocked = jnp.where(lax.broadcasted_iota(jnp.int32, (rows, 1), 0) < length, 0.0, NEG)
    lane = lax.broadcasted_iota(jnp.int32, (rows, 128), 1)
    for head in range(HEADS):
        pair = slice(128 * (head // 2), 128 * (head // 2 + 1))
        mine = (lane < 64) if head % 2 == 0 else (lane >= 64)
        key_one = jnp.where(mine, key[:, pair], jnp.zeros((), LOW))
        scores = transposed_right(key_one, query[:, pair]) + blocked
        weights = jnp.exp(scores - jnp.max(scores, axis=0, keepdims=True))
        probs = (weights * (1.0 / jnp.sum(weights, axis=0, keepdims=True))).astype(LOW)
        probs_ref[0, head] = probs
        context_t_ref[64 * head:64 * (head + 1), :] = product(
            value_t[64 * head:64 * (head + 1)], probs
        ).astype(LOW)

    @pl.when(step == 0)
    def _():
        loads[1].wait()

    attended = transposed_left(context_t_ref[...], wattn[...]) + vec_ref[0, 2:3]
    n1, inv1 = normed(x.astype(F32) + attended)
    first = n1 * gain_ref[0, 0:1] + vec_ref[0, 3:4]
    first_low = first.astype(LOW)
    low_t_ref[...] = first_low.T
    n1_ref[...] = n1.astype(LOW)

    @pl.when(step == 0)
    def _():
        loads[2].wait()
        loads[3].wait()

    total = first + vec_ref[0, 4:5]
    for part in range(4):
        columns = slice(768 * part, 768 * (part + 1))
        hidden, slope = gelu_parts(product(first_low, win[:, columns]) + bin_ref[:, columns])
        hidden = hidden.astype(LOW)
        hidden_ref[:, columns] = hidden
        slope_ref[:, columns] = slope.astype(LOW)
        total = total + product(hidden, wout[columns, :])
    n2, inv2 = normed(total)
    n2_ref[...] = n2.astype(LOW)
    inv_ref[...] = jnp.where(lane < 64, inv1, inv2)
    output = n2 * gain_ref[0, 1:2] + vec_ref[0, 5:6]
    keep = lax.broadcasted_iota(jnp.int32, (rows, 1), 0) < length
    pooled_ref[0] = jnp.sum(jnp.where(keep, output, 0.0), axis=0, keepdims=True) / length.astype(F32)


def encoder(lens, x, w_qkv, w_attn, w_in, w_out, b_in, vectors, gains):
    seqs = lens.shape[0]
    rows = x.shape[0]
    per = rows // seqs

    def by_rows(width):
        return pl.BlockSpec((per, width), lambda s, *_: (s, 0))

    def by_columns(height):
        return pl.BlockSpec((height, per), lambda s, *_: (0, s))

    def full(*shape):
        return pl.BlockSpec(shape, lambda s, *_: (0,) * len(shape))

    anywhere = pl.BlockSpec(memory_space=pl.ANY)
    wide = lambda width, kind=LOW: jax.ShapeDtypeStruct((rows, width), kind)
    tall = jax.ShapeDtypeStruct((768, rows), LOW)
    return pl.pallas_call(
        encoder_kernel,
        grid_spec=pltpu.PrefetchScalarGridSpec(
            num_scalar_prefetch=1,
            grid=(seqs,),
            in_specs=[by_rows(768)] + [anywhere] * 4 + [full(1, 3072), full(1, 6, 768), full(1, 2, 768)],
            out_specs=[
                pl.BlockSpec((1, 1, 768), lambda s, *_: (s, 0, 0)),
                by_rows(768), by_columns(768), by_rows(768),
                pl.BlockSpec((1, HEADS, per, per), lambda s, *_: (s, 0, 0, 0)),
                by_columns(768), by_columns(768), by_columns(768),
                by_rows(768), by_rows(768), by_rows(128), by_rows(3072), by_rows(3072),
            ],
            scratch_shapes=[
                pltpu.VMEM((768, 2304), LOW), pltpu.VMEM((768, 768), LOW),
                pltpu.VMEM((768, 3072), LOW), pltpu.VMEM((3072, 768), LOW),
                pltpu.SemaphoreType.DMA((4,)),
            ],
        ),
        out_shape=[
            jax.ShapeDtypeStruct((seqs, 1, 768), F32),
            wide(768), tall, wide(768),
            jax.ShapeDtypeStruct((seqs, HEADS, per, per), LOW),
            tall, tall, tall, wide(768), wide(768), wide(128, F32), wide(3072), wide(3072),
        ],
        compiler_params=pltpu.CompilerParams(vmem_limit_bytes=56 * MIB),
        name="encoder",
    )(lens, x, w_qkv, w_attn, w_in, w_out, b_in, vectors, gains)


def second_norm_backward(grad_row, length, first_row, n2, inv2, gain):
    scaled = grad_row * gain
    mean = jnp.mean(scaled, axis=1, keepdims=True)
    along = jnp.mean(scaled * n2, axis=1, keepdims=True)
    keep = first_row + lax.broadcasted_iota(jnp.int32, (n2.shape[0], 1), 0) < length
    return jnp.where(keep, inv2 * (scaled - mean - n2 * along), 0.0), keep


def out_kernel(lens, dpool_ref, n2_ref, inv_ref, gain_ref, hidden_ref, packed_ref, small_ref, d_branch):
    step = pl.program_id(0)

    @pl.when(step == 0)
    def _():
        small_ref[...] = jnp.zeros_like(small_ref)
        for seq in range(4):
            rows = slice(256 * seq, 256 * (seq + 1))
            length = lens[seq]
            grad_row = dpool_ref[seq:seq + 1] / length.astype(F32)
            n2 = n2_ref[rows].astype(F32)
            d_second, keep = second_norm_backward(
                grad_row, length, 0, n2, inv_ref[rows, 64:65], gain_ref[0, 1:2]
            )
            low = d_second.astype(LOW)
            d_branch[rows] = low
            small_ref[0:1] += jnp.sum(low.astype(F32), axis=0, keepdims=True)
            small_ref[1:2] += dpool_ref[seq:seq + 1]
            small_ref[2:3] += grad_row * jnp.sum(jnp.where(keep, n2, 0.0), axis=0, keepdims=True)

    grad = transposed_left(hidden_ref[...], d_branch[...]).astype(LOW)
    for core in range(2):
        for way in range(2):
            for part in range(4):
                top = 192 * core + 48 * part
                packed_ref[0, core, way, :, 384 * part:384 * (part + 1)] = grad[
                    top:top + 48, 384 * way:384 * (way + 1)]


def out_gradient(lens, dpool, n2, inv, gains, hidden, n):
    chips = n // 2
    rows = n2.shape[0]

    def full(*shape):
        return pl.BlockSpec(shape, lambda c, *_: (0,) * len(shape))

    return pl.pallas_call(
        out_kernel,
        grid_spec=pltpu.PrefetchScalarGridSpec(
            num_scalar_prefetch=1,
            grid=(chips,),
            in_specs=[
                full(8, 768), full(rows, 768), full(rows, 128), full(1, 2, 768),
                pl.BlockSpec((rows, 384), lambda c, *_: (0, c)),
            ],
            out_specs=[pl.BlockSpec((1, 2, 2, 48, CHUNK), lambda c, *_: (c, 0, 0, 0, 0)), full(8, 768)],
            scratch_shapes=[pltpu.VMEM((rows, 768), LOW)],
        ),
        out_shape=[
            jax.ShapeDtypeStruct((chips, 2, 2, 48, CHUNK), LOW), jax.ShapeDtypeStruct((8, 768), F32),
        ],
        compiler_params=pltpu.CompilerParams(vmem_limit_bytes=48 * MIB),
        name="out_gradient",
    )(lens, dpool, n2, inv, gains, hidden)


def ring_place(chip, chips):
    half, y = chip // 2, lax.rem(chip, 2)
    return jnp.where(y == 0, half, chips - 1 - half)


def ring_chip(place, chips):
    return jnp.where(place < chips // 2, place * 2, (chips - 1 - place) * 2 + 1)


def ring_scratch(n):
    chips = n // 2
    block = (48, CHUNK)
    return [
        pltpu.VMEM((chips, 2) + block, LOW),
        pltpu.VMEM((chips, 2) + block, LOW),
        pltpu.VMEM((chips - 1, 2) + block, LOW),
        pltpu.VMEM((chips - 1, 2) + block, LOW),
        pltpu.SemaphoreType.DMA((chips, 2)),
        pltpu.SemaphoreType.DMA((chips, 2)),
        pltpu.SemaphoreType.DMA((chips, 2)),
        pltpu.SemaphoreType.DMA((chips - 1, SUBS, 2)),
        pltpu.SemaphoreType.DMA((chips - 1, SUBS, 2)),
    ]


class Ring:
    def __init__(self, n, packed, scratch, finish):
        self.n, self.chips, self.packed, self.finish = n, n // 2, packed, finish
        (self.own, self.paired, self.sending, self.got, self.own_sem, self.pair_send, self.pair_recv,
         self.ring_send, self.ring_recv) = scratch
        self.tower, self.me = lax.axis_index("tower"), lax.axis_index("batch")
        chips = self.chips
        self.core = lax.rem(self.me, 2)
        self.place = ring_place(self.me // 2, chips)
        self.sibling = (self.tower, self.me + 1 - 2 * self.core)
        self.next = [
            (self.tower, ring_chip(lax.rem(self.place + 1, chips), chips) * 2 + self.core),
            (self.tower, ring_chip(lax.rem(self.place + chips - 1, chips), chips) * 2 + self.core),
        ]
        self.turns = chips * SUBS

    def target(self, step, way):
        if way == 0:
            return ring_chip(lax.rem(self.place + self.chips - 1 - step + self.chips, self.chips), self.chips)
        return ring_chip(lax.rem(self.place + 1 + step, self.chips), self.chips)

    def own_copy(self, step, way):
        return pltpu.make_async_copy(
            self.packed.at[self.target(step, way), self.core, way], self.own.at[step, way], self.own_sem.at[step, way]
        )

    def pair_copy(self, step, way):
        return pltpu.make_async_remote_copy(
            src_ref=self.packed.at[self.target(step, way), 1 - self.core, way],
            dst_ref=self.paired.at[step, way],
            send_sem=self.pair_send.at[step, way], recv_sem=self.pair_recv.at[step, way],
            device_id=self.sibling, device_id_type=MESH,
        )

    def ring_copy(self, step, sub, way):
        rows = pl.ds(pl.multiple_of(sub * 16, 16), 16)
        return pltpu.make_async_remote_copy(
            src_ref=self.sending.at[step, way, rows], dst_ref=self.got.at[step, way, rows],
            send_sem=self.ring_send.at[step, sub, way], recv_sem=self.ring_recv.at[step, sub, way],
            device_id=self.next[way], device_id_type=MESH,
        )

    def greet(self):
        barrier = pltpu.get_barrier_semaphore()
        for device in [self.sibling] + self.next:
            pl.semaphore_signal(barrier, inc=1, device_id=device, device_id_type=MESH)

    def greeted(self):
        pl.semaphore_wait(pltpu.get_barrier_semaphore(), 3)

    def load(self):
        @pl.loop(0, self.chips)
        def _(step):
            for way in range(2):
                self.own_copy(step, way).start()

    def swap(self):
        @pl.loop(0, self.chips)
        def _(step):
            for way in range(2):
                self.pair_copy(step, way).start()

    def turn(self, index):
        step, sub = index // SUBS, lax.rem(index, SUBS)
        rows = pl.ds(pl.multiple_of(sub * 16, 16), 16)
        last = self.chips - 1

        @pl.when(sub == 0)
        def _():
            for way in range(2):
                self.own_copy(step, way).wait()
                self.pair_copy(step, way).wait_recv()

        def local(way):
            return self.own[step, way, rows].astype(F32) + self.paired[step, way, rows].astype(F32)

        @pl.when(step == 0)
        def _():
            for way in range(2):
                self.sending[step, way, rows] = local(way).astype(LOW)
                self.ring_copy(step, sub, way).start()

        @pl.when((step > 0) & (step < last))
        def _():
            for way in range(2):
                before = lax.max(step - 1, 0)
                self.ring_copy(before, sub, way).wait_recv()
                self.sending[step, way, rows] = (
                    local(way) + self.got[before, way, rows].astype(F32)
                ).astype(LOW)
                self.ring_copy(step, sub, way).start()

        @pl.when(step == last)
        def _():
            for way in range(2):
                self.ring_copy(last - 1, sub, way).wait_recv()
                self.finish(sub, way, local(way) + self.got[last - 1, way, rows].astype(F32))

    def close(self):
        @pl.loop(0, self.chips)
        def _(step):
            for way in range(2):
                self.pair_copy(step, way).wait_send()

        @pl.loop(0, self.chips - 1)
        def _(step):
            for sub in range(SUBS):
                for way in range(2):
                    self.ring_copy(step, sub, way).wait_send()


def at(sub, base=0):
    return pl.ds(pl.multiple_of(base + sub * 16, 16), 16)


def ffn_kernel(
    n, packed, lens, dpool_ref, win_hbm, wout_hbm, n1_hbm, n2_hbm, inv_hbm, slope_hbm, low_t_hbm, gain_ref,
    summed_ref, packed_out, d_sum_out, small_ref, bias_in_ref,
    *scratch,
):
    ring_parts, (win, wout, n1, n2, inv, pre, low_t, d_sum, grads, sems, out_sems) = scratch[:9], scratch[9:]

    def finish(sub, way, total):
        for part in range(4):
            summed_ref[at(sub, 48 * part), 384 * way:384 * (way + 1)] = total[:, 384 * part:384 * (part + 1)]

    ring = Ring(n, packed, ring_parts, finish)
    ring.greet()
    weights = [
        pltpu.make_async_copy(wout_hbm.at[0], wout, sems.at[0, 0]),
        pltpu.make_async_copy(win_hbm.at[0], win, sems.at[0, 1]),
    ]

    def loads(seq):
        rows = pl.ds(pl.multiple_of(seq * 256, 256), 256)
        return [
            pltpu.make_async_copy(source.at[rows], target.at[rows], sems.at[seq + 1, place])
            for place, (source, target) in enumerate(
                [(n2_hbm, n2), (inv_hbm, inv), (slope_hbm, pre), (n1_hbm, n1)]
            )
        ]

    low_load = pltpu.make_async_copy(low_t_hbm, low_t, sems.at[0, 2])
    weights[0].start()
    for copy in loads(0):
        copy.start()
    weights[1].start()
    ring.load()
    ring.greeted()
    ring.swap()
    for seq in range(1, 4):
        for copy in loads(seq):
            copy.start()
    low_load.start()

    small_ref[...] = jnp.zeros_like(small_ref)
    bias_in_ref[...] = jnp.zeros_like(bias_in_ref)
    weights[0].wait()
    weights[1].wait()

    @pl.loop(0, 4)
    def _(seq):
        rows = pl.ds(pl.multiple_of(seq * 256, 256), 256)
        for copy in loads(seq):
            copy.wait()
        length = lens[seq]
        d_second, _ = second_norm_backward(
            dpool_ref[pl.ds(seq, 1)] / length.astype(F32), length, 0, n2[rows].astype(F32), inv[rows, 64:65],
            gain_ref[0, 1:2],
        )
        d_branch = d_second.astype(LOW)
        d_first = d_second
        for part in range(4):
            ring.turn(seq * 4 + part)
            columns = slice(768 * part, 768 * (part + 1))
            d_pre = (
                transposed_right(d_branch, wout[columns, :]) * pre[rows, columns].astype(F32)
            ).astype(LOW)
            pre[rows, columns] = d_pre
            bias_in_ref[:, columns] += jnp.sum(d_pre.astype(F32), axis=0, keepdims=True)
            d_first = d_first + transposed_right(d_pre, win[:, columns])
        normal = n1[rows].astype(F32)
        scaled = d_first * gain_ref[0, 0:1]
        mean = jnp.mean(scaled, axis=1, keepdims=True)
        along = jnp.mean(scaled * normal, axis=1, keepdims=True)
        d_sum_one = inv[rows, 0:1] * (scaled - mean - normal * along)
        d_sum[rows] = d_sum_one
        pltpu.make_async_copy(d_sum.at[rows], d_sum_out.at[rows], out_sems.at[seq]).start()
        small_ref[0:1] += jnp.sum(d_sum_one.astype(LOW).astype(F32), axis=0, keepdims=True)
        small_ref[1:2] += jnp.sum(d_first, axis=0, keepdims=True)
        small_ref[2:3] += jnp.sum(d_first * normal, axis=0, keepdims=True)

    low_load.wait()

    @pl.loop(0, 8)
    def _(part):
        ring.turn(16 + part)
        columns = pl.ds(pl.multiple_of(part * 384, 384), 384)
        grad = product(low_t[...], pre[:, columns]).astype(LOW)
        place = pl.ds(pl.multiple_of(lax.rem(part, 4) * 384, 384), 384)
        grads[:, :, part // 4, :, place] = grad.reshape(n // 2, 2, 48, 384)

    done = pltpu.make_async_copy(grads, packed_out, out_sems.at[4])
    done.start()
    for seq in range(4):
        rows = pl.ds(seq * 256, 256)
        pltpu.make_async_copy(d_sum.at[rows], d_sum_out.at[rows], out_sems.at[seq]).wait()
    done.wait()
    ring.close()


def ffn_backward(packed, lens, dpool, w_in, w_out, n1, n2, inv, slope, low_t, gains, n):
    rows = n1.shape[0]
    anywhere = pl.BlockSpec(memory_space=pl.ANY)
    vmem = pl.BlockSpec(memory_space=pltpu.VMEM)
    return pl.pallas_call(
        partial(ffn_kernel, n),
        in_specs=[anywhere, pl.BlockSpec(memory_space=pltpu.SMEM), vmem] + [anywhere] * 7 + [vmem],
        out_specs=[vmem, anywhere, anywhere, vmem, vmem],
        out_shape=[
            jax.ShapeDtypeStruct((192, 768), F32), jax.ShapeDtypeStruct(packed.shape, LOW),
            jax.ShapeDtypeStruct((rows, 768), F32), jax.ShapeDtypeStruct((8, 768), F32),
            jax.ShapeDtypeStruct((1, 3072), F32),
        ],
        scratch_shapes=ring_scratch(n) + [
            pltpu.VMEM((768, 3072), LOW), pltpu.VMEM((3072, 768), LOW),
            pltpu.VMEM((rows, 768), LOW), pltpu.VMEM((rows, 768), LOW), pltpu.VMEM((rows, 128), F32),
            pltpu.VMEM((rows, 3072), LOW), pltpu.VMEM((768, rows), LOW), pltpu.VMEM((rows, 768), F32),
            pltpu.VMEM(packed.shape, LOW),
            pltpu.SemaphoreType.DMA((5, 4)), pltpu.SemaphoreType.DMA((5,)),
        ],
        compiler_params=pltpu.CompilerParams(collective_id=1, has_side_effects=True, vmem_limit_bytes=56 * MIB),
        name="ffn_backward",
    )(packed, lens, dpool, w_in, w_out, n1, n2, inv, slope, low_t, gains)


def attention_kernel(
    n, packed, wattn_hbm, d_sum_hbm, query_hbm, key_t_hbm, value_hbm, probs_hbm, context_t_hbm, x_t_hbm,
    summed_ref, packed_out, d_proj_out, small_ref,
    *scratch,
):
    ring_parts, (wattn, d_sum, query, key_t, value, probs, context_t, x_t, d_low, d_proj, grads, sems, out_sems) = (
        scratch[:9], scratch[9:]
    )

    def finish(sub, way, total):
        summed_ref[at(sub), CHUNK * way:CHUNK * (way + 1)] = total

    ring = Ring(n, packed, ring_parts, finish)
    ring.greet()
    wattn_load = pltpu.make_async_copy(wattn_hbm.at[0], wattn, sems.at[4, 0])
    x_load = pltpu.make_async_copy(x_t_hbm, x_t, sems.at[4, 1])

    def loads(seq):
        rows = pl.ds(pl.multiple_of(seq * 256, 256), 256)
        return [
            pltpu.make_async_copy(source.at[rows], target.at[rows], sems.at[seq, place])
            for place, (source, target) in enumerate([(d_sum_hbm, d_sum), (query_hbm, query), (value_hbm, value)])
        ] + [
            pltpu.make_async_copy(source.at[:, rows], target.at[:, rows], sems.at[seq, 3 + place])
            for place, (source, target) in enumerate([(key_t_hbm, key_t), (context_t_hbm, context_t)])
        ] + [pltpu.make_async_copy(probs_hbm.at[seq], probs.at[seq], sems.at[seq, 5])]

    wattn_load.start()
    for copy in loads(0):
        copy.start()
    ring.load()
    ring.greeted()
    ring.swap()
    for seq in range(1, 4):
        for copy in loads(seq):
            copy.start()
    x_load.start()
    small_ref[...] = jnp.zeros_like(small_ref)
    wattn_load.wait()
    lane = lax.broadcasted_iota(jnp.int32, (256, 128), 1)
    none = jnp.zeros((), LOW)

    @pl.loop(0, 4)
    def _(seq):
        rows = pl.ds(pl.multiple_of(seq * 256, 256), 256)
        for copy in loads(seq):
            copy.wait()
        d_attended = d_sum[rows].astype(LOW)
        d_low[rows] = d_attended
        d_context = transposed_right(d_attended, wattn[...]).astype(LOW)
        d_context_t = transposed_right(wattn[...], d_attended).astype(LOW)
        for pair in range(6):
            if pair < 4:
                ring.turn(seq * 4 + pair)
            lanes = slice(128 * pair, 128 * (pair + 1))
            key_pair, query_pair, value_pair = key_t[lanes, rows], query[rows, lanes], value[rows, lanes]
            d_context_pair, d_context_t_pair = d_context[:, lanes], d_context_t[lanes]
            weighed = d_context_t_pair.astype(F32) * context_t[lanes, rows].astype(F32)
            d_queries, d_keys, d_values = [], [], []
            for one in range(2):
                half = slice(64 * one, 64 * (one + 1))
                prob = probs[seq, 2 * pair + one]
                value_one = jnp.where((lane < 64) if one == 0 else (lane >= 64), value_pair, none)
                d_prob = product(value_one, d_context_t_pair)
                row_sum = jnp.sum(weighed[half], axis=0, keepdims=True)
                d_score = (prob.astype(F32) * (d_prob - row_sum)).astype(LOW)
                d_values.append(product(prob, d_context_pair))
                d_keys.append(product(d_score, query_pair))
                d_queries.append(product(key_pair[half], d_score))
            d_query = (jnp.concatenate(d_queries, axis=0).T * 0.125).astype(LOW)
            d_key = jnp.where(lane < 64, d_keys[0], d_keys[1]).astype(LOW)
            d_value = jnp.where(lane < 64, d_values[0], d_values[1]).astype(LOW)
            d_proj[rows, 128 * pair:128 * (pair + 1)] = d_query
            d_proj[rows, 768 + 128 * pair:768 + 128 * (pair + 1)] = d_key
            d_proj[rows, 1536 + 128 * pair:1536 + 128 * (pair + 1)] = d_value
            small_ref[0:1, lanes] += jnp.sum(d_query.astype(F32), axis=0, keepdims=True)
            small_ref[1:2, lanes] += jnp.sum(d_value.astype(F32), axis=0, keepdims=True)
        pltpu.make_async_copy(d_proj.at[rows], d_proj_out.at[rows], out_sems.at[seq]).start()

    x_load.wait()
    for way in range(2):
        ring.turn(16 + way)
        grad = product(context_t[...], d_low[:, 384 * way:384 * (way + 1)]).astype(LOW)
        grads[:, :, way, :, 0:384] = grad.reshape(n // 2, 2, 48, 384)

    @pl.loop(0, 6)
    def _(part):
        ring.turn(18 + part)
        grad = product(x_t[...], d_proj[:, pl.ds(pl.multiple_of(part * 384, 384), 384)]).astype(LOW)
        place = pl.ds(pl.multiple_of(384 + lax.rem(part, 3) * 384, 384), 384)
        grads[:, :, part // 3, :, place] = grad.reshape(n // 2, 2, 48, 384)

    done = pltpu.make_async_copy(grads, packed_out, out_sems.at[4])
    done.start()
    for seq in range(4):
        rows = pl.ds(seq * 256, 256)
        pltpu.make_async_copy(d_proj.at[rows], d_proj_out.at[rows], out_sems.at[seq]).wait()
    done.wait()
    ring.close()


def attention_backward(packed, w_attn, d_sum, query, key_t, value, probs, context_t, x_t, n):
    rows = query.shape[0]
    anywhere = pl.BlockSpec(memory_space=pl.ANY)
    vmem = pl.BlockSpec(memory_space=pltpu.VMEM)
    wide, tall = pltpu.VMEM((rows, 768), LOW), pltpu.VMEM((768, rows), LOW)
    return pl.pallas_call(
        partial(attention_kernel, n),
        in_specs=[anywhere] * 9,
        out_specs=[vmem, anywhere, anywhere, vmem],
        out_shape=[
            jax.ShapeDtypeStruct((48, 3072), F32), jax.ShapeDtypeStruct(packed.shape, LOW),
            jax.ShapeDtypeStruct((rows, 2304), LOW), jax.ShapeDtypeStruct((8, 768), F32),
        ],
        scratch_shapes=ring_scratch(n) + [
            pltpu.VMEM((768, 768), LOW), pltpu.VMEM((rows, 768), F32), wide, tall, wide,
            pltpu.VMEM(probs.shape, LOW), tall, tall, wide, pltpu.VMEM((rows, 2304), LOW),
            pltpu.VMEM(packed.shape, LOW),
            pltpu.SemaphoreType.DMA((5, 6)), pltpu.SemaphoreType.DMA((5,)),
        ],
        compiler_params=pltpu.CompilerParams(collective_id=2, has_side_effects=True, vmem_limit_bytes=58 * MIB),
        name="attention_backward",
    )(packed, w_attn, d_sum, query, key_t, value, probs, context_t, x_t)


def tokens_kernel(
    n, packed, wqkv_hbm, d_sum_hbm, d_proj_hbm, out_small_ref, ffn_small_ref, bias_in_ref, attn_small_ref,
    attn_ref, qkv_ref, summed_small_ref, grad_out,
    *scratch,
):
    ring_parts, (wqkv, d_sum, d_proj, small, small_got, sems, out_sems, small_send, small_recv) = (
        scratch[:9], scratch[9:]
    )
    tower, me = lax.axis_index("tower"), lax.axis_index("batch")

    def finish(sub, way, total):
        attn_ref[at(sub), 384 * way:384 * (way + 1)] = total[:, :384]
        qkv_ref[at(sub), 1152 * way:1152 * (way + 1)] = total[:, 384:]

    ring = Ring(n, packed, ring_parts, finish)
    barrier = pltpu.get_barrier_semaphore()

    @pl.loop(1, n)
    def _(step):
        pl.semaphore_signal(
            barrier, inc=1, device_id=(tower, lax.rem(me + step, n)), device_id_type=MESH
        )

    wqkv_load = pltpu.make_async_copy(wqkv_hbm.at[0], wqkv, sems.at[4, 0])

    def loads(seq):
        rows = pl.ds(pl.multiple_of(seq * 256, 256), 256)
        return [
            pltpu.make_async_copy(source.at[rows], target.at[rows], sems.at[seq, place])
            for place, (source, target) in enumerate([(d_sum_hbm, d_sum), (d_proj_hbm, d_proj)])
        ]

    ring.load()
    wqkv_load.start()
    for seq in range(4):
        for copy in loads(seq):
            copy.start()
    rows_of = [
        attn_small_ref[0:1], attn_small_ref[1:2], ffn_small_ref[0:1], ffn_small_ref[1:2],
        out_small_ref[0:1], out_small_ref[1:2], ffn_small_ref[2:3], out_small_ref[2:3],
    ]
    bundle = jnp.concatenate(rows_of, axis=0)
    bias_in = bias_in_ref[...]
    small[...] = jnp.zeros_like(small)
    for device in range(n):
        small[device, 0:8, 0:48] = bundle[:, 48 * device:48 * (device + 1)]
        for part in range(4):
            start = 192 * device + 48 * part
            small[device, 8 + part:9 + part, 0:48] = bias_in[:, start:start + 48]
    pl.semaphore_wait(barrier, n - 1)
    ring.swap()

    def small_copy(step):
        other = lax.rem(me + step, n)
        return pltpu.make_async_remote_copy(
            src_ref=small.at[other], dst_ref=small_got.at[step],
            send_sem=small_send.at[step], recv_sem=small_recv.at[step],
            device_id=(tower, other), device_id_type=MESH,
        )

    for turn in range(SUBS):
        ring.turn(turn)

    @pl.loop(1, n)
    def _(step):
        small_copy(step).start()

    wqkv_load.wait()

    @pl.loop(0, 4)
    def _(seq):
        rows = pl.ds(pl.multiple_of(seq * 256, 256), 256)
        for copy in loads(seq):
            copy.wait()
        for part in range(3):
            ring.turn(SUBS + seq * 3 + part)
            columns = slice(256 * part, 256 * (part + 1))
            d_sum[rows, columns] += transposed_right(d_proj[rows], wqkv[columns, :])
        pltpu.make_async_copy(d_sum.at[rows], grad_out.at[rows], out_sems.at[seq]).start()

    summed_small_ref[...] = small[me]

    @pl.loop(1, n)
    def _(step):
        small_copy(step).wait()
        summed_small_ref[...] += small_got[step]

    @pl.loop(SUBS + 12, ring.turns)
    def _(turn):
        ring.turn(turn)

    for seq in range(4):
        rows = pl.ds(seq * 256, 256)
        pltpu.make_async_copy(d_sum.at[rows], grad_out.at[rows], out_sems.at[seq]).wait()
    ring.close()


def tokens_gradient(packed, w_qkv, d_sum, d_proj, out_small, ffn_small, bias_in, attn_small, n):
    rows = d_sum.shape[0]
    anywhere = pl.BlockSpec(memory_space=pl.ANY)
    vmem = pl.BlockSpec(memory_space=pltpu.VMEM)
    return pl.pallas_call(
        partial(tokens_kernel, n),
        in_specs=[anywhere] * 4 + [vmem] * 4,
        out_specs=[vmem, vmem, vmem, anywhere],
        out_shape=[
            jax.ShapeDtypeStruct((48, 768), F32), jax.ShapeDtypeStruct((48, 2304), F32),
            jax.ShapeDtypeStruct((16, 128), F32), jax.ShapeDtypeStruct((rows, 768), F32),
        ],
        scratch_shapes=ring_scratch(n) + [
            pltpu.VMEM((768, 2304), LOW), pltpu.VMEM((rows, 768), F32), pltpu.VMEM((rows, 2304), LOW),
            pltpu.VMEM((n, 16, 128), F32), pltpu.VMEM((n, 16, 128), F32),
            pltpu.SemaphoreType.DMA((5, 2)), pltpu.SemaphoreType.DMA((4,)),
            pltpu.SemaphoreType.DMA((n,)), pltpu.SemaphoreType.DMA((n,)),
        ],
        compiler_params=pltpu.CompilerParams(collective_id=3, has_side_effects=True, vmem_limit_bytes=48 * MIB),
        name="tokens_gradient",
    )(packed, w_qkv, d_sum, d_proj, out_small, ffn_small, bias_in, attn_small)


def per_device(
    n,
    tokens, lengths, positives, datasets, w_qkv, w_attn_out, w_ffn_in, w_ffn_out, b_ffn_in, biases, gains,
):
    seq_count, seq_len, width = (tokens.shape[1], tokens.shape[2], tokens.shape[3])
    lens = lengths[0]
    inputs = tokens[0].reshape(seq_count * seq_len, width)
    (pooled, query, key_t, value, probs, context_t, low_t, x_t, n1, n2, inv, hidden, slope) = encoder(
        lens, inputs, w_qkv, w_attn_out, w_ffn_in, w_ffn_out, b_ffn_in, biases, gains
    )
    pooled = pooled.reshape(seq_count, width)
    d_pooled = loss_gradient(pooled, positives, datasets, n)
    packed_out, out_small = out_gradient(lens, d_pooled, n2, inv, gains, hidden, n)
    summed_out, packed_in, d_sum, ffn_small, bias_in = ffn_backward(
        packed_out, lens, d_pooled, w_ffn_in, w_ffn_out, n1, n2, inv, slope, low_t, gains, n
    )
    summed_in, packed_rest, d_proj, attn_small = attention_backward(
        packed_in, w_attn_out, d_sum, query, key_t, value, probs, context_t, x_t, n
    )
    summed_attn, summed_qkv, small, grad_tokens = tokens_gradient(
        packed_rest, w_qkv, d_sum, d_proj, out_small, ffn_small, bias_in, attn_small, n
    )
    part = width // n
    return (
        pooled[None],
        grad_tokens.reshape(1, seq_count, seq_len, width),
        summed_qkv[None],
        summed_attn[None],
        summed_in[None],
        summed_out[None],
        small[8:12, :part].reshape(1, 4 * part),
        small[None, 0:6, :part],
        small[None, 6:8, :part],
    )


def from_behind(value, axis, steps):
    count = lax.axis_size(axis)
    leading, last = (max(0, -steps), min(count, count - steps))
    return lax.ppermute(value, axis, [(source, source + steps) for source in range(leading, last)])


def loss_gradient_plain(pooled, positives, datasets):
    seq_count = pooled.shape[0]
    mine = pooled.astype(jnp.bfloat16)
    questions = from_behind(mine, "tower", 1)
    everyone, every_set = (
        lax.all_gather(mine, "batch", axis=0, tiled=True),
        lax.all_gather(datasets.astype(jnp.bfloat16), "batch", axis=0, tiled=True),
    )
    total_seqs = everyone.shape[0]
    columns = lax.broadcasted_iota(jnp.int32, (seq_count, total_seqs), 1)
    chosen = columns == positives[:, None]
    set_row = every_set.astype(jnp.float32)[None, :]
    query_set = jnp.sum(jnp.where(chosen, set_row, 0.0), axis=1, keepdims=True)
    allowed = set_row == query_set
    question_float = questions.astype(jnp.float32)
    everyone_float = everyone.astype(jnp.float32)
    logits = jnp.dot(question_float, everyone_float.T, precision=HIGH) * SCALE
    masked = jnp.where(allowed, logits, NEG)
    softmax_rows = jnp.exp(masked - jax.nn.logsumexp(masked, axis=1, keepdims=True))
    d_logits = (softmax_rows - chosen.astype(jnp.float32)) * SCALE
    d_questions = jnp.dot(d_logits, everyone_float, precision=HIGH).astype(jnp.bfloat16)
    passage_terms = jnp.dot(d_logits.T, question_float, precision=HIGH)
    d_passages = lax.psum_scatter(passage_terms, "batch", scatter_dimension=0, tiled=True)
    returned = from_behind(d_questions, "tower", -1)
    is_passage = lax.axis_index("tower") == 1
    return jnp.where(is_passage, d_passages, returned.astype(jnp.float32))


def per_device_plain(

    tokens, lengths, positives, datasets, w_qkv, w_attn_out, w_ffn_in, w_ffn_out, b_ffn_in, biases, gains,
):
    seq_count, seq_len, width = (tokens.shape[1], tokens.shape[2], tokens.shape[3])
    head_size = width // HEADS
    rows = seq_count * seq_len
    inputs = tokens[0].reshape(rows, width)
    lens = lengths[0]
    weight_qkv = w_qkv[0]
    weight_attn = w_attn_out[0]
    weight_in = w_ffn_in[0]
    weight_out = w_ffn_out[0]
    bias_in = b_ffn_in[0]
    vectors = biases[0]
    scales = gains[0]
    positions = lax.broadcasted_iota(jnp.int32, (seq_count, seq_len), 1)
    keep = positions < lens[:, None]
    keep_float = keep.astype(jnp.float32)
    lens_float = lens.astype(jnp.float32)[:, None]
    shape_heads = (seq_count, seq_len, HEADS, head_size)
    projected = product(inputs, weight_qkv)
    query = (projected[:, :width] + vectors[0]).astype(jnp.bfloat16)
    key_rows = projected[:, width : 2 * width].astype(jnp.bfloat16)
    value = (projected[:, 2 * width :] + vectors[1]).astype(jnp.bfloat16)
    query_heads = query.reshape(shape_heads)
    key_heads = key_rows.reshape(shape_heads)
    value_heads = value.reshape(shape_heads)
    scores = scores_of(query_heads, key_heads, keep)
    log_total = jax.nn.logsumexp(scores, axis=-1, keepdims=True)
    probs_low = jnp.exp(scores - log_total).astype(jnp.bfloat16)
    context = jnp.einsum(
        "shqk,skhe->sqhe", probs_low, value_heads, preferred_element_type=jnp.float32
    )
    context = context.reshape(rows, width).astype(jnp.bfloat16)
    attended = product(context, weight_attn) + vectors[2]
    first_norm, normed_one, inverse_one = norm_forward(
        inputs.astype(jnp.float32) + attended, scales[0], vectors[3]
    )
    first_low = first_norm.astype(jnp.bfloat16)
    hidden_pre = product(first_low, weight_in) + bias_in
    hidden = jax.nn.gelu(hidden_pre, approximate=False).astype(jnp.bfloat16)
    branch = product(hidden, weight_out) + vectors[4]
    output, normed_two, inverse_two = norm_forward(first_norm + branch, scales[1], vectors[5])
    pooled = (
        jnp.sum(output.reshape(seq_count, seq_len, width) * keep_float[:, :, None], axis=1)
        / lens_float
    )
    d_pooled = loss_gradient_plain(pooled, positives, datasets)
    d_output = ((d_pooled / lens_float)[:, None, :] * keep_float[:, :, None]).reshape(rows, width)
    d_second, d_gain_two, d_shift_two = norm_backward(d_output, normed_two, inverse_two, scales[1])
    d_branch = d_second.astype(jnp.bfloat16)
    g_weight_out = transposed_left(hidden, d_branch)
    g_bias_out = jnp.sum(d_branch.astype(jnp.float32), axis=0)
    d_hidden = transposed_right(d_branch, weight_out)
    gelu_pull = jax.vjp(partial(jax.nn.gelu, approximate=False), hidden_pre)[1]
    d_pre = gelu_pull(d_hidden)[0].astype(jnp.bfloat16)
    g_weight_in = transposed_left(first_low, d_pre)
    g_bias_in = jnp.sum(d_pre.astype(jnp.float32), axis=0)
    d_first = d_second + transposed_right(d_pre, weight_in)
    d_sum_one, d_gain_one, d_shift_one = norm_backward(d_first, normed_one, inverse_one, scales[0])
    d_attended = d_sum_one.astype(jnp.bfloat16)
    g_weight_attn = transposed_left(context, d_attended)
    g_bias_attn = jnp.sum(d_attended.astype(jnp.float32), axis=0)
    d_context = transposed_right(d_attended, weight_attn).astype(jnp.bfloat16).reshape(shape_heads)
    again = scores_of(query_heads, key_heads, keep)
    probs = jnp.exp(again - log_total)
    d_value = jnp.einsum(
        "shqk,sqhe->skhe", probs.astype(jnp.bfloat16), d_context, preferred_element_type=jnp.float32
    )
    d_probs = jnp.einsum(
        "sqhe,skhe->shqk", d_context, value_heads, preferred_element_type=jnp.float32
    )
    d_scores = (probs * (d_probs - jnp.sum(d_probs * probs, axis=-1, keepdims=True))).astype(
        jnp.bfloat16
    )
    d_query = (
        jnp.einsum("shqk,skhe->sqhe", d_scores, key_heads, preferred_element_type=jnp.float32)
        * 0.125
    )
    d_key = (
        jnp.einsum("shqk,sqhe->skhe", d_scores, query_heads, preferred_element_type=jnp.float32)
        * 0.125
    )
    d_query_low = d_query.reshape(rows, width).astype(jnp.bfloat16)
    d_key_low = d_key.reshape(rows, width).astype(jnp.bfloat16)
    d_value_low = d_value.reshape(rows, width).astype(jnp.bfloat16)
    d_projected = jnp.concatenate([d_query_low, d_key_low, d_value_low], axis=1)
    g_weight_qkv = transposed_left(inputs, d_projected)
    g_bias_query = jnp.sum(d_query_low.astype(jnp.float32), axis=0)
    g_bias_value = jnp.sum(d_value_low.astype(jnp.float32), axis=0)
    d_inputs = d_sum_one + transposed_right(d_projected, weight_qkv)
    g_vectors = jnp.stack(
        [g_bias_query, g_bias_value, g_bias_attn, d_shift_one, g_bias_out, d_shift_two]
    )
    g_scales = jnp.stack([d_gain_one, d_gain_two])

    def scatter(value, dimension):
        return lax.psum_scatter(value, "batch", scatter_dimension=dimension, tiled=True)

    summed_qkv, summed_attn, summed_in, summed_out = (
        scatter(g_weight_qkv, 0), scatter(g_weight_attn, 0), scatter(g_weight_in, 0), scatter(g_weight_out, 0)
    )
    summed_bias_in, summed_vectors, summed_scales = (
        scatter(g_bias_in, 0), scatter(g_vectors, 1), scatter(g_scales, 1)
    )
    return (
        pooled[None],
        d_inputs.reshape(1, seq_count, seq_len, width),
        summed_qkv[None],
        summed_attn[None],
        summed_in[None],
        summed_out[None],
        summed_bias_in[None],
        summed_vectors[None],
        summed_scales[None],
    )


def solution(mesh):
    n = mesh.shape["batch"]
    direct = n == 16
    in_specs = (
        P("tower", "batch", None, None),
        P("tower", "batch"),
        P("batch"),
        P("batch"),
        P("tower", None, None),
        P("tower", None, None),
        P("tower", None, None),
        P("tower", None, None),
        P("tower", None),
        P("tower", None, None),
        P("tower", None, None),
    )
    out_specs = (
        P("tower", "batch", None),
        P("tower", "batch", None, None),
        P("tower", "batch", None),
        P("tower", "batch", None),
        P("tower", "batch", None),
        P("tower", "batch", None),
        P("tower", "batch"),
        P("tower", None, "batch"),
        P("tower", None, "batch"),
    )
    return jax.shard_map(
        partial(per_device, n) if direct else per_device_plain, mesh=mesh, in_specs=in_specs, out_specs=out_specs, check_vma=False
    )
```

```python
from functools import partial

import jax
import jax.numpy as jnp
from jax import lax
from jax.experimental import pallas as pl
from jax.experimental.pallas import tpu as pltpu
from jax.sharding import PartitionSpec as P

HEADS = 12
EPS = 1e-12
SCALE = 4.0
HIGH = lax.Precision.HIGHEST
MESH = pl.DeviceIdType.MESH
NEG = -1000000000.0
LOW = jnp.bfloat16
F32 = jnp.float32
CHUNKS = 12
MIB = 2**20


def product(left, right):
    return jnp.dot(left, right, preferred_element_type=jnp.float32)


def transposed_left(left, right):
    return lax.dot_general(
        left, right, (((0,), (0,)), ((), ())), preferred_element_type=jnp.float32
    )


def transposed_right(left, right):
    return lax.dot_general(
        left, right, (((1,), (1,)), ((), ())), preferred_element_type=jnp.float32
    )


def norm_forward(total, gain, shift):
    mean = jnp.mean(total, axis=-1, keepdims=True)
    centered = total - mean
    inverse = lax.rsqrt(jnp.mean(centered * centered, axis=-1, keepdims=True) + EPS)
    normed = centered * inverse
    return (normed * gain + shift, normed, inverse)


def norm_backward(grad, normed, inverse, gain):
    scaled = grad * gain
    first_mean = jnp.mean(scaled, axis=-1, keepdims=True)
    second_mean = jnp.mean(scaled * normed, axis=-1, keepdims=True)
    d_total = inverse * (scaled - first_mean - normed * second_mean)
    return (d_total, jnp.sum(grad * normed, axis=0), jnp.sum(grad, axis=0))


def scores_of(query_heads, key_heads, keep):
    raw = (
        jnp.einsum("sqhe,skhe->shqk", query_heads, key_heads, preferred_element_type=jnp.float32)
        * 0.125
    )
    return jnp.where(keep[:, None, None, :], raw, NEG)


def gelu_parts(z):
    t = 1.0 / (1.0 + jnp.abs(z) * (0.3275911 * 0.7071067811865476))
    bell = jnp.exp(z * z * -0.5)
    tail = t * bell * (
        0.127414796 + t * (-0.142248368 + t * (0.7107068705 + t * (-0.7265760135 + t * 0.5307027145)))
    )
    below = jnp.where(z < 0.0, tail, 1.0 - tail)
    return z * below, below + z * bell * 0.3989422804014327


def normed(total):
    mean = jnp.mean(total, axis=-1, keepdims=True)
    centered = total - mean
    inverse = lax.rsqrt(jnp.mean(centered * centered, axis=-1, keepdims=True) + EPS)
    return centered * inverse, inverse


def encoder_kernel(
    lens, x_ref, wqkv_hbm, wattn_hbm, win_hbm, wout_hbm, bin_ref, vec_ref, gain_ref,
    pooled_ref, hidden_ref, slope_ref, n1_ref, n2_ref, inv_ref, low_t_ref, query_ref, key_t_ref, value_ref, probs_ref,
    context_t_ref, x_t_ref,
    wqkv, wattn, win, wout, sems,
):
    step = pl.program_id(0)
    loads = [
        pltpu.make_async_copy(source.at[0], target, sems.at[place])
        for place, (source, target) in enumerate(
            [(wqkv_hbm, wqkv), (wattn_hbm, wattn), (win_hbm, win), (wout_hbm, wout)]
        )
    ]

    @pl.when(step == 0)
    def _():
        for load in loads:
            load.start()
        loads[0].wait()

    length = lens[step]
    x = x_ref[...]
    rows = x.shape[0]
    query = (product(x, wqkv[:, :768]) + vec_ref[0]).astype(LOW) * 0.125
    key = product(x, wqkv[:, 768:1536]).astype(LOW)
    value = (product(x, wqkv[:, 1536:]) + vec_ref[1]).astype(LOW)
    query_ref[...] = query
    value_ref[...] = value
    key_t_ref[...] = key.T
    x_t_ref[...] = x.T
    value_t = value.T
    blocked = jnp.where(lax.broadcasted_iota(jnp.int32, (rows, 1), 0) < length, 0.0, NEG)
    lane = lax.broadcasted_iota(jnp.int32, (rows, 128), 1)

    def scores_of_head(head):
        pair = slice(128 * (head // 2), 128 * (head // 2 + 1))
        mine = (lane < 64) if head % 2 == 0 else (lane >= 64)
        key_one = jnp.where(mine, key[:, pair], jnp.zeros((), LOW))
        return transposed_right(key_one, query[:, pair]) + blocked

    def context_of_head(head, probs):
        context_t_ref[64 * head:64 * (head + 1), :] = product(
            value_t[64 * head:64 * (head + 1)], probs
        ).astype(LOW)

    ahead, behind = [scores_of_head(head) for head in range(4)], []
    for head in range(HEADS):
        if head + 4 < HEADS:
            ahead.append(scores_of_head(head + 4))
        scores = ahead.pop(0)
        weights = jnp.exp(scores - jnp.max(scores, axis=0, keepdims=True))
        probs = (weights * (1.0 / jnp.sum(weights, axis=0, keepdims=True))).astype(LOW)
        probs_ref[:, 256 * head:256 * (head + 1)] = probs
        behind.append((head, probs))
        if len(behind) > 2:
            context_of_head(*behind.pop(0))
    for item in behind:
        context_of_head(*item)

    @pl.when(step == 0)
    def _():
        loads[1].wait()

    attended = transposed_left(context_t_ref[...], wattn[...]) + vec_ref[2]
    n1, inv1 = normed(x.astype(F32) + attended)
    first = n1 * gain_ref[0, 0:1] + vec_ref[3]
    first_low = first.astype(LOW)
    low_t_ref[...] = first_low.T
    n1_ref[...] = n1.astype(LOW)

    @pl.when(step == 0)
    def _():
        loads[2].wait()
        loads[3].wait()

    total = first + vec_ref[4]
    blocks = [slice(768 * part, 768 * (part + 1)) for part in range(4)]
    ahead, late = product(first_low, win[:, blocks[0]]), None
    for part in range(4):
        before = ahead
        if part + 1 < 4:
            ahead = product(first_low, win[:, blocks[part + 1]])
        hidden, slope = gelu_parts(before + bin_ref[:, blocks[part]])
        hidden = hidden.astype(LOW)
        hidden_ref[:, blocks[part]] = hidden
        slope_ref[:, blocks[part]] = slope.astype(LOW)
        if late is not None:
            total = total + product(late, wout[blocks[part - 1], :])
        late = hidden
    total = total + product(late, wout[blocks[3], :])
    n2, inv2 = normed(total)
    n2_ref[...] = n2.astype(LOW)
    inv_ref[...] = jnp.where(lane < 64, inv1, inv2)
    output = n2 * gain_ref[0, 1:2] + vec_ref[5]
    keep = lax.broadcasted_iota(jnp.int32, (rows, 1), 0) < length
    pooled_ref[pl.ds(step, 1)] = jnp.sum(jnp.where(keep, output, 0.0), axis=0, keepdims=True) / length.astype(F32)


def encoder(lens, x, w_qkv, w_attn, w_in, w_out, b_in, vectors, gains):
    seqs = lens.shape[0]
    rows = x.shape[0]
    per = rows // seqs

    def by_rows(width):
        return pl.BlockSpec((per, width), lambda s, *_: (s, 0))

    def by_columns(height):
        return pl.BlockSpec((height, per), lambda s, *_: (0, s))

    def full(*shape):
        return pl.BlockSpec(shape, lambda s, *_: (0,) * len(shape))

    anywhere = pl.BlockSpec(memory_space=pl.ANY)
    def wide(width, kind=LOW):
        return by_rows(width), jax.ShapeDtypeStruct((rows, width), kind)

    tall = by_columns(768), jax.ShapeDtypeStruct((768, rows), LOW)
    kept = [
        wide(3072), wide(3072), wide(768), wide(768), wide(128, F32), tall,
        wide(768), tall, wide(768), wide(3072), tall, tall,
    ]
    return pl.pallas_call(
        encoder_kernel,
        grid_spec=pltpu.PrefetchScalarGridSpec(
            num_scalar_prefetch=1,
            grid=(seqs,),
            in_specs=[by_rows(768)] + [anywhere] * 4 + [full(1, 3072), full(6, 1, 768), full(1, 2, 768)],
            out_specs=[full(seqs, 768)] + [spec for spec, _ in kept],
            scratch_shapes=[
                pltpu.VMEM((768, 2304), LOW), pltpu.VMEM((768, 768), LOW),
                pltpu.VMEM((768, 3072), LOW), pltpu.VMEM((3072, 768), LOW),
                pltpu.SemaphoreType.DMA((4,)),
            ],
        ),
        out_shape=[jax.ShapeDtypeStruct((seqs, 768), F32)] + [shape for _, shape in kept],
        compiler_params=pltpu.CompilerParams(vmem_limit_bytes=56 * MIB),
        name="encoder",
    )(lens, x, w_qkv, w_attn, w_in, w_out, b_in, vectors, gains)


def second_norm_backward(grad_row, length, first_row, n2, inv2, gain):
    scaled = grad_row * gain
    mean = jnp.mean(scaled, axis=1, keepdims=True)
    along = jnp.mean(scaled * n2, axis=1, keepdims=True)
    keep = first_row + lax.broadcasted_iota(jnp.int32, (n2.shape[0], 1), 0) < length
    return jnp.where(keep, inv2 * (scaled - mean - n2 * along), 0.0), keep


def select(condition):
    return jnp.where(condition, 1.0, 0.0)


def aligned(start, size, multiple):
    return pl.ds(pl.multiple_of(start, multiple), size)


class Sums:
    def __init__(self, n, scratch):
        (self.grads, self.paired, self.crossed, self.rows_got, self.got, self.pair_send, self.pair_recv,
         self.cross_send, self.cross_recv, self.z_send, self.z_recv) = scratch
        self.tower, self.me = lax.axis_index("tower"), lax.axis_index("batch")
        self.depth = n // 4
        self.z, self.y, self.core = self.me // 4, lax.rem(self.me // 2, 2), lax.rem(self.me, 2)

    def z_at(self, offset):
        return lax.rem(self.z + offset, self.depth)

    def device(self, z, y, core):
        return (self.tower, z * 4 + y * 2 + core)

    def pair_copy(self, chunk):
        return pltpu.make_async_remote_copy(
            src_ref=self.grads.at[chunk, :, 1 - self.core], dst_ref=self.paired.at[chunk],
            send_sem=self.pair_send.at[chunk], recv_sem=self.pair_recv.at[chunk],
            device_id=self.device(self.z, self.y, 1 - self.core), device_id_type=MESH,
        )

    def cross_copy(self, chunk):
        return pltpu.make_async_remote_copy(
            src_ref=self.grads.at[chunk, 1 - self.y, self.core], dst_ref=self.crossed.at[chunk],
            send_sem=self.cross_send.at[chunk], recv_sem=self.cross_recv.at[chunk],
            device_id=self.device(self.z, 1 - self.y, self.core), device_id_type=MESH,
        )

    def rows_copy(self, chunk):
        return pltpu.make_async_remote_copy(
            src_ref=self.grads.at[chunk, self.y, self.core], dst_ref=self.rows_got.at[chunk],
            send_sem=self.z_send.at[chunk, 0], recv_sem=self.z_recv.at[chunk, 0],
            device_id=self.device(self.z_at(chunk + 1), self.y, self.core), device_id_type=MESH,
        )

    def z_copy(self, chunk, offset):
        return pltpu.make_async_remote_copy(
            src_ref=self.grads.at[chunk, self.y, self.core, self.z_at(offset)],
            dst_ref=self.got.at[chunk - 4, offset - 1],
            send_sem=self.z_send.at[chunk, offset - 1], recv_sem=self.z_recv.at[chunk, offset - 1],
            device_id=self.device(self.z_at(offset), self.y, self.core), device_id_type=MESH,
        )

    def pair(self, chunk):
        self.pair_copy(chunk).start()

    def cross(self, chunk):
        self.pair_copy(chunk).wait_recv()
        place = (chunk, 1 - self.y, self.core)
        self.grads[place] = (self.grads[place].astype(F32) + self.paired[chunk, 1 - self.y].astype(F32)).astype(LOW)
        self.cross_copy(chunk).start()

    def spread(self, chunk, by_rows=False, last=False):
        self.cross_copy(chunk).wait_recv()
        place = (chunk, self.y, self.core)
        self.grads[place] = (
            self.grads[place].astype(F32) + self.paired[chunk, self.y].astype(F32) + self.crossed[chunk].astype(F32)
        ).astype(LOW)
        if by_rows:
            if not last:
                self.rows_copy(chunk).start()
        else:
            for offset in range(1, self.depth):
                self.z_copy(chunk, offset).start()

    def rows_total(self, part):
        total = self.grads[3, self.y, self.core, part].astype(F32)
        for chunk in range(3):
            total = total + self.rows_got[chunk, part].astype(F32)
        return total

    def total(self, chunk):
        total = self.grads[chunk, self.y, self.core, self.z].astype(F32)
        for offset in range(1, self.depth):
            self.z_copy(chunk, offset).wait_recv()
            total = total + self.got[chunk - 4, offset - 1].astype(F32)
        return total

    def close(self):
        @pl.loop(0, CHUNKS)
        def _(chunk):
            self.pair_copy(chunk).wait_send()
            self.cross_copy(chunk).wait_send()

        for chunk in range(3):
            self.rows_copy(chunk).wait_send()

        @pl.loop(4, CHUNKS)
        def _(chunk):
            for offset in range(1, self.depth):
                self.z_copy(chunk, offset).wait_send()


def d_pooled_of(n, tower, me, everyone):
    seqs = 4 * n
    packed = everyone[...]
    questions = packed[:n].reshape(16 * n, 256)
    passages = packed[n:].reshape(16 * n, 256)
    rows = lax.broadcasted_iota(jnp.int32, (seqs, 16 * n), 0)
    places = lax.broadcasted_iota(jnp.int32, (seqs, 16 * n), 1)
    owner, lane = rows // 4, lax.rem(rows, 4)

    def picked(values, row):
        return product(select(places == owner * 16 + row).astype(LOW), values)

    def whole(values):
        parts = [product(select(places == owner * 16 + 4 * part + lane).astype(LOW), values) for part in range(3)]
        return jnp.concatenate(parts, axis=1)

    column_lane = lax.broadcasted_iota(jnp.int32, (seqs, 256), 1)
    column_want = lax.rem(lax.broadcasted_iota(jnp.int32, (seqs, 256), 0), 4)

    def column(row):
        return jnp.sum(
            jnp.where(column_lane == column_want, picked(passages, row), 0.0), axis=1, keepdims=True
        )

    question_float, passage_float = whole(questions), whole(passages)
    positives, sets = column(12), column(13)
    first = lax.broadcasted_iota(jnp.int32, (seqs, seqs), 0)
    second = lax.broadcasted_iota(jnp.int32, (seqs, seqs), 1)
    set_row = jnp.sum(jnp.where(first == second, sets, 0.0), axis=0, keepdims=True)
    chosen = second.astype(F32) == positives
    query_set = jnp.sum(jnp.where(chosen, set_row, 0.0), axis=1, keepdims=True)
    logits = transposed_right(question_float.astype(LOW), passage_float.astype(LOW)) * SCALE
    masked = jnp.where(set_row == query_set, logits, NEG)
    weights = jnp.exp(masked - jnp.max(masked, axis=1, keepdims=True))
    softmax = weights / jnp.sum(weights, axis=1, keepdims=True)
    d_logits = (softmax - select(chosen)) * SCALE
    mine_row = lax.broadcasted_iota(jnp.int32, (8, seqs), 0)
    mine_column = lax.broadcasted_iota(jnp.int32, (8, seqs), 1)
    own = select((mine_column == me * 4 + mine_row) & (mine_row < 4))
    by_question = jnp.dot(own, d_logits, precision=HIGH, preferred_element_type=F32)
    by_passage = lax.dot_general(
        own, d_logits, (((1,), (1,)), ((), ())), precision=HIGH, preferred_element_type=F32
    )
    is_passage = tower == 1
    terms = jnp.where(is_passage, by_passage, by_question)
    others = jnp.where(is_passage, question_float, passage_float)
    grad = jnp.dot(terms, others, precision=HIGH, preferred_element_type=F32)
    return jnp.where(is_passage, grad, grad.astype(LOW).astype(F32))


def backward_kernel(
    n, lens, positives, datasets, pooled_ref, gain_ref, wqkv_hbm, wattn_hbm, win_hbm, wout_hbm,
    hidden_hbm, slope_hbm, n1_hbm, n2_hbm, inv_hbm, low_t_hbm, query_hbm, key_t_hbm, value_hbm, probs_hbm,
    context_t_hbm, x_t_hbm,
    out_ref, in_ref, attn_ref, qkv_ref, summed_small_ref, tokens_out,
    grads, paired, crossed, rows_got, got, pair_send, pair_recv, cross_send, cross_recv, z_send, z_recv,
    first_weights, second_weights, wide, tall, rows_a, rows_b, rows_c, key_t, context_t, inv, stage,
    rows_small, bias_in, small, small_got, mine, everyone, d_pooled,
    sems, stage_sems, small_send, small_recv, pool_send, pool_recv,
):
    tower, me = lax.axis_index("tower"), lax.axis_index("batch")
    flat = tower * n + me
    everybody = 2 * n
    sums = Sums(
        n, (grads, paired, crossed, rows_got, got, pair_send, pair_recv, cross_send, cross_recv, z_send, z_recv)
    )
    barrier = pltpu.get_barrier_semaphore()

    def other_device(step):
        other = lax.rem(flat + step, everybody)
        return other // n, lax.rem(other, n)

    @pl.loop(1, everybody)
    def _(step):
        pl.semaphore_signal(barrier, inc=1, device_id=other_device(step), device_id_type=MESH)

    def load(place, source, target):
        return pltpu.make_async_copy(source, target, sems.at[place])

    def seq_rows(seq):
        return aligned(seq * 256, 256, 256)

    def block(part):
        return slice(768 * part, 768 * (part + 1))

    n2_load, inv_load = load(0, n2_hbm, rows_a), load(1, inv_hbm, inv)
    hidden_loads = [
        load(2 + part, hidden_hbm.at[:, aligned(sums.z_at(part + 1) * 768, 768, 128)], wide.at[:, block(part)])
        for part in range(4)
    ]
    slope_loads = [load(10 + part, slope_hbm.at[:, block(part)], wide.at[:, block(part)]) for part in range(4)]
    out_load = load(14, wout_hbm.at[0], first_weights)
    in_loads = [load(15 + part, win_hbm.at[0, :, block(part)], second_weights.at[block(part)]) for part in range(4)]
    n1_load, low_load = load(19, n1_hbm, rows_b), load(20, low_t_hbm, tall)
    key_load, context_load = load(21, key_t_hbm, key_t), load(22, context_t_hbm, context_t)
    attn_load = load(23, wattn_hbm.at[0], first_weights.at[block(0)])
    qkv_loads = [
        load(24 + part, wqkv_hbm.at[0, :, block(part)], first_weights.at[block(part + 1)]) for part in range(3)
    ]
    query_load, value_load, x_load = load(27, query_hbm, rows_a), load(28, value_hbm, rows_b), load(29, x_t_hbm, tall)

    def probs_load(seq):
        return load(30 + seq, probs_hbm.at[seq_rows(seq)], wide.at[seq_rows(seq)])

    for copy in [n2_load, inv_load] + hidden_loads + [out_load] + in_loads + [n1_load, low_load, key_load, context_load]:
        copy.start()

    row = lax.broadcasted_iota(jnp.int32, (4, 256), 0)
    lane = lax.broadcasted_iota(jnp.int32, (4, 256), 1)
    extra = jnp.zeros((4, 256), F32)
    for seq in range(4):
        for place, numbers in enumerate((positives, datasets)):
            extra = jnp.where((row == place) & (lane == seq), numbers[seq].astype(F32), extra)
    pooled = pooled_ref[...]
    pooled_block = jnp.concatenate(
        [pooled[:, 0:256], pooled[:, 256:512], pooled[:, 512:768], extra], axis=0
    ).astype(LOW)
    mine[...] = pooled_block
    everyone[flat] = pooled_block
    rows_small[...] = jnp.zeros_like(rows_small)
    bias_in[...] = jnp.zeros_like(bias_in)
    pl.semaphore_wait(barrier, everybody - 1)

    def pool_copy(step):
        return pltpu.make_async_remote_copy(
            src_ref=mine, dst_ref=everyone.at[flat], send_sem=pool_send.at[step], recv_sem=pool_recv.at[step],
            device_id=other_device(step), device_id_type=MESH,
        )

    @pl.loop(1, everybody)
    def _(step):
        pool_copy(step).start()

    @pl.loop(1, everybody)
    def _(step):
        pool_copy(step).wait_recv()

    d_pooled[...] = d_pooled_of(n, tower, me, everyone)

    n2_load.wait()
    inv_load.wait()

    def second_backward(seq):
        length = lens[seq]
        grad_row = d_pooled[pl.ds(seq, 1)] / length.astype(F32)
        normal = rows_a[seq_rows(seq)].astype(F32)
        d_second, keep = second_norm_backward(
            grad_row, length, 0, normal, inv[seq_rows(seq), 64:65], gain_ref[0, 1:2]
        )
        return d_second, keep, normal, grad_row

    @pl.loop(0, 4)
    def _(seq):
        d_second, keep, normal, grad_row = second_backward(seq)
        low = d_second.astype(LOW)
        rows_c[seq_rows(seq)] = low
        rows_small[4:5] += jnp.sum(low.astype(F32), axis=0, keepdims=True)
        rows_small[5:6] += d_pooled[pl.ds(seq, 1)]
        rows_small[7:8] += grad_row * jnp.sum(jnp.where(keep, normal, 0.0), axis=0, keepdims=True)

    for part in range(4):
        hidden_loads[part].wait()
        for y in range(2):
            columns = slice(768 * part + 384 * y, 768 * part + 384 * (y + 1))
            grads[part, y] = transposed_left(wide[:, columns], rows_c[...]).astype(LOW).reshape(2, 4, 48, 768)
        slope_loads[part].start()
        sums.pair(part)
        if part in (1, 2):
            sums.cross(part - 1)

    @pl.loop(1, everybody)
    def _(step):
        pool_copy(step).wait_send()

    for copy in [out_load] + in_loads + [n1_load] + slope_loads:
        copy.wait()

    def stage_copy(seq, kind):
        slot, rows = stage.at[lax.rem(seq, 2)], tokens_out.at[seq_rows(seq)]
        source, target = (rows, slot) if kind == 1 else (slot, rows)
        return pltpu.make_async_copy(source, target, stage_sems.at[kind, seq])

    @pl.loop(0, 4)
    def _(seq):
        @pl.when(seq >= 1)
        def _():
            sums.spread(lax.max(seq - 1, 0), by_rows=True)

        @pl.when((seq >= 1) & (seq <= 2))
        def _():
            sums.cross(lax.min(seq + 1, 3))

        rows = seq_rows(seq)
        d_second = second_backward(seq)[0]
        d_branch = rows_c[rows]
        d_first = d_second
        for part in range(4):
            d_pre = (
                transposed_right(d_branch, first_weights[block(part), :]) * wide[rows, block(part)].astype(F32)
            ).astype(LOW)
            wide[rows, block(part)] = d_pre
            bias_in[:, block(part)] += jnp.sum(d_pre.astype(F32), axis=0, keepdims=True)
            d_first = d_first + transposed_right(d_pre, second_weights[block(part), :])
        normal = rows_b[rows].astype(F32)
        scaled = d_first * gain_ref[0, 0:1]
        mean = jnp.mean(scaled, axis=1, keepdims=True)
        along = jnp.mean(scaled * normal, axis=1, keepdims=True)
        d_sum_one = inv[rows, 0:1] * (scaled - mean - normal * along)

        @pl.when(seq >= 2)
        def _():
            stage_copy(lax.max(seq - 2, 0), 0).wait()

        stage[lax.rem(seq, 2)] = d_sum_one
        stage_copy(seq, 0).start()
        d_attended = d_sum_one.astype(LOW)
        rows_c[rows] = d_attended
        rows_small[2:3] += jnp.sum(d_attended.astype(F32), axis=0, keepdims=True)
        rows_small[3:4] += jnp.sum(d_first, axis=0, keepdims=True)
        rows_small[6:7] += jnp.sum(d_first * normal, axis=0, keepdims=True)

    for copy in [attn_load] + qkv_loads + [query_load, value_load]:
        copy.start()
    low_load.wait()

    def store(chunk, rows_ref, columns):
        for half in range(2):
            grad = product(rows_ref[384 * half:384 * (half + 1)], columns).astype(LOW)
            for z in range(2):
                grads[chunk, :, :, 2 * half + z] = grad[192 * z:192 * (z + 1)].reshape(2, 2, 48, 768)
        sums.pair(chunk)

    for part in range(4):
        store(4 + part, tall, wide[:, block(part)])
        if part == 1:
            sums.spread(3, by_rows=True, last=True)
        if part in (1, 2):
            sums.cross(3 + part)
    for seq in range(4):
        probs_load(seq).start()
    x_load.start()

    context_load.wait()
    store(8, context_t, rows_c[...])
    for copy in [attn_load] + qkv_loads + [query_load, value_load, key_load]:
        copy.wait()
    lane = lax.broadcasted_iota(jnp.int32, (256, 128), 1)
    none = jnp.zeros((), LOW)

    @pl.loop(0, 4)
    def _(seq):
        rows = seq_rows(seq)

        @pl.when(seq >= 1)
        def _():
            sums.spread(3 + lax.max(seq, 1))
            sums.cross(5 + lax.max(seq, 1))

        probs_load(seq).wait()
        d_attended = rows_c[rows]
        weight = first_weights[block(0), :]
        d_context = transposed_right(d_attended, weight).astype(LOW)
        d_context_t = transposed_right(weight, d_attended).astype(LOW)
        for pair in range(6):
            lanes = slice(128 * pair, 128 * (pair + 1))
            key_pair, query_pair, value_pair = key_t[lanes, rows], rows_a[rows, lanes], rows_b[rows, lanes]
            d_context_pair, d_context_t_pair = d_context[:, lanes], d_context_t[lanes]
            weighed = d_context_t_pair.astype(F32) * context_t[lanes, rows].astype(F32)
            d_queries, d_keys, d_values = [], [], []
            for one in range(2):
                half = slice(64 * one, 64 * (one + 1))
                head = 2 * pair + one
                prob = wide[rows, 256 * head:256 * (head + 1)]
                value_one = jnp.where((lane < 64) if one == 0 else (lane >= 64), value_pair, none)
                d_prob = product(value_one, d_context_t_pair)
                row_sum = jnp.sum(weighed[half], axis=0, keepdims=True)
                d_score = (prob.astype(F32) * (d_prob - row_sum)).astype(LOW)
                d_values.append(product(prob, d_context_pair))
                d_keys.append(product(d_score, query_pair))
                d_queries.append(product(key_pair[half], d_score))
            d_query = (jnp.concatenate(d_queries, axis=0).T * 0.125).astype(LOW)
            d_key = jnp.where(lane < 64, d_keys[0], d_keys[1]).astype(LOW)
            d_value = jnp.where(lane < 64, d_values[0], d_values[1]).astype(LOW)
            for part, value in enumerate((d_query, d_key, d_value)):
                second_weights[aligned(1024 * part + seq * 256, 256, 256), lanes] = value
            rows_small[0:1, lanes] += jnp.sum(d_query.astype(F32), axis=0, keepdims=True)
            rows_small[1:2, lanes] += jnp.sum(d_value.astype(F32), axis=0, keepdims=True)

    for seq in (2, 3):
        stage_copy(seq, 0).wait()
    for seq in (0, 1):
        stage_copy(seq, 1).start()
    x_load.wait()
    sums.spread(7)
    for part in range(3):
        store(9 + part, tall, second_weights[1024 * part:1024 * (part + 1), :])
        if part == 1:
            sums.cross(9)

    bundle, bias_row = rows_small[...], bias_in[...]
    small[...] = jnp.zeros_like(small)
    for device in range(n):
        small[device, 0:8, 0:48] = bundle[:, 48 * device:48 * (device + 1)]
        for part in range(4):
            start = 192 * device + 48 * part
            small[device, 8 + part:9 + part, 0:48] = bias_row[:, start:start + 48]

    def small_copy(step):
        other = lax.rem(me + step, n)
        return pltpu.make_async_remote_copy(
            src_ref=small.at[other], dst_ref=small_got.at[step],
            send_sem=small_send.at[step], recv_sem=small_recv.at[step],
            device_id=(tower, other), device_id_type=MESH,
        )

    sums.spread(8)
    sums.cross(10)

    @pl.loop(1, n)
    def _(step):
        small_copy(step).start()

    def tokens(seq):
        stage_copy(seq, 1).wait()
        slot = seq % 2
        total = stage[slot]
        for part in range(3):
            total = total + transposed_right(
                second_weights[1024 * part + seq * 256:1024 * part + seq * 256 + 256, :],
                first_weights[block(part + 1), :],
            )
        stage[slot] = total
        stage_copy(seq, 2).start()

    tokens(0)
    tokens(1)
    sums.spread(9)
    sums.cross(11)
    for seq in (2, 3):
        stage_copy(seq - 2, 2).wait()
        stage_copy(seq, 1).start()
    tokens(2)
    tokens(3)
    summed_small_ref[...] = small[me]

    @pl.loop(1, n)
    def _(step):
        small_copy(step).wait()
        summed_small_ref[...] += small_got[step]

    for chunk in range(3):
        sums.rows_copy(chunk).wait_recv()
    for part in range(4):
        out_ref[48 * part:48 * (part + 1)] = sums.rows_total(part)
    for chunk in range(4, 8):
        in_ref[:, block(chunk - 4)] = sums.total(chunk)
    sums.spread(10)
    attn_ref[...] = sums.total(8)
    qkv_ref[:, block(0)] = sums.total(9)
    sums.spread(11)
    qkv_ref[:, block(1)] = sums.total(10)
    qkv_ref[:, block(2)] = sums.total(11)
    for seq in (2, 3):
        stage_copy(seq, 2).wait()
    sums.close()


def backward(lens, positives, datasets, pooled, gains, weights, activations, n):
    rows = activations[0].shape[0]
    anywhere = pl.BlockSpec(memory_space=pl.ANY)
    vmem = pl.BlockSpec(memory_space=pltpu.VMEM)
    scalars = pl.BlockSpec(memory_space=pltpu.SMEM)
    tile = (48, 768)
    dma = pltpu.SemaphoreType.DMA
    return pl.pallas_call(
        partial(backward_kernel, n),
        in_specs=[scalars] * 3 + [vmem] * 2 + [anywhere] * (4 + len(activations)),
        out_specs=[vmem] * 5 + [anywhere],
        out_shape=[
            jax.ShapeDtypeStruct(shape, F32)
            for shape in ((192, 768), (48, 3072), (48, 768), (48, 2304), (16, 128), (rows, 768))
        ],
        scratch_shapes=[
            pltpu.VMEM((CHUNKS, 2, 2, 4) + tile, LOW), pltpu.VMEM((CHUNKS, 2, 4) + tile, LOW),
            pltpu.VMEM((CHUNKS, 4) + tile, LOW), pltpu.VMEM((3, 4) + tile, LOW), pltpu.VMEM((CHUNKS - 4, 3) + tile, LOW),
            dma((CHUNKS,)), dma((CHUNKS,)), dma((CHUNKS,)), dma((CHUNKS,)), dma((CHUNKS, 3)), dma((CHUNKS, 3)),
            pltpu.VMEM((3072, 768), LOW), pltpu.VMEM((3072, 768), LOW), pltpu.VMEM((rows, 3072), LOW),
            pltpu.VMEM((768, rows), LOW), pltpu.VMEM((rows, 768), LOW), pltpu.VMEM((rows, 768), LOW),
            pltpu.VMEM((rows, 768), LOW), pltpu.VMEM((768, rows), LOW), pltpu.VMEM((768, rows), LOW),
            pltpu.VMEM((rows, 128), F32), pltpu.VMEM((2, 256, 768), F32),
            pltpu.VMEM((8, 768), F32), pltpu.VMEM((1, 3072), F32),
            pltpu.VMEM((n, 16, 128), F32), pltpu.VMEM((n, 16, 128), F32),
            pltpu.VMEM((16, 256), LOW), pltpu.VMEM((2 * n, 16, 256), LOW), pltpu.VMEM((8, 768), F32),
            dma((34,)), dma((3, 4)), dma((n,)), dma((n,)), dma((2 * n,)), dma((2 * n,)),
        ],
        compiler_params=pltpu.CompilerParams(collective_id=1, has_side_effects=True, vmem_limit_bytes=60 * MIB),
        name="backward",
    )(lens, positives, datasets, pooled, gains, *weights, *activations)


def deliver_kernel(
    out_hbm, in_hbm, attn_hbm, qkv_hbm, small_hbm, tokens_hbm,
    out_to, in_to, attn_to, qkv_to, bias_in_to, vectors_to, gains_to, tokens_to,
    out_held, in_held, attn_held, qkv_held, small_held, held, sems,
):
    parts, rows = held.shape[0], held.shape[1]
    ways = [
        (tokens_hbm.at[pl.ds(rows * part, rows)], held.at[part], tokens_to.at[pl.ds(rows * part, rows)])
        for part in range(parts)
    ] + [
        (out_hbm, out_held, out_to), (in_hbm, in_held, in_to), (attn_hbm, attn_held, attn_to),
        (qkv_hbm, qkv_held, qkv_to),
    ]
    fetches = [
        pltpu.make_async_copy(source, middle, sems.at[0, place]) for place, (source, middle, _) in enumerate(ways)
    ]
    sends = [
        pltpu.make_async_copy(middle, target, sems.at[1, place]) for place, (_, middle, target) in enumerate(ways)
    ]
    small_fetch = pltpu.make_async_copy(small_hbm, small_held, sems.at[0, len(ways)])
    small_fetch.start()
    for fetch in fetches:
        fetch.start()
    for fetch, send in zip(fetches, sends):
        fetch.wait()
        send.start()
    small_fetch.wait()
    small = small_held[...]
    for row in range(6):
        vectors_to[row] = small[row:row + 1, :48]
    gains_to[...] = small[6:8, :48]
    bias_in_to[...] = jnp.concatenate([small[8 + part:9 + part, :48] for part in range(4)], axis=1)
    for send in sends:
        send.wait()


def deliver(*arrays):
    *sums, small, tokens = arrays
    anywhere = pl.BlockSpec(memory_space=pl.ANY)
    vmem = pl.BlockSpec(memory_space=pltpu.VMEM)
    shapes = [array.shape for array in sums] + [(1, 192), (6, 1, 48), (2, 48), tokens.shape]
    rows, width = tokens.shape
    parts = 4
    return pl.pallas_call(
        deliver_kernel,
        in_specs=[anywhere] * 6,
        out_specs=[anywhere] * 4 + [vmem] * 3 + [anywhere],
        out_shape=[jax.ShapeDtypeStruct(shape, F32) for shape in shapes],
        scratch_shapes=[pltpu.VMEM(array.shape, F32) for array in sums]
        + [pltpu.VMEM(small.shape, F32), pltpu.VMEM((parts, rows // parts, width), F32)]
        + [pltpu.SemaphoreType.DMA((2, parts + 5))],
        compiler_params=pltpu.CompilerParams(vmem_limit_bytes=60 * MIB),
        name="deliver",
    )(*arrays)


def per_device(
    n,
    tokens, lengths, positives, datasets, w_qkv, w_attn_out, w_ffn_in, w_ffn_out, b_ffn_in, biases, gains,
):
    seq_count, seq_len, width = (tokens.shape[1], tokens.shape[2], tokens.shape[3])
    lens = lengths[0]
    inputs = tokens[0].reshape(seq_count * seq_len, width)
    weights = (w_qkv, w_attn_out, w_ffn_in, w_ffn_out)
    pooled, *activations = encoder(lens, inputs, *weights, b_ffn_in, biases.transpose(1, 0, 2), gains)
    *sums, grad_tokens = backward(lens, positives, datasets, pooled, gains, weights, activations, n)
    summed_out, summed_in, summed_attn, summed_qkv, bias_in, vectors, scales, grad_tokens = deliver(*sums, grad_tokens)
    return (
        pooled[None],
        grad_tokens.reshape(1, seq_count, seq_len, width),
        summed_qkv[None],
        summed_attn[None],
        summed_in[None],
        summed_out[None],
        bias_in,
        vectors.transpose(1, 0, 2),
        scales[None],
    )


def from_behind(value, axis, steps):
    count = lax.axis_size(axis)
    leading, last = (max(0, -steps), min(count, count - steps))
    return lax.ppermute(value, axis, [(source, source + steps) for source in range(leading, last)])


def loss_gradient_plain(pooled, positives, datasets):
    seq_count = pooled.shape[0]
    mine = pooled.astype(jnp.bfloat16)
    questions = from_behind(mine, "tower", 1)
    everyone, every_set = (
        lax.all_gather(mine, "batch", axis=0, tiled=True),
        lax.all_gather(datasets.astype(jnp.bfloat16), "batch", axis=0, tiled=True),
    )
    total_seqs = everyone.shape[0]
    columns = lax.broadcasted_iota(jnp.int32, (seq_count, total_seqs), 1)
    chosen = columns == positives[:, None]
    set_row = every_set.astype(jnp.float32)[None, :]
    query_set = jnp.sum(jnp.where(chosen, set_row, 0.0), axis=1, keepdims=True)
    allowed = set_row == query_set
    question_float = questions.astype(jnp.float32)
    everyone_float = everyone.astype(jnp.float32)
    logits = jnp.dot(question_float, everyone_float.T, precision=HIGH) * SCALE
    masked = jnp.where(allowed, logits, NEG)
    softmax_rows = jnp.exp(masked - jax.nn.logsumexp(masked, axis=1, keepdims=True))
    d_logits = (softmax_rows - chosen.astype(jnp.float32)) * SCALE
    d_questions = jnp.dot(d_logits, everyone_float, precision=HIGH).astype(jnp.bfloat16)
    passage_terms = jnp.dot(d_logits.T, question_float, precision=HIGH)
    d_passages = lax.psum_scatter(passage_terms, "batch", scatter_dimension=0, tiled=True)
    returned = from_behind(d_questions, "tower", -1)
    is_passage = lax.axis_index("tower") == 1
    return jnp.where(is_passage, d_passages, returned.astype(jnp.float32))


def per_device_plain(

    tokens, lengths, positives, datasets, w_qkv, w_attn_out, w_ffn_in, w_ffn_out, b_ffn_in, biases, gains,
):
    seq_count, seq_len, width = (tokens.shape[1], tokens.shape[2], tokens.shape[3])
    head_size = width // HEADS
    rows = seq_count * seq_len
    inputs = tokens[0].reshape(rows, width)
    lens = lengths[0]
    weight_qkv = w_qkv[0]
    weight_attn = w_attn_out[0]
    weight_in = w_ffn_in[0]
    weight_out = w_ffn_out[0]
    bias_in = b_ffn_in[0]
    vectors = biases[0]
    scales = gains[0]
    positions = lax.broadcasted_iota(jnp.int32, (seq_count, seq_len), 1)
    keep = positions < lens[:, None]
    keep_float = keep.astype(jnp.float32)
    lens_float = lens.astype(jnp.float32)[:, None]
    shape_heads = (seq_count, seq_len, HEADS, head_size)
    projected = product(inputs, weight_qkv)
    query = (projected[:, :width] + vectors[0]).astype(jnp.bfloat16)
    key_rows = projected[:, width : 2 * width].astype(jnp.bfloat16)
    value = (projected[:, 2 * width :] + vectors[1]).astype(jnp.bfloat16)
    query_heads = query.reshape(shape_heads)
    key_heads = key_rows.reshape(shape_heads)
    value_heads = value.reshape(shape_heads)
    scores = scores_of(query_heads, key_heads, keep)
    log_total = jax.nn.logsumexp(scores, axis=-1, keepdims=True)
    probs_low = jnp.exp(scores - log_total).astype(jnp.bfloat16)
    context = jnp.einsum(
        "shqk,skhe->sqhe", probs_low, value_heads, preferred_element_type=jnp.float32
    )
    context = context.reshape(rows, width).astype(jnp.bfloat16)
    attended = product(context, weight_attn) + vectors[2]
    first_norm, normed_one, inverse_one = norm_forward(
        inputs.astype(jnp.float32) + attended, scales[0], vectors[3]
    )
    first_low = first_norm.astype(jnp.bfloat16)
    hidden_pre = product(first_low, weight_in) + bias_in
    hidden = jax.nn.gelu(hidden_pre, approximate=False).astype(jnp.bfloat16)
    branch = product(hidden, weight_out) + vectors[4]
    output, normed_two, inverse_two = norm_forward(first_norm + branch, scales[1], vectors[5])
    pooled = (
        jnp.sum(output.reshape(seq_count, seq_len, width) * keep_float[:, :, None], axis=1)
        / lens_float
    )
    d_pooled = loss_gradient_plain(pooled, positives, datasets)
    d_output = ((d_pooled / lens_float)[:, None, :] * keep_float[:, :, None]).reshape(rows, width)
    d_second, d_gain_two, d_shift_two = norm_backward(d_output, normed_two, inverse_two, scales[1])
    d_branch = d_second.astype(jnp.bfloat16)
    g_weight_out = transposed_left(hidden, d_branch)
    g_bias_out = jnp.sum(d_branch.astype(jnp.float32), axis=0)
    d_hidden = transposed_right(d_branch, weight_out)
    gelu_pull = jax.vjp(partial(jax.nn.gelu, approximate=False), hidden_pre)[1]
    d_pre = gelu_pull(d_hidden)[0].astype(jnp.bfloat16)
    g_weight_in = transposed_left(first_low, d_pre)
    g_bias_in = jnp.sum(d_pre.astype(jnp.float32), axis=0)
    d_first = d_second + transposed_right(d_pre, weight_in)
    d_sum_one, d_gain_one, d_shift_one = norm_backward(d_first, normed_one, inverse_one, scales[0])
    d_attended = d_sum_one.astype(jnp.bfloat16)
    g_weight_attn = transposed_left(context, d_attended)
    g_bias_attn = jnp.sum(d_attended.astype(jnp.float32), axis=0)
    d_context = transposed_right(d_attended, weight_attn).astype(jnp.bfloat16).reshape(shape_heads)
    again = scores_of(query_heads, key_heads, keep)
    probs = jnp.exp(again - log_total)
    d_value = jnp.einsum(
        "shqk,sqhe->skhe", probs.astype(jnp.bfloat16), d_context, preferred_element_type=jnp.float32
    )
    d_probs = jnp.einsum(
        "sqhe,skhe->shqk", d_context, value_heads, preferred_element_type=jnp.float32
    )
    d_scores = (probs * (d_probs - jnp.sum(d_probs * probs, axis=-1, keepdims=True))).astype(
        jnp.bfloat16
    )
    d_query = (
        jnp.einsum("shqk,skhe->sqhe", d_scores, key_heads, preferred_element_type=jnp.float32)
        * 0.125
    )
    d_key = (
        jnp.einsum("shqk,sqhe->skhe", d_scores, query_heads, preferred_element_type=jnp.float32)
        * 0.125
    )
    d_query_low = d_query.reshape(rows, width).astype(jnp.bfloat16)
    d_key_low = d_key.reshape(rows, width).astype(jnp.bfloat16)
    d_value_low = d_value.reshape(rows, width).astype(jnp.bfloat16)
    d_projected = jnp.concatenate([d_query_low, d_key_low, d_value_low], axis=1)
    g_weight_qkv = transposed_left(inputs, d_projected)
    g_bias_query = jnp.sum(d_query_low.astype(jnp.float32), axis=0)
    g_bias_value = jnp.sum(d_value_low.astype(jnp.float32), axis=0)
    d_inputs = d_sum_one + transposed_right(d_projected, weight_qkv)
    g_vectors = jnp.stack(
        [g_bias_query, g_bias_value, g_bias_attn, d_shift_one, g_bias_out, d_shift_two]
    )
    g_scales = jnp.stack([d_gain_one, d_gain_two])

    def scatter(value, dimension):
        return lax.psum_scatter(value, "batch", scatter_dimension=dimension, tiled=True)

    summed_qkv, summed_attn, summed_in, summed_out = (
        scatter(g_weight_qkv, 0), scatter(g_weight_attn, 0), scatter(g_weight_in, 0), scatter(g_weight_out, 0)
    )
    summed_bias_in, summed_vectors, summed_scales = (
        scatter(g_bias_in, 0), scatter(g_vectors, 1), scatter(g_scales, 1)
    )
    return (
        pooled[None],
        d_inputs.reshape(1, seq_count, seq_len, width),
        summed_qkv[None],
        summed_attn[None],
        summed_in[None],
        summed_out[None],
        summed_bias_in[None],
        summed_vectors[None],
        summed_scales[None],
    )


def solution(mesh):
    n = mesh.shape["batch"]
    direct = n == 16
    in_specs = (
        P("tower", "batch", None, None),
        P("tower", "batch"),
        P("batch"),
        P("batch"),
        P("tower", None, None),
        P("tower", None, None),
        P("tower", None, None),
        P("tower", None, None),
        P("tower", None),
        P("tower", None, None),
        P("tower", None, None),
    )
    out_specs = (
        P("tower", "batch", None),
        P("tower", "batch", None, None),
        P("tower", "batch", None),
        P("tower", "batch", None),
        P("tower", "batch", None),
        P("tower", "batch", None),
        P("tower", "batch"),
        P("tower", None, "batch"),
        P("tower", None, "batch"),
    )
    return jax.shard_map(
        partial(per_device, n) if direct else per_device_plain, mesh=mesh, in_specs=in_specs, out_specs=out_specs, check_vma=False
    )
```

```python
from functools import partial

import jax
import jax.numpy as jnp
from jax import lax
from jax.experimental import pallas as pl
from jax.experimental.pallas import tpu as pltpu
from jax.sharding import PartitionSpec as P

HEADS = 12
EPS = 1e-12
SCALE = 4.0
HIGH = lax.Precision.HIGHEST
MESH = pl.DeviceIdType.MESH
NEG = -1000000000.0
LOW = jnp.bfloat16
F32 = jnp.float32
CHUNKS = 12
MIB = 2**20


def product(left, right):
    return jnp.dot(left, right, preferred_element_type=jnp.float32)


def transposed_left(left, right):
    return lax.dot_general(
        left, right, (((0,), (0,)), ((), ())), preferred_element_type=jnp.float32
    )


def transposed_right(left, right):
    return lax.dot_general(
        left, right, (((1,), (1,)), ((), ())), preferred_element_type=jnp.float32
    )


def norm_forward(total, gain, shift):
    mean = jnp.mean(total, axis=-1, keepdims=True)
    centered = total - mean
    inverse = lax.rsqrt(jnp.mean(centered * centered, axis=-1, keepdims=True) + EPS)
    normed = centered * inverse
    return (normed * gain + shift, normed, inverse)


def norm_backward(grad, normed, inverse, gain):
    scaled = grad * gain
    first_mean = jnp.mean(scaled, axis=-1, keepdims=True)
    second_mean = jnp.mean(scaled * normed, axis=-1, keepdims=True)
    d_total = inverse * (scaled - first_mean - normed * second_mean)
    return (d_total, jnp.sum(grad * normed, axis=0), jnp.sum(grad, axis=0))


def scores_of(query_heads, key_heads, keep):
    raw = (
        jnp.einsum("sqhe,skhe->shqk", query_heads, key_heads, preferred_element_type=jnp.float32)
        * 0.125
    )
    return jnp.where(keep[:, None, None, :], raw, NEG)


def gelu_parts(z):
    t = 1.0 / (1.0 + jnp.abs(z) * (0.3275911 * 0.7071067811865476))
    bell = jnp.exp(z * z * -0.5)
    tail = t * bell * (
        0.127414796 + t * (-0.142248368 + t * (0.7107068705 + t * (-0.7265760135 + t * 0.5307027145)))
    )
    below = jnp.where(z < 0.0, tail, 1.0 - tail)
    return z * below, below + z * bell * 0.3989422804014327


def normed(total):
    mean = jnp.mean(total, axis=-1, keepdims=True)
    centered = total - mean
    inverse = lax.rsqrt(jnp.mean(centered * centered, axis=-1, keepdims=True) + EPS)
    return centered * inverse, inverse


def encoder_kernel(
    lens, x_ref, wqkv_hbm, wattn_hbm, win_hbm, wout_hbm, bin_ref, vec_ref, gain_ref,
    pooled_ref, hidden_ref, slope_ref, n1_ref, n2_ref, inv_ref, low_t_ref, query_ref, key_t_ref, value_ref, probs_ref,
    context_t_ref, x_t_ref,
    wqkv, wattn, win, wout, sems,
):
    step = pl.program_id(0)
    loads = [
        pltpu.make_async_copy(source.at[0], target, sems.at[place])
        for place, (source, target) in enumerate(
            [(wqkv_hbm, wqkv), (wattn_hbm, wattn), (win_hbm, win), (wout_hbm, wout)]
        )
    ]

    @pl.when(step == 0)
    def _():
        for load in loads:
            load.start()
        loads[0].wait()

    length = lens[step]
    x = x_ref[...]
    rows = x.shape[0]
    query = (product(x, wqkv[:, :768]) + vec_ref[0]).astype(LOW) * 0.125
    key = product(x, wqkv[:, 768:1536]).astype(LOW)
    value = (product(x, wqkv[:, 1536:]) + vec_ref[1]).astype(LOW)
    query_ref[...] = query
    value_ref[...] = value
    key_t_ref[...] = key.T
    x_t_ref[...] = x.T
    value_t = value.T
    blocked = jnp.where(lax.broadcasted_iota(jnp.int32, (rows, 1), 0) < length, 0.0, NEG)
    lane = lax.broadcasted_iota(jnp.int32, (rows, 128), 1)

    def scores_of_head(head):
        pair = slice(128 * (head // 2), 128 * (head // 2 + 1))
        mine = (lane < 64) if head % 2 == 0 else (lane >= 64)
        key_one = jnp.where(mine, key[:, pair], jnp.zeros((), LOW))
        return transposed_right(key_one, query[:, pair]) + blocked

    def context_of_head(head, probs):
        context_t_ref[64 * head:64 * (head + 1), :] = product(
            value_t[64 * head:64 * (head + 1)], probs
        ).astype(LOW)

    ahead, behind = [scores_of_head(head) for head in range(4)], []
    for head in range(HEADS):
        if head + 4 < HEADS:
            ahead.append(scores_of_head(head + 4))
        scores = ahead.pop(0)
        weights = jnp.exp(scores - jnp.max(scores, axis=0, keepdims=True))
        probs = (weights * (1.0 / jnp.sum(weights, axis=0, keepdims=True))).astype(LOW)
        probs_ref[:, 256 * head:256 * (head + 1)] = probs
        behind.append((head, probs))
        if len(behind) > 2:
            context_of_head(*behind.pop(0))
    for item in behind:
        context_of_head(*item)

    @pl.when(step == 0)
    def _():
        loads[1].wait()

    attended = transposed_left(context_t_ref[...], wattn[...]) + vec_ref[2]
    n1, inv1 = normed(x.astype(F32) + attended)
    first = n1 * gain_ref[0, 0:1] + vec_ref[3]
    first_low = first.astype(LOW)
    low_t_ref[...] = first_low.T
    n1_ref[...] = n1.astype(LOW)

    @pl.when(step == 0)
    def _():
        loads[2].wait()
        loads[3].wait()

    total = first + vec_ref[4]
    blocks = [slice(768 * part, 768 * (part + 1)) for part in range(4)]
    ahead, late = product(first_low, win[:, blocks[0]]), None
    for part in range(4):
        before = ahead
        if part + 1 < 4:
            ahead = product(first_low, win[:, blocks[part + 1]])
        hidden, slope = gelu_parts(before + bin_ref[:, blocks[part]])
        hidden = hidden.astype(LOW)
        hidden_ref[:, blocks[part]] = hidden
        slope_ref[:, blocks[part]] = slope.astype(LOW)
        if late is not None:
            total = total + product(late, wout[blocks[part - 1], :])
        late = hidden
    total = total + product(late, wout[blocks[3], :])
    n2, inv2 = normed(total)
    n2_ref[...] = n2.astype(LOW)
    inv_ref[...] = jnp.where(lane < 64, inv1, inv2)
    output = n2 * gain_ref[0, 1:2] + vec_ref[5]
    keep = lax.broadcasted_iota(jnp.int32, (rows, 1), 0) < length
    pooled_ref[pl.ds(step, 1)] = jnp.sum(jnp.where(keep, output, 0.0), axis=0, keepdims=True) / length.astype(F32)


def encoder(lens, x, w_qkv, w_attn, w_in, w_out, b_in, vectors, gains):
    seqs = lens.shape[0]
    rows = x.shape[0]
    per = rows // seqs

    def by_rows(width):
        return pl.BlockSpec((per, width), lambda s, *_: (s, 0))

    def by_columns(height):
        return pl.BlockSpec((height, per), lambda s, *_: (0, s))

    def full(*shape):
        return pl.BlockSpec(shape, lambda s, *_: (0,) * len(shape))

    anywhere = pl.BlockSpec(memory_space=pl.ANY)
    def wide(width, kind=LOW):
        return by_rows(width), jax.ShapeDtypeStruct((rows, width), kind)

    tall = by_columns(768), jax.ShapeDtypeStruct((768, rows), LOW)
    kept = [
        wide(3072), wide(3072), wide(768), wide(768), wide(128, F32), tall,
        wide(768), tall, wide(768), wide(3072), tall, tall,
    ]
    return pl.pallas_call(
        encoder_kernel,
        grid_spec=pltpu.PrefetchScalarGridSpec(
            num_scalar_prefetch=1,
            grid=(seqs,),
            in_specs=[by_rows(768)] + [anywhere] * 4 + [full(1, 3072), full(6, 1, 768), full(1, 2, 768)],
            out_specs=[full(seqs, 768)] + [spec for spec, _ in kept],
            scratch_shapes=[
                pltpu.VMEM((768, 2304), LOW), pltpu.VMEM((768, 768), LOW),
                pltpu.VMEM((768, 3072), LOW), pltpu.VMEM((3072, 768), LOW),
                pltpu.SemaphoreType.DMA((4,)),
            ],
        ),
        out_shape=[jax.ShapeDtypeStruct((seqs, 768), F32)] + [shape for _, shape in kept],
        compiler_params=pltpu.CompilerParams(vmem_limit_bytes=56 * MIB),
        name="encoder",
    )(lens, x, w_qkv, w_attn, w_in, w_out, b_in, vectors, gains)


def second_norm_backward(grad_row, length, first_row, n2, inv2, gain):
    scaled = grad_row * gain
    mean = jnp.mean(scaled, axis=1, keepdims=True)
    along = jnp.mean(scaled * n2, axis=1, keepdims=True)
    keep = first_row + lax.broadcasted_iota(jnp.int32, (n2.shape[0], 1), 0) < length
    return jnp.where(keep, inv2 * (scaled - mean - n2 * along), 0.0), keep


def select(condition):
    return jnp.where(condition, 1.0, 0.0)


def aligned(start, size, multiple):
    return pl.ds(pl.multiple_of(start, multiple), size)


class Sums:
    def __init__(self, n, scratch):
        (self.grads, self.paired, self.crossed, self.rows_got, self.got, self.pair_send, self.pair_recv,
         self.cross_send, self.cross_recv, self.z_send, self.z_recv) = scratch
        self.tower, self.me = lax.axis_index("tower"), lax.axis_index("batch")
        self.depth = n // 4
        self.z, self.y, self.core = self.me // 4, lax.rem(self.me // 2, 2), lax.rem(self.me, 2)

    def z_at(self, offset):
        return lax.rem(self.z + offset, self.depth)

    def device(self, z, y, core):
        return (self.tower, z * 4 + y * 2 + core)

    def pair_copy(self, chunk):
        return pltpu.make_async_remote_copy(
            src_ref=self.grads.at[chunk, :, 1 - self.core], dst_ref=self.paired.at[chunk],
            send_sem=self.pair_send.at[chunk], recv_sem=self.pair_recv.at[chunk],
            device_id=self.device(self.z, self.y, 1 - self.core), device_id_type=MESH,
        )

    def cross_copy(self, chunk):
        return pltpu.make_async_remote_copy(
            src_ref=self.grads.at[chunk, 1 - self.y, self.core], dst_ref=self.crossed.at[chunk],
            send_sem=self.cross_send.at[chunk], recv_sem=self.cross_recv.at[chunk],
            device_id=self.device(self.z, 1 - self.y, self.core), device_id_type=MESH,
        )

    def rows_copy(self, chunk):
        return pltpu.make_async_remote_copy(
            src_ref=self.grads.at[chunk, self.y, self.core], dst_ref=self.rows_got.at[chunk],
            send_sem=self.z_send.at[chunk, 0], recv_sem=self.z_recv.at[chunk, 0],
            device_id=self.device(self.z_at(chunk + 1), self.y, self.core), device_id_type=MESH,
        )

    def z_copy(self, chunk, offset):
        return pltpu.make_async_remote_copy(
            src_ref=self.grads.at[chunk, self.y, self.core, self.z_at(offset)],
            dst_ref=self.got.at[chunk - 4, offset - 1],
            send_sem=self.z_send.at[chunk, offset - 1], recv_sem=self.z_recv.at[chunk, offset - 1],
            device_id=self.device(self.z_at(offset), self.y, self.core), device_id_type=MESH,
        )

    def pair(self, chunk):
        self.pair_copy(chunk).start()

    def cross(self, chunk):
        self.pair_copy(chunk).wait_recv()
        place = (chunk, 1 - self.y, self.core)
        self.grads[place] = (self.grads[place].astype(F32) + self.paired[chunk, 1 - self.y].astype(F32)).astype(LOW)
        self.cross_copy(chunk).start()

    def spread(self, chunk, by_rows=False, last=False):
        self.cross_copy(chunk).wait_recv()
        place = (chunk, self.y, self.core)
        self.grads[place] = (
            self.grads[place].astype(F32) + self.paired[chunk, self.y].astype(F32) + self.crossed[chunk].astype(F32)
        ).astype(LOW)
        if by_rows:
            if not last:
                self.rows_copy(chunk).start()
        else:
            for offset in range(1, self.depth):
                self.z_copy(chunk, offset).start()

    def rows_total(self, part):
        total = self.grads[3, self.y, self.core, part].astype(F32)
        for chunk in range(3):
            total = total + self.rows_got[chunk, part].astype(F32)
        return total

    def total(self, chunk):
        total = self.grads[chunk, self.y, self.core, self.z].astype(F32)
        for offset in range(1, self.depth):
            self.z_copy(chunk, offset).wait_recv()
            total = total + self.got[chunk - 4, offset - 1].astype(F32)
        return total

    def close(self):
        @pl.loop(0, CHUNKS)
        def _(chunk):
            self.pair_copy(chunk).wait_send()
            self.cross_copy(chunk).wait_send()

        for chunk in range(3):
            self.rows_copy(chunk).wait_send()

        @pl.loop(4, CHUNKS)
        def _(chunk):
            for offset in range(1, self.depth):
                self.z_copy(chunk, offset).wait_send()


def d_pooled_of(n, tower, me, everyone):
    seqs = 4 * n
    packed = everyone[...]
    questions, passages = (
        jnp.concatenate([packed[core, side].reshape(8 * n, 256) for core in range(2)], axis=0) for side in range(2)
    )
    rows = lax.broadcasted_iota(jnp.int32, (seqs, 16 * n), 0)
    places = lax.broadcasted_iota(jnp.int32, (seqs, 16 * n), 1)
    owner, lane = lax.rem(rows // 4, 2) * (n // 2) + rows // 8, lax.rem(rows, 4)

    def picked(values, row):
        return product(select(places == owner * 16 + row).astype(LOW), values)

    def whole(values):
        parts = [product(select(places == owner * 16 + 4 * part + lane).astype(LOW), values) for part in range(3)]
        return jnp.concatenate(parts, axis=1)

    column_lane = lax.broadcasted_iota(jnp.int32, (seqs, 256), 1)
    column_want = lax.rem(lax.broadcasted_iota(jnp.int32, (seqs, 256), 0), 4)

    def column(row):
        return jnp.sum(
            jnp.where(column_lane == column_want, picked(passages, row), 0.0), axis=1, keepdims=True
        )

    question_float, passage_float = whole(questions), whole(passages)
    positives, sets = column(12), column(13)
    first = lax.broadcasted_iota(jnp.int32, (seqs, seqs), 0)
    second = lax.broadcasted_iota(jnp.int32, (seqs, seqs), 1)
    set_row = jnp.sum(jnp.where(first == second, sets, 0.0), axis=0, keepdims=True)
    chosen = second.astype(F32) == positives
    query_set = jnp.sum(jnp.where(chosen, set_row, 0.0), axis=1, keepdims=True)
    logits = transposed_right(question_float.astype(LOW), passage_float.astype(LOW)) * SCALE
    masked = jnp.where(set_row == query_set, logits, NEG)
    weights = jnp.exp(masked - jnp.max(masked, axis=1, keepdims=True))
    softmax = weights / jnp.sum(weights, axis=1, keepdims=True)
    d_logits = (softmax - select(chosen)) * SCALE
    mine_row = lax.broadcasted_iota(jnp.int32, (8, seqs), 0)
    mine_column = lax.broadcasted_iota(jnp.int32, (8, seqs), 1)
    own = select((mine_column == me * 4 + mine_row) & (mine_row < 4))
    by_question = jnp.dot(own, d_logits, precision=HIGH, preferred_element_type=F32)
    by_passage = lax.dot_general(
        own, d_logits, (((1,), (1,)), ((), ())), precision=HIGH, preferred_element_type=F32
    )
    is_passage = tower == 1
    terms = jnp.where(is_passage, by_passage, by_question)
    others = jnp.where(is_passage, question_float, passage_float)
    grad = jnp.dot(terms, others, precision=HIGH, preferred_element_type=F32)
    return jnp.where(is_passage, grad, grad.astype(LOW).astype(F32))


def backward_kernel(
    n, lens, positives, datasets, pooled_ref, gain_ref, wqkv_hbm, wattn_hbm, win_hbm, wout_hbm,
    hidden_hbm, slope_hbm, n1_hbm, n2_hbm, inv_hbm, low_t_hbm, query_hbm, key_t_hbm, value_hbm, probs_hbm,
    context_t_hbm, x_t_hbm,
    out_ref, in_ref, attn_ref, qkv_ref, summed_small_ref, tokens_out,
    grads, paired, crossed, rows_got, got, pair_send, pair_recv, cross_send, cross_recv, z_send, z_recv,
    first_weights, second_weights, wide, tall, rows_a, rows_b, rows_c, key_t, context_t, inv, stage,
    rows_small, bias_in, small, small_got, mine, everyone, d_pooled,
    sems, stage_sems, small_send, small_recv, pool_send, pool_recv,
):
    tower, me = lax.axis_index("tower"), lax.axis_index("batch")
    chips = n // 2
    chip, core = me // 2, lax.rem(me, 2)
    sums = Sums(
        n, (grads, paired, crossed, rows_got, got, pair_send, pair_recv, cross_send, cross_recv, z_send, z_recv)
    )
    barrier = pltpu.get_barrier_semaphore()

    @pl.loop(1, n)
    def _(step):
        pl.semaphore_signal(
            barrier, inc=1, device_id=(tower, lax.rem(me + step, n)), device_id_type=MESH
        )

    @pl.loop(0, chips)
    def _(other):
        pl.semaphore_signal(
            barrier, inc=1, device_id=(1 - tower, 2 * other + core), device_id_type=MESH
        )

    def load(place, source, target):
        return pltpu.make_async_copy(source, target, sems.at[place])

    def seq_rows(seq):
        return aligned(seq * 256, 256, 256)

    def block(part):
        return slice(768 * part, 768 * (part + 1))

    n2_load, inv_load = load(0, n2_hbm, rows_a), load(1, inv_hbm, inv)
    hidden_loads = [
        load(2 + part, hidden_hbm.at[:, aligned(sums.z_at(part + 1) * 768, 768, 128)], wide.at[:, block(part)])
        for part in range(4)
    ]
    slope_loads = [load(10 + part, slope_hbm.at[:, block(part)], wide.at[:, block(part)]) for part in range(4)]
    out_load = load(14, wout_hbm.at[0], first_weights)
    in_loads = [load(15 + part, win_hbm.at[0, :, block(part)], second_weights.at[block(part)]) for part in range(4)]
    n1_load, low_load = load(19, n1_hbm, rows_b), load(20, low_t_hbm, tall)
    key_load, context_load = load(21, key_t_hbm, key_t), load(22, context_t_hbm, context_t)
    attn_load = load(23, wattn_hbm.at[0], first_weights.at[block(0)])
    qkv_loads = [
        load(24 + part, wqkv_hbm.at[0, :, block(part)], first_weights.at[block(part + 1)]) for part in range(3)
    ]
    query_load, value_load, x_load = load(27, query_hbm, rows_a), load(28, value_hbm, rows_b), load(29, x_t_hbm, tall)

    def probs_load(seq):
        return load(30 + seq, probs_hbm.at[seq_rows(seq)], wide.at[seq_rows(seq)])

    for copy in [n2_load, inv_load] + hidden_loads + [out_load] + in_loads + [n1_load, low_load, key_load, context_load]:
        copy.start()

    row = lax.broadcasted_iota(jnp.int32, (4, 256), 0)
    lane = lax.broadcasted_iota(jnp.int32, (4, 256), 1)
    extra = jnp.zeros((4, 256), F32)
    for seq in range(4):
        for place, numbers in enumerate((positives, datasets)):
            extra = jnp.where((row == place) & (lane == seq), numbers[seq].astype(F32), extra)
    pooled = pooled_ref[...]
    pooled_block = jnp.concatenate(
        [pooled[:, 0:256], pooled[:, 256:512], pooled[:, 512:768], extra], axis=0
    ).astype(LOW)
    mine[...] = pooled_block

    @pl.when(tower == 0)
    def _():
        everyone[core, 0] = jnp.zeros((chips, 16, 256), LOW)

    everyone[core, tower, chip] = pooled_block
    rows_small[...] = jnp.zeros_like(rows_small)
    bias_in[...] = jnp.zeros_like(bias_in)
    pl.semaphore_wait(barrier, n - 1 + chips)

    def pool_copy(side, step, slot):
        return pltpu.make_async_remote_copy(
            src_ref=mine, dst_ref=everyone.at[core, tower, chip],
            send_sem=pool_send.at[slot], recv_sem=pool_recv.at[slot],
            device_id=(side, 2 * lax.rem(chip + step, chips) + core), device_id_type=MESH,
        )

    pool_forward = pltpu.make_async_remote_copy(
        src_ref=everyone.at[core], dst_ref=everyone.at[core],
        send_sem=pool_send.at[n], recv_sem=pool_recv.at[n],
        device_id=(tower, me + 1 - 2 * core), device_id_type=MESH,
    )

    @pl.loop(0, chips)
    def _(step):
        pool_copy(1 - tower, step, chips + step).start()

    @pl.when(tower == 1)
    def _():
        @pl.loop(1, chips)
        def _(step):
            pool_copy(1, step, step).start()

        @pl.loop(1, chips)
        def _(step):
            pool_copy(1, step, step).wait_recv()

    @pl.loop(0, chips)
    def _(step):
        pool_copy(1 - tower, step, chips + step).wait_recv()

    pool_forward.start()
    pool_forward.wait_recv()
    d_pooled[...] = d_pooled_of(n, tower, me, everyone)

    n2_load.wait()
    inv_load.wait()

    def second_backward(seq):
        length = lens[seq]
        grad_row = d_pooled[pl.ds(seq, 1)] / length.astype(F32)
        normal = rows_a[seq_rows(seq)].astype(F32)
        d_second, keep = second_norm_backward(
            grad_row, length, 0, normal, inv[seq_rows(seq), 64:65], gain_ref[0, 1:2]
        )
        return d_second, keep, normal, grad_row

    @pl.loop(0, 4)
    def _(seq):
        d_second, keep, normal, grad_row = second_backward(seq)
        low = d_second.astype(LOW)
        rows_c[seq_rows(seq)] = low
        rows_small[4:5] += jnp.sum(low.astype(F32), axis=0, keepdims=True)
        rows_small[5:6] += d_pooled[pl.ds(seq, 1)]
        rows_small[7:8] += grad_row * jnp.sum(jnp.where(keep, normal, 0.0), axis=0, keepdims=True)

    for part in range(4):
        hidden_loads[part].wait()
        for y in range(2):
            columns = slice(768 * part + 384 * y, 768 * part + 384 * (y + 1))
            grads[part, y] = transposed_left(wide[:, columns], rows_c[...]).astype(LOW).reshape(2, 4, 48, 768)
        slope_loads[part].start()
        sums.pair(part)
        if part in (1, 2):
            sums.cross(part - 1)

    @pl.loop(0, chips)
    def _(step):
        pool_copy(1 - tower, step, chips + step).wait_send()

    @pl.when(tower == 1)
    def _():
        @pl.loop(1, chips)
        def _(step):
            pool_copy(1, step, step).wait_send()

    pool_forward.wait_send()

    for copy in [out_load] + in_loads + [n1_load] + slope_loads:
        copy.wait()

    def stage_copy(seq, kind):
        slot, rows = stage.at[lax.rem(seq, 2)], tokens_out.at[seq_rows(seq)]
        source, target = (rows, slot) if kind == 1 else (slot, rows)
        return pltpu.make_async_copy(source, target, stage_sems.at[kind, seq])

    @pl.loop(0, 4)
    def _(seq):
        @pl.when(seq >= 1)
        def _():
            sums.spread(lax.max(seq - 1, 0), by_rows=True)

        @pl.when((seq >= 1) & (seq <= 2))
        def _():
            sums.cross(lax.min(seq + 1, 3))

        rows = seq_rows(seq)
        d_second = second_backward(seq)[0]
        d_branch = rows_c[rows]
        d_first = d_second
        ahead, late = transposed_right(d_branch, first_weights[block(0), :]), None
        for part in range(4):
            d_hidden = ahead
            if part < 3:
                ahead = transposed_right(d_branch, first_weights[block(part + 1), :])
            d_pre = (d_hidden * wide[rows, block(part)].astype(F32)).astype(LOW)
            wide[rows, block(part)] = d_pre
            bias_in[:, block(part)] += jnp.sum(d_pre.astype(F32), axis=0, keepdims=True)
            if late is not None:
                d_first = d_first + transposed_right(late, second_weights[block(part - 1), :])
            late = d_pre
        d_first = d_first + transposed_right(late, second_weights[block(3), :])
        normal = rows_b[rows].astype(F32)
        scaled = d_first * gain_ref[0, 0:1]
        mean = jnp.mean(scaled, axis=1, keepdims=True)
        along = jnp.mean(scaled * normal, axis=1, keepdims=True)
        d_sum_one = inv[rows, 0:1] * (scaled - mean - normal * along)

        @pl.when(seq >= 2)
        def _():
            stage_copy(lax.max(seq - 2, 0), 0).wait()

        stage[lax.rem(seq, 2)] = d_sum_one
        stage_copy(seq, 0).start()
        d_attended = d_sum_one.astype(LOW)
        rows_c[rows] = d_attended
        rows_small[2:3] += jnp.sum(d_attended.astype(F32), axis=0, keepdims=True)
        rows_small[3:4] += jnp.sum(d_first, axis=0, keepdims=True)
        rows_small[6:7] += jnp.sum(d_first * normal, axis=0, keepdims=True)

    for copy in [attn_load] + qkv_loads + [query_load, value_load]:
        copy.start()
    low_load.wait()

    def store(chunk, rows_ref, columns):
        for half in range(2):
            grad = product(rows_ref[384 * half:384 * (half + 1)], columns).astype(LOW)
            for z in range(2):
                grads[chunk, :, :, 2 * half + z] = grad[192 * z:192 * (z + 1)].reshape(2, 2, 48, 768)
        sums.pair(chunk)

    for part in range(4):
        store(4 + part, tall, wide[:, block(part)])
        if part == 1:
            sums.spread(3, by_rows=True, last=True)
        if part in (1, 2):
            sums.cross(3 + part)
    for seq in range(4):
        probs_load(seq).start()
    x_load.start()

    context_load.wait()
    store(8, context_t, rows_c[...])
    for copy in [attn_load] + qkv_loads + [query_load, value_load, key_load]:
        copy.wait()
    lane = lax.broadcasted_iota(jnp.int32, (256, 128), 1)
    none = jnp.zeros((), LOW)

    @pl.loop(0, 4)
    def _(seq):
        rows = seq_rows(seq)

        @pl.when(seq >= 1)
        def _():
            sums.spread(3 + lax.max(seq, 1))
            sums.cross(5 + lax.max(seq, 1))

        probs_load(seq).wait()
        d_attended = rows_c[rows]
        weight = first_weights[block(0), :]
        d_context = transposed_right(d_attended, weight).astype(LOW)
        d_context_t = transposed_right(weight, d_attended).astype(LOW)

        def d_probs_of(pair):
            lanes = slice(128 * pair, 128 * (pair + 1))
            value_pair = rows_b[rows, lanes]
            return [
                product(jnp.where(mask, value_pair, none), d_context_t[lanes]) for mask in (lane < 64, lane >= 64)
            ]

        ahead, late = d_probs_of(0), None

        def d_projected_of(pair, probs, d_scores):
            lanes = slice(128 * pair, 128 * (pair + 1))
            key_pair, query_pair, d_context_pair = key_t[lanes, rows], rows_a[rows, lanes], d_context[:, lanes]
            d_values = [product(prob, d_context_pair) for prob in probs]
            d_keys = [product(d_score, query_pair) for d_score in d_scores]
            d_queries = [product(key_pair[64 * one:64 * (one + 1)], d_scores[one]) for one in range(2)]
            d_query = (jnp.concatenate(d_queries, axis=0).T * 0.125).astype(LOW)
            d_key = jnp.where(lane < 64, d_keys[0], d_keys[1]).astype(LOW)
            d_value = jnp.where(lane < 64, d_values[0], d_values[1]).astype(LOW)
            for part, value in enumerate((d_query, d_key, d_value)):
                second_weights[aligned(1024 * part + seq * 256, 256, 256), lanes] = value
            rows_small[0:1, lanes] += jnp.sum(d_query.astype(F32), axis=0, keepdims=True)
            rows_small[1:2, lanes] += jnp.sum(d_value.astype(F32), axis=0, keepdims=True)

        for pair in range(6):
            d_probs = ahead
            if pair < 5:
                ahead = d_probs_of(pair + 1)
            lanes = slice(128 * pair, 128 * (pair + 1))
            weighed = d_context_t[lanes].astype(F32) * context_t[lanes, rows].astype(F32)
            probs, d_scores = [], []
            for one in range(2):
                head = 2 * pair + one
                row_sum = jnp.sum(weighed[64 * one:64 * (one + 1)], axis=0, keepdims=True)
                prob = wide[rows, 256 * head:256 * (head + 1)]
                probs.append(prob)
                d_scores.append((prob.astype(F32) * (d_probs[one] - row_sum)).astype(LOW))
            if late is not None:
                d_projected_of(*late)
            late = pair, probs, d_scores
        d_projected_of(*late)

    for seq in (2, 3):
        stage_copy(seq, 0).wait()
    for seq in (0, 1):
        stage_copy(seq, 1).start()
    x_load.wait()
    sums.spread(7)
    for part in range(3):
        store(9 + part, tall, second_weights[1024 * part:1024 * (part + 1), :])
        if part == 1:
            sums.cross(9)

    bundle, bias_row = rows_small[...], bias_in[...]
    small[...] = jnp.zeros_like(small)
    for device in range(n):
        small[device, 0:8, 0:48] = bundle[:, 48 * device:48 * (device + 1)]
        for part in range(4):
            start = 192 * device + 48 * part
            small[device, 8 + part:9 + part, 0:48] = bias_row[:, start:start + 48]

    def small_copy(step):
        other = lax.rem(me + step, n)
        return pltpu.make_async_remote_copy(
            src_ref=small.at[other], dst_ref=small_got.at[step],
            send_sem=small_send.at[step], recv_sem=small_recv.at[step],
            device_id=(tower, other), device_id_type=MESH,
        )

    sums.spread(8)
    sums.cross(10)

    @pl.loop(1, n)
    def _(step):
        small_copy(step).start()

    def tokens(seq):
        stage_copy(seq, 1).wait()
        slot = seq % 2
        total = stage[slot]
        for part in range(3):
            total = total + transposed_right(
                second_weights[1024 * part + seq * 256:1024 * part + seq * 256 + 256, :],
                first_weights[block(part + 1), :],
            )
        stage[slot] = total
        stage_copy(seq, 2).start()

    tokens(0)
    tokens(1)
    sums.spread(9)
    sums.cross(11)
    for seq in (2, 3):
        stage_copy(seq - 2, 2).wait()
        stage_copy(seq, 1).start()
    tokens(2)
    tokens(3)
    summed_small_ref[...] = small[me]

    @pl.loop(1, n)
    def _(step):
        small_copy(step).wait()
        summed_small_ref[...] += small_got[step]

    for chunk in range(3):
        sums.rows_copy(chunk).wait_recv()
    for part in range(4):
        out_ref[48 * part:48 * (part + 1)] = sums.rows_total(part)
    for chunk in range(4, 8):
        in_ref[:, block(chunk - 4)] = sums.total(chunk)
    sums.spread(10)
    attn_ref[...] = sums.total(8)
    qkv_ref[:, block(0)] = sums.total(9)
    sums.spread(11)
    qkv_ref[:, block(1)] = sums.total(10)
    qkv_ref[:, block(2)] = sums.total(11)
    for seq in (2, 3):
        stage_copy(seq, 2).wait()
    sums.close()


def backward(lens, positives, datasets, pooled, gains, weights, activations, n):
    rows = activations[0].shape[0]
    anywhere = pl.BlockSpec(memory_space=pl.ANY)
    vmem = pl.BlockSpec(memory_space=pltpu.VMEM)
    scalars = pl.BlockSpec(memory_space=pltpu.SMEM)
    tile = (48, 768)
    dma = pltpu.SemaphoreType.DMA
    return pl.pallas_call(
        partial(backward_kernel, n),
        in_specs=[scalars] * 3 + [vmem] * 2 + [anywhere] * (4 + len(activations)),
        out_specs=[vmem] * 5 + [anywhere],
        out_shape=[
            jax.ShapeDtypeStruct(shape, F32)
            for shape in ((192, 768), (48, 3072), (48, 768), (48, 2304), (16, 128), (rows, 768))
        ],
        scratch_shapes=[
            pltpu.VMEM((CHUNKS, 2, 2, 4) + tile, LOW), pltpu.VMEM((CHUNKS, 2, 4) + tile, LOW),
            pltpu.VMEM((CHUNKS, 4) + tile, LOW), pltpu.VMEM((3, 4) + tile, LOW), pltpu.VMEM((CHUNKS - 4, 3) + tile, LOW),
            dma((CHUNKS,)), dma((CHUNKS,)), dma((CHUNKS,)), dma((CHUNKS,)), dma((CHUNKS, 3)), dma((CHUNKS, 3)),
            pltpu.VMEM((3072, 768), LOW), pltpu.VMEM((3072, 768), LOW), pltpu.VMEM((rows, 3072), LOW),
            pltpu.VMEM((768, rows), LOW), pltpu.VMEM((rows, 768), LOW), pltpu.VMEM((rows, 768), LOW),
            pltpu.VMEM((rows, 768), LOW), pltpu.VMEM((768, rows), LOW), pltpu.VMEM((768, rows), LOW),
            pltpu.VMEM((rows, 128), F32), pltpu.VMEM((2, 256, 768), F32),
            pltpu.VMEM((8, 768), F32), pltpu.VMEM((1, 3072), F32),
            pltpu.VMEM((n, 16, 128), F32), pltpu.VMEM((n, 16, 128), F32),
            pltpu.VMEM((16, 256), LOW), pltpu.VMEM((2, 2, n // 2, 16, 256), LOW), pltpu.VMEM((8, 768), F32),
            dma((34,)), dma((3, 4)), dma((n,)), dma((n,)), dma((2 * n,)), dma((2 * n,)),
        ],
        compiler_params=pltpu.CompilerParams(collective_id=1, has_side_effects=True, vmem_limit_bytes=60 * MIB),
        name="backward",
    )(lens, positives, datasets, pooled, gains, *weights, *activations)


def deliver_kernel(
    out_hbm, in_hbm, attn_hbm, qkv_hbm, small_hbm, tokens_hbm,
    out_to, in_to, attn_to, qkv_to, bias_in_to, vectors_to, gains_to, tokens_to,
    out_held, in_held, attn_held, qkv_held, small_held, held, sems,
):
    parts, rows = held.shape[0], held.shape[1]
    ways = [
        (tokens_hbm.at[pl.ds(rows * part, rows)], held.at[part], tokens_to.at[pl.ds(rows * part, rows)])
        for part in range(parts)
    ] + [
        (out_hbm, out_held, out_to), (in_hbm, in_held, in_to), (attn_hbm, attn_held, attn_to),
        (qkv_hbm, qkv_held, qkv_to),
    ]
    fetches = [
        pltpu.make_async_copy(source, middle, sems.at[0, place]) for place, (source, middle, _) in enumerate(ways)
    ]
    sends = [
        pltpu.make_async_copy(middle, target, sems.at[1, place]) for place, (_, middle, target) in enumerate(ways)
    ]
    small_fetch = pltpu.make_async_copy(small_hbm, small_held, sems.at[0, len(ways)])
    small_fetch.start()
    for fetch in fetches:
        fetch.start()
    for fetch, send in zip(fetches, sends):
        fetch.wait()
        send.start()
    small_fetch.wait()
    small = small_held[...]
    for row in range(6):
        vectors_to[row] = small[row:row + 1, :48]
    gains_to[...] = small[6:8, :48]
    bias_in_to[...] = jnp.concatenate([small[8 + part:9 + part, :48] for part in range(4)], axis=1)
    for send in sends:
        send.wait()


def deliver(*arrays):
    *sums, small, tokens = arrays
    anywhere = pl.BlockSpec(memory_space=pl.ANY)
    vmem = pl.BlockSpec(memory_space=pltpu.VMEM)
    shapes = [array.shape for array in sums] + [(1, 192), (6, 1, 48), (2, 48), tokens.shape]
    rows, width = tokens.shape
    parts = 4
    return pl.pallas_call(
        deliver_kernel,
        in_specs=[anywhere] * 6,
        out_specs=[anywhere] * 4 + [vmem] * 3 + [anywhere],
        out_shape=[jax.ShapeDtypeStruct(shape, F32) for shape in shapes],
        scratch_shapes=[pltpu.VMEM(array.shape, F32) for array in sums]
        + [pltpu.VMEM(small.shape, F32), pltpu.VMEM((parts, rows // parts, width), F32)]
        + [pltpu.SemaphoreType.DMA((2, parts + 5))],
        compiler_params=pltpu.CompilerParams(vmem_limit_bytes=60 * MIB),
        name="deliver",
    )(*arrays)


def per_device(
    n,
    tokens, lengths, positives, datasets, w_qkv, w_attn_out, w_ffn_in, w_ffn_out, b_ffn_in, biases, gains,
):
    seq_count, seq_len, width = (tokens.shape[1], tokens.shape[2], tokens.shape[3])
    lens = lengths[0]
    inputs = tokens[0].reshape(seq_count * seq_len, width)
    weights = (w_qkv, w_attn_out, w_ffn_in, w_ffn_out)
    pooled, *activations = encoder(lens, inputs, *weights, b_ffn_in, biases.transpose(1, 0, 2), gains)
    *sums, grad_tokens = backward(lens, positives, datasets, pooled, gains, weights, activations, n)
    summed_out, summed_in, summed_attn, summed_qkv, bias_in, vectors, scales, grad_tokens = deliver(*sums, grad_tokens)
    return (
        pooled[None],
        grad_tokens.reshape(1, seq_count, seq_len, width),
        summed_qkv[None],
        summed_attn[None],
        summed_in[None],
        summed_out[None],
        bias_in,
        vectors.transpose(1, 0, 2),
        scales[None],
    )


def from_behind(value, axis, steps):
    count = lax.axis_size(axis)
    leading, last = (max(0, -steps), min(count, count - steps))
    return lax.ppermute(value, axis, [(source, source + steps) for source in range(leading, last)])


def loss_gradient_plain(pooled, positives, datasets):
    seq_count = pooled.shape[0]
    mine = pooled.astype(jnp.bfloat16)
    questions = from_behind(mine, "tower", 1)
    everyone, every_set = (
        lax.all_gather(mine, "batch", axis=0, tiled=True),
        lax.all_gather(datasets.astype(jnp.bfloat16), "batch", axis=0, tiled=True),
    )
    total_seqs = everyone.shape[0]
    columns = lax.broadcasted_iota(jnp.int32, (seq_count, total_seqs), 1)
    chosen = columns == positives[:, None]
    set_row = every_set.astype(jnp.float32)[None, :]
    query_set = jnp.sum(jnp.where(chosen, set_row, 0.0), axis=1, keepdims=True)
    allowed = set_row == query_set
    question_float = questions.astype(jnp.float32)
    everyone_float = everyone.astype(jnp.float32)
    logits = jnp.dot(question_float, everyone_float.T, precision=HIGH) * SCALE
    masked = jnp.where(allowed, logits, NEG)
    softmax_rows = jnp.exp(masked - jax.nn.logsumexp(masked, axis=1, keepdims=True))
    d_logits = (softmax_rows - chosen.astype(jnp.float32)) * SCALE
    d_questions = jnp.dot(d_logits, everyone_float, precision=HIGH).astype(jnp.bfloat16)
    passage_terms = jnp.dot(d_logits.T, question_float, precision=HIGH)
    d_passages = lax.psum_scatter(passage_terms, "batch", scatter_dimension=0, tiled=True)
    returned = from_behind(d_questions, "tower", -1)
    is_passage = lax.axis_index("tower") == 1
    return jnp.where(is_passage, d_passages, returned.astype(jnp.float32))


def per_device_plain(

    tokens, lengths, positives, datasets, w_qkv, w_attn_out, w_ffn_in, w_ffn_out, b_ffn_in, biases, gains,
):
    seq_count, seq_len, width = (tokens.shape[1], tokens.shape[2], tokens.shape[3])
    head_size = width // HEADS
    rows = seq_count * seq_len
    inputs = tokens[0].reshape(rows, width)
    lens = lengths[0]
    weight_qkv = w_qkv[0]
    weight_attn = w_attn_out[0]
    weight_in = w_ffn_in[0]
    weight_out = w_ffn_out[0]
    bias_in = b_ffn_in[0]
    vectors = biases[0]
    scales = gains[0]
    positions = lax.broadcasted_iota(jnp.int32, (seq_count, seq_len), 1)
    keep = positions < lens[:, None]
    keep_float = keep.astype(jnp.float32)
    lens_float = lens.astype(jnp.float32)[:, None]
    shape_heads = (seq_count, seq_len, HEADS, head_size)
    projected = product(inputs, weight_qkv)
    query = (projected[:, :width] + vectors[0]).astype(jnp.bfloat16)
    key_rows = projected[:, width : 2 * width].astype(jnp.bfloat16)
    value = (projected[:, 2 * width :] + vectors[1]).astype(jnp.bfloat16)
    query_heads = query.reshape(shape_heads)
    key_heads = key_rows.reshape(shape_heads)
    value_heads = value.reshape(shape_heads)
    scores = scores_of(query_heads, key_heads, keep)
    log_total = jax.nn.logsumexp(scores, axis=-1, keepdims=True)
    probs_low = jnp.exp(scores - log_total).astype(jnp.bfloat16)
    context = jnp.einsum(
        "shqk,skhe->sqhe", probs_low, value_heads, preferred_element_type=jnp.float32
    )
    context = context.reshape(rows, width).astype(jnp.bfloat16)
    attended = product(context, weight_attn) + vectors[2]
    first_norm, normed_one, inverse_one = norm_forward(
        inputs.astype(jnp.float32) + attended, scales[0], vectors[3]
    )
    first_low = first_norm.astype(jnp.bfloat16)
    hidden_pre = product(first_low, weight_in) + bias_in
    hidden = jax.nn.gelu(hidden_pre, approximate=False).astype(jnp.bfloat16)
    branch = product(hidden, weight_out) + vectors[4]
    output, normed_two, inverse_two = norm_forward(first_norm + branch, scales[1], vectors[5])
    pooled = (
        jnp.sum(output.reshape(seq_count, seq_len, width) * keep_float[:, :, None], axis=1)
        / lens_float
    )
    d_pooled = loss_gradient_plain(pooled, positives, datasets)
    d_output = ((d_pooled / lens_float)[:, None, :] * keep_float[:, :, None]).reshape(rows, width)
    d_second, d_gain_two, d_shift_two = norm_backward(d_output, normed_two, inverse_two, scales[1])
    d_branch = d_second.astype(jnp.bfloat16)
    g_weight_out = transposed_left(hidden, d_branch)
    g_bias_out = jnp.sum(d_branch.astype(jnp.float32), axis=0)
    d_hidden = transposed_right(d_branch, weight_out)
    gelu_pull = jax.vjp(partial(jax.nn.gelu, approximate=False), hidden_pre)[1]
    d_pre = gelu_pull(d_hidden)[0].astype(jnp.bfloat16)
    g_weight_in = transposed_left(first_low, d_pre)
    g_bias_in = jnp.sum(d_pre.astype(jnp.float32), axis=0)
    d_first = d_second + transposed_right(d_pre, weight_in)
    d_sum_one, d_gain_one, d_shift_one = norm_backward(d_first, normed_one, inverse_one, scales[0])
    d_attended = d_sum_one.astype(jnp.bfloat16)
    g_weight_attn = transposed_left(context, d_attended)
    g_bias_attn = jnp.sum(d_attended.astype(jnp.float32), axis=0)
    d_context = transposed_right(d_attended, weight_attn).astype(jnp.bfloat16).reshape(shape_heads)
    again = scores_of(query_heads, key_heads, keep)
    probs = jnp.exp(again - log_total)
    d_value = jnp.einsum(
        "shqk,sqhe->skhe", probs.astype(jnp.bfloat16), d_context, preferred_element_type=jnp.float32
    )
    d_probs = jnp.einsum(
        "sqhe,skhe->shqk", d_context, value_heads, preferred_element_type=jnp.float32
    )
    d_scores = (probs * (d_probs - jnp.sum(d_probs * probs, axis=-1, keepdims=True))).astype(
        jnp.bfloat16
    )
    d_query = (
        jnp.einsum("shqk,skhe->sqhe", d_scores, key_heads, preferred_element_type=jnp.float32)
        * 0.125
    )
    d_key = (
        jnp.einsum("shqk,sqhe->skhe", d_scores, query_heads, preferred_element_type=jnp.float32)
        * 0.125
    )
    d_query_low = d_query.reshape(rows, width).astype(jnp.bfloat16)
    d_key_low = d_key.reshape(rows, width).astype(jnp.bfloat16)
    d_value_low = d_value.reshape(rows, width).astype(jnp.bfloat16)
    d_projected = jnp.concatenate([d_query_low, d_key_low, d_value_low], axis=1)
    g_weight_qkv = transposed_left(inputs, d_projected)
    g_bias_query = jnp.sum(d_query_low.astype(jnp.float32), axis=0)
    g_bias_value = jnp.sum(d_value_low.astype(jnp.float32), axis=0)
    d_inputs = d_sum_one + transposed_right(d_projected, weight_qkv)
    g_vectors = jnp.stack(
        [g_bias_query, g_bias_value, g_bias_attn, d_shift_one, g_bias_out, d_shift_two]
    )
    g_scales = jnp.stack([d_gain_one, d_gain_two])

    def scatter(value, dimension):
        return lax.psum_scatter(value, "batch", scatter_dimension=dimension, tiled=True)

    summed_qkv, summed_attn, summed_in, summed_out = (
        scatter(g_weight_qkv, 0), scatter(g_weight_attn, 0), scatter(g_weight_in, 0), scatter(g_weight_out, 0)
    )
    summed_bias_in, summed_vectors, summed_scales = (
        scatter(g_bias_in, 0), scatter(g_vectors, 1), scatter(g_scales, 1)
    )
    return (
        pooled[None],
        d_inputs.reshape(1, seq_count, seq_len, width),
        summed_qkv[None],
        summed_attn[None],
        summed_in[None],
        summed_out[None],
        summed_bias_in[None],
        summed_vectors[None],
        summed_scales[None],
    )


def solution(mesh):
    n = mesh.shape["batch"]
    direct = n == 16
    in_specs = (
        P("tower", "batch", None, None),
        P("tower", "batch"),
        P("batch"),
        P("batch"),
        P("tower", None, None),
        P("tower", None, None),
        P("tower", None, None),
        P("tower", None, None),
        P("tower", None),
        P("tower", None, None),
        P("tower", None, None),
    )
    out_specs = (
        P("tower", "batch", None),
        P("tower", "batch", None, None),
        P("tower", "batch", None),
        P("tower", "batch", None),
        P("tower", "batch", None),
        P("tower", "batch", None),
        P("tower", "batch"),
        P("tower", None, "batch"),
        P("tower", None, "batch"),
    )
    return jax.shard_map(
        partial(per_device, n) if direct else per_device_plain, mesh=mesh, in_specs=in_specs, out_specs=out_specs, check_vma=False
    )
```

```python
from functools import partial

import jax
import jax.numpy as jnp
from jax import lax
from jax.experimental import pallas as pl
from jax.experimental.pallas import tpu as pltpu
from jax.sharding import PartitionSpec as P

HEADS = 12
EPS = 1e-12
SCALE = 4.0
HIGH = lax.Precision.HIGHEST
MESH = pl.DeviceIdType.MESH
NEG = -1000000000.0
LOW = jnp.bfloat16
F32 = jnp.float32
CHUNKS = 12
MIB = 2**20


def product(left, right):
    return jnp.dot(left, right, preferred_element_type=jnp.float32)


def transposed_left(left, right):
    return lax.dot_general(
        left, right, (((0,), (0,)), ((), ())), preferred_element_type=jnp.float32
    )


def transposed_right(left, right):
    return lax.dot_general(
        left, right, (((1,), (1,)), ((), ())), preferred_element_type=jnp.float32
    )


def norm_forward(total, gain, shift):
    mean = jnp.mean(total, axis=-1, keepdims=True)
    centered = total - mean
    inverse = lax.rsqrt(jnp.mean(centered * centered, axis=-1, keepdims=True) + EPS)
    normed = centered * inverse
    return (normed * gain + shift, normed, inverse)


def norm_backward(grad, normed, inverse, gain):
    scaled = grad * gain
    first_mean = jnp.mean(scaled, axis=-1, keepdims=True)
    second_mean = jnp.mean(scaled * normed, axis=-1, keepdims=True)
    d_total = inverse * (scaled - first_mean - normed * second_mean)
    return (d_total, jnp.sum(grad * normed, axis=0), jnp.sum(grad, axis=0))


def scores_of(query_heads, key_heads, keep):
    raw = (
        jnp.einsum("sqhe,skhe->shqk", query_heads, key_heads, preferred_element_type=jnp.float32)
        * 0.125
    )
    return jnp.where(keep[:, None, None, :], raw, NEG)


def gelu_parts(z):
    t = 1.0 / (1.0 + jnp.abs(z) * (0.3275911 * 0.7071067811865476))
    bell = jnp.exp(z * z * -0.5)
    tail = t * bell * (
        0.127414796 + t * (-0.142248368 + t * (0.7107068705 + t * (-0.7265760135 + t * 0.5307027145)))
    )
    below = jnp.where(z < 0.0, tail, 1.0 - tail)
    return z * below, below + z * bell * 0.3989422804014327


def normed(total):
    mean = jnp.mean(total, axis=-1, keepdims=True)
    centered = total - mean
    inverse = lax.rsqrt(jnp.mean(centered * centered, axis=-1, keepdims=True) + EPS)
    return centered * inverse, inverse


def encoder_kernel(
    lens, x_ref, wqkv_hbm, wattn_hbm, win_hbm, wout_hbm, bin_ref, vec_ref, gain_ref,
    pooled_ref, hidden_ref, slope_ref, n1_ref, n2_ref, inv_ref, low_t_ref, query_ref, key_t_ref, value_ref, probs_ref,
    context_t_ref, x_t_ref,
    wqkv, wattn, win, wout, sems,
):
    step = pl.program_id(0)
    loads = [
        pltpu.make_async_copy(source.at[0], target, sems.at[place])
        for place, (source, target) in enumerate(
            [(wqkv_hbm, wqkv), (wattn_hbm, wattn), (win_hbm, win), (wout_hbm, wout)]
        )
    ]

    @pl.when(step == 0)
    def _():
        for load in loads:
            load.start()
        loads[0].wait()

    length = lens[step]
    x = x_ref[...]
    rows = x.shape[0]
    query = (product(x, wqkv[:, :768]) + vec_ref[0]).astype(LOW) * 0.125
    key = product(x, wqkv[:, 768:1536]).astype(LOW)
    value = (product(x, wqkv[:, 1536:]) + vec_ref[1]).astype(LOW)
    query_ref[...] = query
    value_ref[...] = value
    key_t_ref[...] = key.T
    x_t_ref[...] = x.T
    value_t = value.T
    blocked = jnp.where(lax.broadcasted_iota(jnp.int32, (rows, 1), 0) < length, 0.0, NEG)
    lane = lax.broadcasted_iota(jnp.int32, (rows, 128), 1)

    def scores_of_head(head):
        pair = slice(128 * (head // 2), 128 * (head // 2 + 1))
        mine = (lane < 64) if head % 2 == 0 else (lane >= 64)
        key_one = jnp.where(mine, key[:, pair], jnp.zeros((), LOW))
        return transposed_right(key_one, query[:, pair]) + blocked

    def context_of_head(head, probs):
        context_t_ref[64 * head:64 * (head + 1), :] = product(
            value_t[64 * head:64 * (head + 1)], probs
        ).astype(LOW)

    ahead, behind = [scores_of_head(head) for head in range(4)], []
    for head in range(HEADS):
        if head + 4 < HEADS:
            ahead.append(scores_of_head(head + 4))
        scores = ahead.pop(0)
        weights = jnp.exp(scores - jnp.max(scores, axis=0, keepdims=True))
        probs = (weights * (1.0 / jnp.sum(weights, axis=0, keepdims=True))).astype(LOW)
        probs_ref[:, 256 * head:256 * (head + 1)] = probs
        behind.append((head, probs))
        if len(behind) > 2:
            context_of_head(*behind.pop(0))
    for item in behind:
        context_of_head(*item)

    @pl.when(step == 0)
    def _():
        loads[1].wait()

    attended = transposed_left(context_t_ref[...], wattn[...]) + vec_ref[2]
    n1, inv1 = normed(x.astype(F32) + attended)
    first = n1 * gain_ref[0, 0:1] + vec_ref[3]
    first_low = first.astype(LOW)
    low_t_ref[...] = first_low.T
    n1_ref[...] = n1.astype(LOW)

    @pl.when(step == 0)
    def _():
        loads[2].wait()
        loads[3].wait()

    total = first + vec_ref[4]
    blocks = [slice(768 * part, 768 * (part + 1)) for part in range(4)]
    ahead, late = product(first_low, win[:, blocks[0]]), None
    for part in range(4):
        before = ahead
        if part + 1 < 4:
            ahead = product(first_low, win[:, blocks[part + 1]])
        hidden, slope = gelu_parts(before + bin_ref[:, blocks[part]])
        hidden = hidden.astype(LOW)
        hidden_ref[:, blocks[part]] = hidden
        slope_ref[:, blocks[part]] = slope.astype(LOW)
        if late is not None:
            total = total + product(late, wout[blocks[part - 1], :])
        late = hidden
    total = total + product(late, wout[blocks[3], :])
    n2, inv2 = normed(total)
    n2_ref[...] = n2.astype(LOW)
    inv_ref[...] = jnp.where(lane < 64, inv1, inv2)
    output = n2 * gain_ref[0, 1:2] + vec_ref[5]
    keep = lax.broadcasted_iota(jnp.int32, (rows, 1), 0) < length
    pooled_ref[pl.ds(step, 1)] = jnp.sum(jnp.where(keep, output, 0.0), axis=0, keepdims=True) / length.astype(F32)


def encoder(lens, x, w_qkv, w_attn, w_in, w_out, b_in, vectors, gains):
    seqs = lens.shape[0]
    rows = x.shape[0]
    per = rows // seqs

    def by_rows(width):
        return pl.BlockSpec((per, width), lambda s, *_: (s, 0))

    def by_columns(height):
        return pl.BlockSpec((height, per), lambda s, *_: (0, s))

    def full(*shape):
        return pl.BlockSpec(shape, lambda s, *_: (0,) * len(shape))

    anywhere = pl.BlockSpec(memory_space=pl.ANY)
    def wide(width, kind=LOW):
        return by_rows(width), jax.ShapeDtypeStruct((rows, width), kind)

    tall = by_columns(768), jax.ShapeDtypeStruct((768, rows), LOW)
    kept = [
        wide(3072), wide(3072), wide(768), wide(768), wide(128, F32), tall,
        wide(768), tall, wide(768), wide(3072), tall, tall,
    ]
    return pl.pallas_call(
        encoder_kernel,
        grid_spec=pltpu.PrefetchScalarGridSpec(
            num_scalar_prefetch=1,
            grid=(seqs,),
            in_specs=[by_rows(768)] + [anywhere] * 4 + [full(1, 3072), full(6, 1, 768), full(1, 2, 768)],
            out_specs=[full(seqs, 768)] + [spec for spec, _ in kept],
            scratch_shapes=[
                pltpu.VMEM((768, 2304), LOW), pltpu.VMEM((768, 768), LOW),
                pltpu.VMEM((768, 3072), LOW), pltpu.VMEM((3072, 768), LOW),
                pltpu.SemaphoreType.DMA((4,)),
            ],
        ),
        out_shape=[jax.ShapeDtypeStruct((seqs, 768), F32)] + [shape for _, shape in kept],
        compiler_params=pltpu.CompilerParams(vmem_limit_bytes=56 * MIB),
        name="encoder",
    )(lens, x, w_qkv, w_attn, w_in, w_out, b_in, vectors, gains)


def second_norm_backward(grad_row, length, first_row, n2, inv2, gain):
    scaled = grad_row * gain
    mean = jnp.mean(scaled, axis=1, keepdims=True)
    along = jnp.mean(scaled * n2, axis=1, keepdims=True)
    keep = first_row + lax.broadcasted_iota(jnp.int32, (n2.shape[0], 1), 0) < length
    return jnp.where(keep, inv2 * (scaled - mean - n2 * along), 0.0), keep


def select(condition):
    return jnp.where(condition, 1.0, 0.0)


def aligned(start, size, multiple):
    return pl.ds(pl.multiple_of(start, multiple), size)


class Sums:
    def __init__(self, n, scratch):
        (self.grads, self.paired, self.crossed, self.rows_got, self.relayed, self.got, self.z_first, self.pair_send, self.pair_recv,
         self.cross_send, self.cross_recv, self.z_send, self.z_recv) = scratch
        self.tower, self.me = lax.axis_index("tower"), lax.axis_index("batch")
        self.depth = n // 4
        self.z, self.y, self.core = self.me // 4, lax.rem(self.me // 2, 2), lax.rem(self.me, 2)
        self.inner = (self.z == 1) | (self.z == 2)
        self.beside = jnp.where(self.z < 2, 1 - self.z, 5 - self.z)
        self.first = jnp.where(self.z < 2, 1, 0)

    def z_at(self, offset):
        return lax.rem(self.z + offset, self.depth)

    def device(self, z, y, core):
        return (self.tower, z * 4 + y * 2 + core)

    def pair_copy(self, chunk):
        return pltpu.make_async_remote_copy(
            src_ref=self.grads.at[chunk, :, 1 - self.core], dst_ref=self.paired.at[chunk],
            send_sem=self.pair_send.at[chunk], recv_sem=self.pair_recv.at[chunk],
            device_id=self.device(self.z, self.y, 1 - self.core), device_id_type=MESH,
        )

    def cross_copy(self, chunk):
        return pltpu.make_async_remote_copy(
            src_ref=self.grads.at[chunk, 1 - self.y, self.core], dst_ref=self.crossed.at[chunk],
            send_sem=self.cross_send.at[chunk], recv_sem=self.cross_recv.at[chunk],
            device_id=self.device(self.z, 1 - self.y, self.core), device_id_type=MESH,
        )

    def rows_copy(self, chunk):
        return pltpu.make_async_remote_copy(
            src_ref=self.grads.at[chunk, self.y, self.core], dst_ref=self.rows_got.at[chunk],
            send_sem=self.z_send.at[chunk, 0], recv_sem=self.z_recv.at[chunk, 0],
            device_id=self.device(self.z_at(chunk + 1), self.y, self.core), device_id_type=MESH,
        )

    def z_copy(self, chunk, part, target, slot):
        return pltpu.make_async_remote_copy(
            src_ref=self.grads.at[chunk, self.y, self.core, part], dst_ref=self.got.at[chunk - 4, slot],
            send_sem=self.z_send.at[chunk, slot], recv_sem=self.z_recv.at[chunk, slot],
            device_id=self.device(target, self.y, self.core), device_id_type=MESH,
        )

    def relay_copy(self, chunk):
        return pltpu.make_async_remote_copy(
            src_ref=self.grads.at[chunk, self.y, self.core, pl.ds(self.first, 3)], dst_ref=self.relayed.at[chunk - 4],
            send_sem=self.z_send.at[chunk, 2], recv_sem=self.z_recv.at[chunk, 2],
            device_id=self.device(self.beside, self.y, self.core), device_id_type=MESH,
        )

    def near_copy(self, chunk):
        return pltpu.make_async_remote_copy(
            src_ref=self.grads.at[chunk, self.y, self.core, self.beside], dst_ref=self.got.at[chunk - 4, 0],
            send_sem=self.z_send.at[chunk, 2], recv_sem=self.z_recv.at[chunk, 0],
            device_id=self.device(self.beside, self.y, self.core), device_id_type=MESH,
        )

    def mate_copy(self, chunk):
        return self.z_copy(chunk, 3 - self.z, 3 - self.z, 0)

    def far_copy(self, chunk):
        far = 3 - self.beside
        return self.z_copy(chunk, far, far, 1)

    def straight_copy(self, chunk, offset):
        return self.z_copy(chunk, self.z_at(offset), self.z_at(offset), offset - 1)

    def z_first_copy(self, chunk, offset):
        return pltpu.make_async_remote_copy(
            src_ref=self.grads.at[chunk, :, self.core, self.z_at(offset)], dst_ref=self.z_first.at[offset - 1],
            send_sem=self.z_send.at[chunk, offset - 1], recv_sem=self.z_recv.at[chunk, offset - 1],
            device_id=self.device(self.z_at(offset), self.y, self.core), device_id_type=MESH,
        )

    def y_last_copy(self, chunk):
        return pltpu.make_async_remote_copy(
            src_ref=self.grads.at[chunk, 1 - self.y, self.core, self.z], dst_ref=self.crossed.at[chunk, 0],
            send_sem=self.cross_send.at[chunk], recv_sem=self.cross_recv.at[chunk],
            device_id=self.device(self.z, 1 - self.y, self.core), device_id_type=MESH,
        )

    def z_first_spread(self, chunk):
        self.pair_copy(chunk).wait_recv()
        for y in range(2):
            for z in range(self.depth):
                place = (chunk, y, self.core, z)
                self.grads[place] = (self.grads[place].astype(F32) + self.paired[chunk, y, z].astype(F32)).astype(LOW)
        for offset in range(1, self.depth):
            self.z_first_copy(chunk, offset).start()

    def z_first_sum(self, chunk, y):
        total = self.grads[chunk, y, self.core, self.z].astype(F32)
        for slot in range(self.depth - 1):
            total = total + self.z_first[slot, y].astype(F32)
        return total

    def z_first_cross(self, chunk):
        for offset in range(1, self.depth):
            self.z_first_copy(chunk, offset).wait_recv()
        self.grads[chunk, 1 - self.y, self.core, self.z] = self.z_first_sum(chunk, 1 - self.y).astype(LOW)
        self.y_last_copy(chunk).start()

    def z_first_total(self, chunk):
        self.y_last_copy(chunk).wait_recv()
        return self.z_first_sum(chunk, self.y) + self.crossed[chunk, 0].astype(F32)

    def pair(self, chunk):
        self.pair_copy(chunk).start()

    def cross(self, chunk):
        self.pair_copy(chunk).wait_recv()
        for part in range(4):
            place = (chunk, 1 - self.y, self.core, part)
            self.grads[place] = (
                self.grads[place].astype(F32) + self.paired[chunk, 1 - self.y, part].astype(F32)
            ).astype(LOW)
        self.cross_copy(chunk).start()

    def spread(self, chunk, by_rows=False, last=False, straight=False):
        self.cross_copy(chunk).wait_recv()
        for part in range(4):
            place = (chunk, self.y, self.core, part)
            self.grads[place] = (
                self.grads[place].astype(F32) + self.paired[chunk, self.y, part].astype(F32)
                + self.crossed[chunk, part].astype(F32)
            ).astype(LOW)
        if by_rows:
            if not last:
                self.rows_copy(chunk).start()
        elif straight:
            for offset in range(1, self.depth):
                self.straight_copy(chunk, offset).start()
        else:
            @pl.when(self.inner)
            def _():
                self.near_copy(chunk).start()

            @pl.when(jnp.logical_not(self.inner))
            def _():
                self.relay_copy(chunk).start()

    def relay(self, chunk):
        @pl.when(self.inner)
        def _():
            self.relay_copy(chunk).wait_recv()
            for part in range(3):
                place = (chunk, self.y, self.core, self.first + part)
                self.grads[place] = (
                    self.grads[place].astype(F32) + self.relayed[chunk - 4, part].astype(F32)
                ).astype(LOW)
            self.mate_copy(chunk).start()
            self.far_copy(chunk).start()

    def rows_total(self, part):
        total = self.grads[3, self.y, self.core, part].astype(F32)
        for chunk in range(3):
            total = total + self.rows_got[chunk, part].astype(F32)
        return total

    def total(self, chunk):
        self.mate_copy(chunk).wait_recv()

        @pl.when(jnp.logical_not(self.inner))
        def _():
            self.far_copy(chunk).wait_recv()

        total = self.grads[chunk, self.y, self.core, self.z].astype(F32) + self.got[chunk - 4, 0].astype(F32)
        return total + jnp.where(self.inner, 0.0, self.got[chunk - 4, 1].astype(F32))

    def straight_total(self, chunk):
        total = self.grads[chunk, self.y, self.core, self.z].astype(F32)
        for offset in range(1, self.depth):
            self.straight_copy(chunk, offset).wait_recv()
            total = total + self.got[chunk - 4, offset - 1].astype(F32)
        return total

    def close(self):
        for chunk in range(CHUNKS):
            self.pair_copy(chunk).wait_send()
            (self.y_last_copy(chunk) if chunk == 8 else self.cross_copy(chunk)).wait_send()

        for offset in range(1, self.depth):
            self.z_first_copy(8, offset).wait_send()
            for chunk in range(9, CHUNKS):
                self.straight_copy(chunk, offset).wait_send()

        for chunk in range(3):
            self.rows_copy(chunk).wait_send()

        @pl.loop(4, 8)
        def _(chunk):
            @pl.when(self.inner)
            def _():
                self.near_copy(chunk).wait_send()
                self.mate_copy(chunk).wait_send()
                self.far_copy(chunk).wait_send()

            @pl.when(jnp.logical_not(self.inner))
            def _():
                self.relay_copy(chunk).wait_send()


def d_pooled_of(n, tower, me, everyone):
    seqs = 4 * n
    packed = everyone[...]
    questions, passages = (
        jnp.concatenate([packed[core, side].reshape(8 * n, 256) for core in range(2)], axis=0) for side in range(2)
    )
    rows = lax.broadcasted_iota(jnp.int32, (seqs, 16 * n), 0)
    places = lax.broadcasted_iota(jnp.int32, (seqs, 16 * n), 1)
    owner, lane = lax.rem(rows // 4, 2) * (n // 2) + rows // 8, lax.rem(rows, 4)

    def picked(values, row):
        return product(select(places == owner * 16 + row).astype(LOW), values)

    def whole(values):
        parts = [product(select(places == owner * 16 + 4 * part + lane).astype(LOW), values) for part in range(3)]
        return jnp.concatenate(parts, axis=1)

    column_lane = lax.broadcasted_iota(jnp.int32, (seqs, 256), 1)
    column_want = lax.rem(lax.broadcasted_iota(jnp.int32, (seqs, 256), 0), 4)

    def column(row):
        return jnp.sum(
            jnp.where(column_lane == column_want, picked(passages, row), 0.0), axis=1, keepdims=True
        )

    question_float, passage_float = whole(questions), whole(passages)
    positives, sets = column(12), column(13)
    first = lax.broadcasted_iota(jnp.int32, (seqs, seqs), 0)
    second = lax.broadcasted_iota(jnp.int32, (seqs, seqs), 1)
    set_row = jnp.sum(jnp.where(first == second, sets, 0.0), axis=0, keepdims=True)
    chosen = second.astype(F32) == positives
    query_set = jnp.sum(jnp.where(chosen, set_row, 0.0), axis=1, keepdims=True)
    logits = transposed_right(question_float.astype(LOW), passage_float.astype(LOW)) * SCALE
    masked = jnp.where(set_row == query_set, logits, NEG)
    weights = jnp.exp(masked - jnp.max(masked, axis=1, keepdims=True))
    softmax = weights / jnp.sum(weights, axis=1, keepdims=True)
    d_logits = (softmax - select(chosen)) * SCALE
    mine_row = lax.broadcasted_iota(jnp.int32, (8, seqs), 0)
    mine_column = lax.broadcasted_iota(jnp.int32, (8, seqs), 1)
    own = select((mine_column == me * 4 + mine_row) & (mine_row < 4))
    by_question = jnp.dot(own, d_logits, precision=HIGH, preferred_element_type=F32)
    by_passage = lax.dot_general(
        own, d_logits, (((1,), (1,)), ((), ())), precision=HIGH, preferred_element_type=F32
    )
    is_passage = tower == 1
    terms = jnp.where(is_passage, by_passage, by_question)
    others = jnp.where(is_passage, question_float, passage_float)
    grad = jnp.dot(terms, others, precision=HIGH, preferred_element_type=F32)
    return jnp.where(is_passage, grad, grad.astype(LOW).astype(F32))


def backward_kernel(
    n, lens, positives, datasets, pooled_ref, gain_ref, wqkv_hbm, wattn_hbm, win_hbm, wout_hbm,
    hidden_hbm, slope_hbm, n1_hbm, n2_hbm, inv_hbm, low_t_hbm, query_hbm, key_t_hbm, value_hbm, probs_hbm,
    context_t_hbm, x_t_hbm,
    out_ref, in_ref, attn_ref, qkv_ref, summed_small_ref, tokens_out,
    grads, paired, crossed, rows_got, relayed, got, z_first, pair_send, pair_recv, cross_send, cross_recv, z_send, z_recv,
    first_weights, second_weights, wide, tall, rows_a, rows_b, rows_c, key_t, context_t, inv, stage,
    rows_small, bias_in, small, small_got, mine, everyone, d_pooled,
    sems, stage_sems, small_send, small_recv, pool_send, pool_recv,
):
    tower, me = lax.axis_index("tower"), lax.axis_index("batch")
    chips = n // 2
    chip, core = me // 2, lax.rem(me, 2)
    sums = Sums(
        n, (grads, paired, crossed, rows_got, relayed, got, z_first, pair_send, pair_recv, cross_send, cross_recv, z_send, z_recv)
    )
    barrier = pltpu.get_barrier_semaphore()

    @pl.loop(1, n)
    def _(step):
        pl.semaphore_signal(
            barrier, inc=1, device_id=(tower, lax.rem(me + step, n)), device_id_type=MESH
        )

    @pl.loop(0, chips)
    def _(other):
        pl.semaphore_signal(
            barrier, inc=1, device_id=(1 - tower, 2 * other + core), device_id_type=MESH
        )

    def load(place, source, target):
        return pltpu.make_async_copy(source, target, sems.at[place])

    def seq_rows(seq):
        return aligned(seq * 256, 256, 256)

    def block(part):
        return slice(768 * part, 768 * (part + 1))

    n2_load, inv_load = load(0, n2_hbm, rows_a), load(1, inv_hbm, inv)
    hidden_loads = [
        load(2 + part, hidden_hbm.at[:, aligned(sums.z_at(part + 1) * 768, 768, 128)], wide.at[:, block(part)])
        for part in range(4)
    ]
    slope_loads = [load(10 + part, slope_hbm.at[:, block(part)], wide.at[:, block(part)]) for part in range(4)]
    out_load = load(14, wout_hbm.at[0], first_weights)
    in_loads = [load(15 + part, win_hbm.at[0, :, block(part)], second_weights.at[block(part)]) for part in range(4)]
    n1_load, low_load = load(19, n1_hbm, rows_b), load(20, low_t_hbm, tall)
    key_load, context_load = load(21, key_t_hbm, key_t), load(22, context_t_hbm, context_t)
    attn_load = load(23, wattn_hbm.at[0], first_weights.at[block(0)])
    qkv_loads = [
        load(24 + part, wqkv_hbm.at[0, :, block(part)], first_weights.at[block(part + 1)]) for part in range(3)
    ]
    query_load, value_load, x_load = load(27, query_hbm, rows_a), load(28, value_hbm, rows_b), load(29, x_t_hbm, tall)

    def probs_load(seq):
        return load(30 + seq, probs_hbm.at[seq_rows(seq)], wide.at[seq_rows(seq)])

    for copy in [n2_load, inv_load] + hidden_loads + [out_load] + in_loads + [n1_load, low_load, key_load, context_load]:
        copy.start()

    row = lax.broadcasted_iota(jnp.int32, (4, 256), 0)
    lane = lax.broadcasted_iota(jnp.int32, (4, 256), 1)
    extra = jnp.zeros((4, 256), F32)
    for seq in range(4):
        for place, numbers in enumerate((positives, datasets)):
            extra = jnp.where((row == place) & (lane == seq), numbers[seq].astype(F32), extra)
    pooled = pooled_ref[...]
    pooled_block = jnp.concatenate(
        [pooled[:, 0:256], pooled[:, 256:512], pooled[:, 512:768], extra], axis=0
    ).astype(LOW)
    mine[...] = pooled_block

    @pl.when(tower == 0)
    def _():
        everyone[core, 0] = jnp.zeros((chips, 16, 256), LOW)

    everyone[core, tower, chip] = pooled_block
    rows_small[...] = jnp.zeros_like(rows_small)
    bias_in[...] = jnp.zeros_like(bias_in)
    pl.semaphore_wait(barrier, n - 1 + chips)

    def pool_copy(side, step, slot):
        return pltpu.make_async_remote_copy(
            src_ref=mine, dst_ref=everyone.at[core, tower, chip],
            send_sem=pool_send.at[slot], recv_sem=pool_recv.at[slot],
            device_id=(side, 2 * lax.rem(chip + step, chips) + core), device_id_type=MESH,
        )

    pool_forward = pltpu.make_async_remote_copy(
        src_ref=everyone.at[core], dst_ref=everyone.at[core],
        send_sem=pool_send.at[n], recv_sem=pool_recv.at[n],
        device_id=(tower, me + 1 - 2 * core), device_id_type=MESH,
    )

    @pl.loop(0, chips)
    def _(step):
        pool_copy(1 - tower, step, chips + step).start()

    @pl.when(tower == 1)
    def _():
        @pl.loop(1, chips)
        def _(step):
            pool_copy(1, step, step).start()

        @pl.loop(1, chips)
        def _(step):
            pool_copy(1, step, step).wait_recv()

    @pl.loop(0, chips)
    def _(step):
        pool_copy(1 - tower, step, chips + step).wait_recv()

    pool_forward.start()
    pool_forward.wait_recv()
    d_pooled[...] = d_pooled_of(n, tower, me, everyone)

    n2_load.wait()
    inv_load.wait()

    def second_backward(seq):
        length = lens[seq]
        grad_row = d_pooled[pl.ds(seq, 1)] / length.astype(F32)
        normal = rows_a[seq_rows(seq)].astype(F32)
        d_second, keep = second_norm_backward(
            grad_row, length, 0, normal, inv[seq_rows(seq), 64:65], gain_ref[0, 1:2]
        )
        return d_second, keep, normal, grad_row

    @pl.loop(0, 4)
    def _(seq):
        d_second, keep, normal, grad_row = second_backward(seq)
        low = d_second.astype(LOW)
        rows_c[seq_rows(seq)] = low
        rows_small[4:5] += jnp.sum(low.astype(F32), axis=0, keepdims=True)
        rows_small[5:6] += d_pooled[pl.ds(seq, 1)]
        rows_small[7:8] += grad_row * jnp.sum(jnp.where(keep, normal, 0.0), axis=0, keepdims=True)

    for part in range(4):
        hidden_loads[part].wait()
        for y in range(2):
            columns = slice(768 * part + 384 * y, 768 * part + 384 * (y + 1))
            grads[part, y] = transposed_left(wide[:, columns], rows_c[...]).astype(LOW).reshape(2, 4, 48, 768)
        slope_loads[part].start()
        sums.pair(part)
        if part > 0:
            sums.cross(part - 1)

    @pl.loop(0, chips)
    def _(step):
        pool_copy(1 - tower, step, chips + step).wait_send()

    @pl.when(tower == 1)
    def _():
        @pl.loop(1, chips)
        def _(step):
            pool_copy(1, step, step).wait_send()

    pool_forward.wait_send()

    for copy in [out_load] + in_loads + [n1_load] + slope_loads:
        copy.wait()

    def stage_copy(seq, kind):
        slot, rows = stage.at[lax.rem(seq, 2)], tokens_out.at[seq_rows(seq)]
        source, target = (rows, slot) if kind == 1 else (slot, rows)
        return pltpu.make_async_copy(source, target, stage_sems.at[kind, seq])

    @pl.loop(0, 4)
    def _(seq):
        @pl.when(seq >= 2)
        def _():
            sums.spread(lax.max(seq - 2, 0), by_rows=True)

        @pl.when(seq == 1)
        def _():
            sums.cross(3)

        rows = seq_rows(seq)
        d_second = second_backward(seq)[0]
        d_branch = rows_c[rows]
        d_first = d_second
        ahead, late = transposed_right(d_branch, first_weights[block(0), :]), None
        for part in range(4):
            d_hidden = ahead
            if part < 3:
                ahead = transposed_right(d_branch, first_weights[block(part + 1), :])
            d_pre = (d_hidden * wide[rows, block(part)].astype(F32)).astype(LOW)
            wide[rows, block(part)] = d_pre
            bias_in[:, block(part)] += jnp.sum(d_pre.astype(F32), axis=0, keepdims=True)
            if late is not None:
                d_first = d_first + transposed_right(late, second_weights[block(part - 1), :])
            late = d_pre
        d_first = d_first + transposed_right(late, second_weights[block(3), :])
        normal = rows_b[rows].astype(F32)
        scaled = d_first * gain_ref[0, 0:1]
        mean = jnp.mean(scaled, axis=1, keepdims=True)
        along = jnp.mean(scaled * normal, axis=1, keepdims=True)
        d_sum_one = inv[rows, 0:1] * (scaled - mean - normal * along)

        @pl.when(seq >= 2)
        def _():
            stage_copy(lax.max(seq - 2, 0), 0).wait()

        stage[lax.rem(seq, 2)] = d_sum_one
        stage_copy(seq, 0).start()
        d_attended = d_sum_one.astype(LOW)
        rows_c[rows] = d_attended
        rows_small[2:3] += jnp.sum(d_attended.astype(F32), axis=0, keepdims=True)
        rows_small[3:4] += jnp.sum(d_first, axis=0, keepdims=True)
        rows_small[6:7] += jnp.sum(d_first * normal, axis=0, keepdims=True)

    for copy in [attn_load] + qkv_loads + [query_load, value_load]:
        copy.start()
    low_load.wait()

    def store(chunk, rows_ref, columns):
        for half in range(2):
            grad = product(rows_ref[384 * half:384 * (half + 1)], columns).astype(LOW)
            for z in range(2):
                grads[chunk, :, :, 2 * half + z] = grad[192 * z:192 * (z + 1)].reshape(2, 2, 48, 768)
        sums.pair(chunk)

    for part in range(4):
        store(4 + part, tall, wide[:, block(part)])
        if part in (1, 2):
            sums.cross(3 + part)
        if part in (0, 2):
            sums.spread(2 + part // 2, by_rows=True, last=part == 2)
    for seq in range(4):
        probs_load(seq).start()
    x_load.start()

    context_load.wait()
    store(8, context_t, rows_c[...])
    for copy in [attn_load] + qkv_loads + [query_load, value_load, key_load]:
        copy.wait()
    lane = lax.broadcasted_iota(jnp.int32, (256, 128), 1)
    none = jnp.zeros((), LOW)

    @pl.loop(0, 4)
    def _(seq):
        rows = seq_rows(seq)

        @pl.when(seq >= 1)
        def _():
            sums.spread(3 + lax.max(seq, 1))

        @pl.when((seq == 1) | (seq == 2))
        def _():
            sums.cross(5 + lax.min(lax.max(seq, 1), 2))

        @pl.when(seq == 3)
        def _():
            sums.relay(4)

        @pl.when(seq == 0)
        def _():
            sums.z_first_spread(8)

        probs_load(seq).wait()
        d_attended = rows_c[rows]
        weight = first_weights[block(0), :]
        d_context = transposed_right(d_attended, weight).astype(LOW)
        d_context_t = transposed_right(weight, d_attended).astype(LOW)

        def d_probs_of(pair):
            lanes = slice(128 * pair, 128 * (pair + 1))
            value_pair = rows_b[rows, lanes]
            return [
                product(jnp.where(mask, value_pair, none), d_context_t[lanes]) for mask in (lane < 64, lane >= 64)
            ]

        ahead, late = d_probs_of(0), None

        def d_projected_of(pair, probs, d_scores):
            lanes = slice(128 * pair, 128 * (pair + 1))
            key_pair, query_pair, d_context_pair = key_t[lanes, rows], rows_a[rows, lanes], d_context[:, lanes]
            d_values = [product(prob, d_context_pair) for prob in probs]
            d_keys = [product(d_score, query_pair) for d_score in d_scores]
            d_queries = [product(key_pair[64 * one:64 * (one + 1)], d_scores[one]) for one in range(2)]
            d_query = (jnp.concatenate(d_queries, axis=0).T * 0.125).astype(LOW)
            d_key = jnp.where(lane < 64, d_keys[0], d_keys[1]).astype(LOW)
            d_value = jnp.where(lane < 64, d_values[0], d_values[1]).astype(LOW)
            for part, value in enumerate((d_query, d_key, d_value)):
                second_weights[aligned(1024 * part + seq * 256, 256, 256), lanes] = value
            rows_small[0:1, lanes] += jnp.sum(d_query.astype(F32), axis=0, keepdims=True)
            rows_small[1:2, lanes] += jnp.sum(d_value.astype(F32), axis=0, keepdims=True)

        for pair in range(6):
            d_probs = ahead
            if pair < 5:
                ahead = d_probs_of(pair + 1)
            lanes = slice(128 * pair, 128 * (pair + 1))
            weighed = d_context_t[lanes].astype(F32) * context_t[lanes, rows].astype(F32)
            probs, d_scores = [], []
            for one in range(2):
                head = 2 * pair + one
                row_sum = jnp.sum(weighed[64 * one:64 * (one + 1)], axis=0, keepdims=True)
                prob = wide[rows, 256 * head:256 * (head + 1)]
                probs.append(prob)
                d_scores.append((prob.astype(F32) * (d_probs[one] - row_sum)).astype(LOW))
            if late is not None:
                d_projected_of(*late)
            late = pair, probs, d_scores
        d_projected_of(*late)

    for seq in (2, 3):
        stage_copy(seq, 0).wait()
    for seq in (0, 1):
        stage_copy(seq, 1).start()
    x_load.wait()
    for part in range(3):
        store(9 + part, tall, second_weights[1024 * part:1024 * (part + 1), :])
        if part == 0:
            sums.relay(5)
            sums.spread(7)
        else:
            sums.cross(8 + part)

    bundle, bias_row = rows_small[...], bias_in[...]
    small[...] = jnp.zeros_like(small)
    for device in range(n):
        small[device, 0:8, 0:48] = bundle[:, 48 * device:48 * (device + 1)]
        for part in range(4):
            start = 192 * device + 48 * part
            small[device, 8 + part:9 + part, 0:48] = bias_row[:, start:start + 48]

    def small_copy(step):
        other = lax.rem(me + step, n)
        return pltpu.make_async_remote_copy(
            src_ref=small.at[other], dst_ref=small_got.at[step],
            send_sem=small_send.at[step], recv_sem=small_recv.at[step],
            device_id=(tower, other), device_id_type=MESH,
        )


    @pl.loop(1, n)
    def _(step):
        small_copy(step).start()

    def tokens(seq):
        stage_copy(seq, 1).wait()
        slot = seq % 2
        total = stage[slot]
        for part in range(3):
            total = total + transposed_right(
                second_weights[1024 * part + seq * 256:1024 * part + seq * 256 + 256, :],
                first_weights[block(part + 1), :],
            )
        stage[slot] = total
        stage_copy(seq, 2).start()

    tokens(0)
    tokens(1)
    sums.relay(6)
    sums.relay(7)
    sums.z_first_cross(8)
    sums.spread(9, straight=True)
    sums.cross(11)
    for seq in (2, 3):
        stage_copy(seq - 2, 2).wait()
        stage_copy(seq, 1).start()
    tokens(2)
    tokens(3)
    summed_small_ref[...] = small[me]

    @pl.loop(1, n)
    def _(step):
        small_copy(step).wait()
        summed_small_ref[...] += small_got[step]

    for chunk in range(3):
        sums.rows_copy(chunk).wait_recv()
    for part in range(4):
        out_ref[48 * part:48 * (part + 1)] = sums.rows_total(part)
    for chunk in range(4, 8):
        in_ref[:, block(chunk - 4)] = sums.total(chunk)
    attn_ref[...] = sums.z_first_total(8)
    sums.spread(10, straight=True)
    qkv_ref[:, block(0)] = sums.straight_total(9)
    sums.spread(11, straight=True)
    qkv_ref[:, block(1)] = sums.straight_total(10)
    qkv_ref[:, block(2)] = sums.straight_total(11)
    for seq in (2, 3):
        stage_copy(seq, 2).wait()
    sums.close()


def backward(lens, positives, datasets, pooled, gains, weights, activations, n):
    rows = activations[0].shape[0]
    anywhere = pl.BlockSpec(memory_space=pl.ANY)
    vmem = pl.BlockSpec(memory_space=pltpu.VMEM)
    scalars = pl.BlockSpec(memory_space=pltpu.SMEM)
    tile = (48, 768)
    dma = pltpu.SemaphoreType.DMA
    return pl.pallas_call(
        partial(backward_kernel, n),
        in_specs=[scalars] * 3 + [vmem] * 2 + [anywhere] * (4 + len(activations)),
        out_specs=[vmem] * 5 + [anywhere],
        out_shape=[
            jax.ShapeDtypeStruct(shape, F32)
            for shape in ((192, 768), (48, 3072), (48, 768), (48, 2304), (16, 128), (rows, 768))
        ],
        scratch_shapes=[
            pltpu.VMEM((CHUNKS, 2, 2, 4) + tile, LOW), pltpu.VMEM((CHUNKS, 2, 4) + tile, LOW),
            pltpu.VMEM((CHUNKS, 4) + tile, LOW), pltpu.VMEM((3, 4) + tile, LOW),
            pltpu.VMEM((4, 3) + tile, LOW), pltpu.VMEM((CHUNKS - 4, 3) + tile, LOW),
            pltpu.VMEM((3, 2) + tile, LOW),
            dma((CHUNKS,)), dma((CHUNKS,)), dma((CHUNKS,)), dma((CHUNKS,)), dma((CHUNKS, 3)), dma((CHUNKS, 3)),
            pltpu.VMEM((3072, 768), LOW), pltpu.VMEM((3072, 768), LOW), pltpu.VMEM((rows, 3072), LOW),
            pltpu.VMEM((768, rows), LOW), pltpu.VMEM((rows, 768), LOW), pltpu.VMEM((rows, 768), LOW),
            pltpu.VMEM((rows, 768), LOW), pltpu.VMEM((768, rows), LOW), pltpu.VMEM((768, rows), LOW),
            pltpu.VMEM((rows, 128), F32), pltpu.VMEM((2, 256, 768), F32),
            pltpu.VMEM((8, 768), F32), pltpu.VMEM((1, 3072), F32),
            pltpu.VMEM((n, 16, 128), F32), pltpu.VMEM((n, 16, 128), F32),
            pltpu.VMEM((16, 256), LOW), pltpu.VMEM((2, 2, n // 2, 16, 256), LOW), pltpu.VMEM((8, 768), F32),
            dma((34,)), dma((3, 4)), dma((n,)), dma((n,)), dma((2 * n,)), dma((2 * n,)),
        ],
        compiler_params=pltpu.CompilerParams(collective_id=1, has_side_effects=True, vmem_limit_bytes=60 * MIB),
        name="backward",
    )(lens, positives, datasets, pooled, gains, *weights, *activations)


def deliver_kernel(
    out_hbm, in_hbm, attn_hbm, qkv_hbm, small_hbm, tokens_hbm,
    out_to, in_to, attn_to, qkv_to, bias_in_to, vectors_to, gains_to, tokens_to,
    out_held, in_held, attn_held, qkv_held, small_held, held, sems,
):
    parts, rows = held.shape[0], held.shape[1]
    ways = [
        (tokens_hbm.at[pl.ds(rows * part, rows)], held.at[part], tokens_to.at[pl.ds(rows * part, rows)])
        for part in range(parts)
    ] + [
        (out_hbm, out_held, out_to), (in_hbm, in_held, in_to), (attn_hbm, attn_held, attn_to),
        (qkv_hbm, qkv_held, qkv_to),
    ]
    fetches = [
        pltpu.make_async_copy(source, middle, sems.at[0, place]) for place, (source, middle, _) in enumerate(ways)
    ]
    sends = [
        pltpu.make_async_copy(middle, target, sems.at[1, place]) for place, (_, middle, target) in enumerate(ways)
    ]
    small_fetch = pltpu.make_async_copy(small_hbm, small_held, sems.at[0, len(ways)])
    small_fetch.start()
    for fetch in fetches:
        fetch.start()
    for fetch, send in zip(fetches, sends):
        fetch.wait()
        send.start()
    small_fetch.wait()
    small = small_held[...]
    for row in range(6):
        vectors_to[row] = small[row:row + 1, :48]
    gains_to[...] = small[6:8, :48]
    bias_in_to[...] = jnp.concatenate([small[8 + part:9 + part, :48] for part in range(4)], axis=1)
    for send in sends:
        send.wait()


def deliver(*arrays):
    *sums, small, tokens = arrays
    anywhere = pl.BlockSpec(memory_space=pl.ANY)
    vmem = pl.BlockSpec(memory_space=pltpu.VMEM)
    shapes = [array.shape for array in sums] + [(1, 192), (6, 1, 48), (2, 48), tokens.shape]
    rows, width = tokens.shape
    parts = 4
    return pl.pallas_call(
        deliver_kernel,
        in_specs=[anywhere] * 6,
        out_specs=[anywhere] * 4 + [vmem] * 3 + [anywhere],
        out_shape=[jax.ShapeDtypeStruct(shape, F32) for shape in shapes],
        scratch_shapes=[pltpu.VMEM(array.shape, F32) for array in sums]
        + [pltpu.VMEM(small.shape, F32), pltpu.VMEM((parts, rows // parts, width), F32)]
        + [pltpu.SemaphoreType.DMA((2, parts + 5))],
        compiler_params=pltpu.CompilerParams(vmem_limit_bytes=60 * MIB),
        name="deliver",
    )(*arrays)


def per_device(
    n,
    tokens, lengths, positives, datasets, w_qkv, w_attn_out, w_ffn_in, w_ffn_out, b_ffn_in, biases, gains,
):
    seq_count, seq_len, width = (tokens.shape[1], tokens.shape[2], tokens.shape[3])
    lens = lengths[0]
    inputs = tokens[0].reshape(seq_count * seq_len, width)
    weights = (w_qkv, w_attn_out, w_ffn_in, w_ffn_out)
    pooled, *activations = encoder(lens, inputs, *weights, b_ffn_in, biases.transpose(1, 0, 2), gains)
    *sums, grad_tokens = backward(lens, positives, datasets, pooled, gains, weights, activations, n)
    summed_out, summed_in, summed_attn, summed_qkv, bias_in, vectors, scales, grad_tokens = deliver(*sums, grad_tokens)
    return (
        pooled[None],
        grad_tokens.reshape(1, seq_count, seq_len, width),
        summed_qkv[None],
        summed_attn[None],
        summed_in[None],
        summed_out[None],
        bias_in,
        vectors.transpose(1, 0, 2),
        scales[None],
    )


def from_behind(value, axis, steps):
    count = lax.axis_size(axis)
    leading, last = (max(0, -steps), min(count, count - steps))
    return lax.ppermute(value, axis, [(source, source + steps) for source in range(leading, last)])


def loss_gradient_plain(pooled, positives, datasets):
    seq_count = pooled.shape[0]
    mine = pooled.astype(jnp.bfloat16)
    questions = from_behind(mine, "tower", 1)
    everyone, every_set = (
        lax.all_gather(mine, "batch", axis=0, tiled=True),
        lax.all_gather(datasets.astype(jnp.bfloat16), "batch", axis=0, tiled=True),
    )
    total_seqs = everyone.shape[0]
    columns = lax.broadcasted_iota(jnp.int32, (seq_count, total_seqs), 1)
    chosen = columns == positives[:, None]
    set_row = every_set.astype(jnp.float32)[None, :]
    query_set = jnp.sum(jnp.where(chosen, set_row, 0.0), axis=1, keepdims=True)
    allowed = set_row == query_set
    question_float = questions.astype(jnp.float32)
    everyone_float = everyone.astype(jnp.float32)
    logits = jnp.dot(question_float, everyone_float.T, precision=HIGH) * SCALE
    masked = jnp.where(allowed, logits, NEG)
    softmax_rows = jnp.exp(masked - jax.nn.logsumexp(masked, axis=1, keepdims=True))
    d_logits = (softmax_rows - chosen.astype(jnp.float32)) * SCALE
    d_questions = jnp.dot(d_logits, everyone_float, precision=HIGH).astype(jnp.bfloat16)
    passage_terms = jnp.dot(d_logits.T, question_float, precision=HIGH)
    d_passages = lax.psum_scatter(passage_terms, "batch", scatter_dimension=0, tiled=True)
    returned = from_behind(d_questions, "tower", -1)
    is_passage = lax.axis_index("tower") == 1
    return jnp.where(is_passage, d_passages, returned.astype(jnp.float32))


def per_device_plain(

    tokens, lengths, positives, datasets, w_qkv, w_attn_out, w_ffn_in, w_ffn_out, b_ffn_in, biases, gains,
):
    seq_count, seq_len, width = (tokens.shape[1], tokens.shape[2], tokens.shape[3])
    head_size = width // HEADS
    rows = seq_count * seq_len
    inputs = tokens[0].reshape(rows, width)
    lens = lengths[0]
    weight_qkv = w_qkv[0]
    weight_attn = w_attn_out[0]
    weight_in = w_ffn_in[0]
    weight_out = w_ffn_out[0]
    bias_in = b_ffn_in[0]
    vectors = biases[0]
    scales = gains[0]
    positions = lax.broadcasted_iota(jnp.int32, (seq_count, seq_len), 1)
    keep = positions < lens[:, None]
    keep_float = keep.astype(jnp.float32)
    lens_float = lens.astype(jnp.float32)[:, None]
    shape_heads = (seq_count, seq_len, HEADS, head_size)
    projected = product(inputs, weight_qkv)
    query = (projected[:, :width] + vectors[0]).astype(jnp.bfloat16)
    key_rows = projected[:, width : 2 * width].astype(jnp.bfloat16)
    value = (projected[:, 2 * width :] + vectors[1]).astype(jnp.bfloat16)
    query_heads = query.reshape(shape_heads)
    key_heads = key_rows.reshape(shape_heads)
    value_heads = value.reshape(shape_heads)
    scores = scores_of(query_heads, key_heads, keep)
    log_total = jax.nn.logsumexp(scores, axis=-1, keepdims=True)
    probs_low = jnp.exp(scores - log_total).astype(jnp.bfloat16)
    context = jnp.einsum(
        "shqk,skhe->sqhe", probs_low, value_heads, preferred_element_type=jnp.float32
    )
    context = context.reshape(rows, width).astype(jnp.bfloat16)
    attended = product(context, weight_attn) + vectors[2]
    first_norm, normed_one, inverse_one = norm_forward(
        inputs.astype(jnp.float32) + attended, scales[0], vectors[3]
    )
    first_low = first_norm.astype(jnp.bfloat16)
    hidden_pre = product(first_low, weight_in) + bias_in
    hidden = jax.nn.gelu(hidden_pre, approximate=False).astype(jnp.bfloat16)
    branch = product(hidden, weight_out) + vectors[4]
    output, normed_two, inverse_two = norm_forward(first_norm + branch, scales[1], vectors[5])
    pooled = (
        jnp.sum(output.reshape(seq_count, seq_len, width) * keep_float[:, :, None], axis=1)
        / lens_float
    )
    d_pooled = loss_gradient_plain(pooled, positives, datasets)
    d_output = ((d_pooled / lens_float)[:, None, :] * keep_float[:, :, None]).reshape(rows, width)
    d_second, d_gain_two, d_shift_two = norm_backward(d_output, normed_two, inverse_two, scales[1])
    d_branch = d_second.astype(jnp.bfloat16)
    g_weight_out = transposed_left(hidden, d_branch)
    g_bias_out = jnp.sum(d_branch.astype(jnp.float32), axis=0)
    d_hidden = transposed_right(d_branch, weight_out)
    gelu_pull = jax.vjp(partial(jax.nn.gelu, approximate=False), hidden_pre)[1]
    d_pre = gelu_pull(d_hidden)[0].astype(jnp.bfloat16)
    g_weight_in = transposed_left(first_low, d_pre)
    g_bias_in = jnp.sum(d_pre.astype(jnp.float32), axis=0)
    d_first = d_second + transposed_right(d_pre, weight_in)
    d_sum_one, d_gain_one, d_shift_one = norm_backward(d_first, normed_one, inverse_one, scales[0])
    d_attended = d_sum_one.astype(jnp.bfloat16)
    g_weight_attn = transposed_left(context, d_attended)
    g_bias_attn = jnp.sum(d_attended.astype(jnp.float32), axis=0)
    d_context = transposed_right(d_attended, weight_attn).astype(jnp.bfloat16).reshape(shape_heads)
    again = scores_of(query_heads, key_heads, keep)
    probs = jnp.exp(again - log_total)
    d_value = jnp.einsum(
        "shqk,sqhe->skhe", probs.astype(jnp.bfloat16), d_context, preferred_element_type=jnp.float32
    )
    d_probs = jnp.einsum(
        "sqhe,skhe->shqk", d_context, value_heads, preferred_element_type=jnp.float32
    )
    d_scores = (probs * (d_probs - jnp.sum(d_probs * probs, axis=-1, keepdims=True))).astype(
        jnp.bfloat16
    )
    d_query = (
        jnp.einsum("shqk,skhe->sqhe", d_scores, key_heads, preferred_element_type=jnp.float32)
        * 0.125
    )
    d_key = (
        jnp.einsum("shqk,sqhe->skhe", d_scores, query_heads, preferred_element_type=jnp.float32)
        * 0.125
    )
    d_query_low = d_query.reshape(rows, width).astype(jnp.bfloat16)
    d_key_low = d_key.reshape(rows, width).astype(jnp.bfloat16)
    d_value_low = d_value.reshape(rows, width).astype(jnp.bfloat16)
    d_projected = jnp.concatenate([d_query_low, d_key_low, d_value_low], axis=1)
    g_weight_qkv = transposed_left(inputs, d_projected)
    g_bias_query = jnp.sum(d_query_low.astype(jnp.float32), axis=0)
    g_bias_value = jnp.sum(d_value_low.astype(jnp.float32), axis=0)
    d_inputs = d_sum_one + transposed_right(d_projected, weight_qkv)
    g_vectors = jnp.stack(
        [g_bias_query, g_bias_value, g_bias_attn, d_shift_one, g_bias_out, d_shift_two]
    )
    g_scales = jnp.stack([d_gain_one, d_gain_two])

    def scatter(value, dimension):
        return lax.psum_scatter(value, "batch", scatter_dimension=dimension, tiled=True)

    summed_qkv, summed_attn, summed_in, summed_out = (
        scatter(g_weight_qkv, 0), scatter(g_weight_attn, 0), scatter(g_weight_in, 0), scatter(g_weight_out, 0)
    )
    summed_bias_in, summed_vectors, summed_scales = (
        scatter(g_bias_in, 0), scatter(g_vectors, 1), scatter(g_scales, 1)
    )
    return (
        pooled[None],
        d_inputs.reshape(1, seq_count, seq_len, width),
        summed_qkv[None],
        summed_attn[None],
        summed_in[None],
        summed_out[None],
        summed_bias_in[None],
        summed_vectors[None],
        summed_scales[None],
    )


def solution(mesh):
    n = mesh.shape["batch"]
    direct = n == 16
    in_specs = (
        P("tower", "batch", None, None),
        P("tower", "batch"),
        P("batch"),
        P("batch"),
        P("tower", None, None),
        P("tower", None, None),
        P("tower", None, None),
        P("tower", None, None),
        P("tower", None),
        P("tower", None, None),
        P("tower", None, None),
    )
    out_specs = (
        P("tower", "batch", None),
        P("tower", "batch", None, None),
        P("tower", "batch", None),
        P("tower", "batch", None),
        P("tower", "batch", None),
        P("tower", "batch", None),
        P("tower", "batch"),
        P("tower", None, "batch"),
        P("tower", None, "batch"),
    )
    return jax.shard_map(
        partial(per_device, n) if direct else per_device_plain, mesh=mesh, in_specs=in_specs, out_specs=out_specs, check_vma=False
    )
```

```python
from functools import partial

import jax
import jax.numpy as jnp
from jax import lax
from jax.experimental import pallas as pl
from jax.experimental.pallas import tpu as pltpu
from jax.sharding import PartitionSpec as P

HEADS = 12
EPS = 1e-12
SCALE = 4.0
HIGH = lax.Precision.HIGHEST
MESH = pl.DeviceIdType.MESH
NEG = -1000000000.0
LOW = jnp.bfloat16
F32 = jnp.float32
CHUNKS = 12
MIB = 2**20


def product(left, right):
    return jnp.dot(left, right, preferred_element_type=jnp.float32)


def transposed_left(left, right):
    return lax.dot_general(
        left, right, (((0,), (0,)), ((), ())), preferred_element_type=jnp.float32
    )


def transposed_right(left, right):
    return lax.dot_general(
        left, right, (((1,), (1,)), ((), ())), preferred_element_type=jnp.float32
    )


def norm_forward(total, gain, shift):
    mean = jnp.mean(total, axis=-1, keepdims=True)
    centered = total - mean
    inverse = lax.rsqrt(jnp.mean(centered * centered, axis=-1, keepdims=True) + EPS)
    normed = centered * inverse
    return (normed * gain + shift, normed, inverse)


def norm_backward(grad, normed, inverse, gain):
    scaled = grad * gain
    first_mean = jnp.mean(scaled, axis=-1, keepdims=True)
    second_mean = jnp.mean(scaled * normed, axis=-1, keepdims=True)
    d_total = inverse * (scaled - first_mean - normed * second_mean)
    return (d_total, jnp.sum(grad * normed, axis=0), jnp.sum(grad, axis=0))


def scores_of(query_heads, key_heads, keep):
    raw = (
        jnp.einsum("sqhe,skhe->shqk", query_heads, key_heads, preferred_element_type=jnp.float32)
        * 0.125
    )
    return jnp.where(keep[:, None, None, :], raw, NEG)


def gelu_parts(z):
    t = 1.0 / (1.0 + jnp.abs(z) * (0.3275911 * 0.7071067811865476))
    bell = jnp.exp(z * z * -0.5)
    tail = t * bell * (
        0.127414796 + t * (-0.142248368 + t * (0.7107068705 + t * (-0.7265760135 + t * 0.5307027145)))
    )
    below = jnp.where(z < 0.0, tail, 1.0 - tail)
    return z * below, below + z * bell * 0.3989422804014327


def normed(total):
    mean = jnp.mean(total, axis=-1, keepdims=True)
    centered = total - mean
    inverse = lax.rsqrt(jnp.mean(centered * centered, axis=-1, keepdims=True) + EPS)
    return centered * inverse, inverse


def encoder_kernel(
    lens, x_ref, wqkv_hbm, wattn_hbm, win_hbm, wout_hbm, bin_ref, vec_ref, gain_ref,
    pooled_ref, hidden_ref, slope_ref, n1_ref, n2_ref, inv_ref, low_t_ref, query_ref, key_t_ref, value_ref, probs_ref,
    context_t_ref, x_t_ref,
    wqkv, wattn, win, wout, sems,
):
    step = pl.program_id(0)
    loads = [
        pltpu.make_async_copy(source.at[0], target, sems.at[place])
        for place, (source, target) in enumerate(
            [(wqkv_hbm, wqkv), (wattn_hbm, wattn), (win_hbm, win), (wout_hbm, wout)]
        )
    ]

    @pl.when(step == 0)
    def _():
        for load in loads:
            load.start()
        loads[0].wait()

    length = lens[step]
    x = x_ref[...]
    rows = x.shape[0]
    query = (product(x, wqkv[:, :768]) + vec_ref[0]).astype(LOW) * 0.125
    key = product(x, wqkv[:, 768:1536]).astype(LOW)
    value = (product(x, wqkv[:, 1536:]) + vec_ref[1]).astype(LOW)
    query_ref[...] = query
    value_ref[...] = value
    key_t_ref[...] = key.T
    x_t_ref[...] = x.T
    value_t = value.T
    blocked = jnp.where(lax.broadcasted_iota(jnp.int32, (rows, 1), 0) < length, 0.0, NEG)
    lane = lax.broadcasted_iota(jnp.int32, (rows, 128), 1)

    def scores_of_head(head):
        pair = slice(128 * (head // 2), 128 * (head // 2 + 1))
        mine = (lane < 64) if head % 2 == 0 else (lane >= 64)
        key_one = jnp.where(mine, key[:, pair], jnp.zeros((), LOW))
        return transposed_right(key_one, query[:, pair]) + blocked

    def context_of_head(head, probs):
        context_t_ref[64 * head:64 * (head + 1), :] = product(
            value_t[64 * head:64 * (head + 1)], probs
        ).astype(LOW)

    ahead, behind = [scores_of_head(head) for head in range(4)], []
    for head in range(HEADS):
        if head + 4 < HEADS:
            ahead.append(scores_of_head(head + 4))
        scores = ahead.pop(0)
        weights = jnp.exp(scores - jnp.max(scores, axis=0, keepdims=True))
        probs = (weights * (1.0 / jnp.sum(weights, axis=0, keepdims=True))).astype(LOW)
        probs_ref[:, 256 * head:256 * (head + 1)] = probs
        behind.append((head, probs))
        if len(behind) > 2:
            context_of_head(*behind.pop(0))
    for item in behind:
        context_of_head(*item)

    @pl.when(step == 0)
    def _():
        loads[1].wait()

    attended = transposed_left(context_t_ref[...], wattn[...]) + vec_ref[2]
    n1, inv1 = normed(x.astype(F32) + attended)
    first = n1 * gain_ref[0, 0:1] + vec_ref[3]
    first_low = first.astype(LOW)
    low_t_ref[...] = first_low.T
    n1_ref[...] = n1.astype(LOW)

    @pl.when(step == 0)
    def _():
        loads[2].wait()
        loads[3].wait()

    total = first + vec_ref[4]
    blocks = [slice(768 * part, 768 * (part + 1)) for part in range(4)]
    ahead, late = product(first_low, win[:, blocks[0]]), None
    for part in range(4):
        before = ahead
        if part + 1 < 4:
            ahead = product(first_low, win[:, blocks[part + 1]])
        hidden, slope = gelu_parts(before + bin_ref[:, blocks[part]])
        hidden = hidden.astype(LOW)
        hidden_ref[:, blocks[part]] = hidden
        slope_ref[:, blocks[part]] = slope.astype(LOW)
        if late is not None:
            total = total + product(late, wout[blocks[part - 1], :])
        late = hidden
    total = total + product(late, wout[blocks[3], :])
    n2, inv2 = normed(total)
    n2_ref[...] = n2.astype(LOW)
    inv_ref[...] = jnp.where(lane < 64, inv1, inv2)
    output = n2 * gain_ref[0, 1:2] + vec_ref[5]
    keep = lax.broadcasted_iota(jnp.int32, (rows, 1), 0) < length
    pooled_ref[pl.ds(step, 1)] = jnp.sum(jnp.where(keep, output, 0.0), axis=0, keepdims=True) / length.astype(F32)


def encoder(lens, x, w_qkv, w_attn, w_in, w_out, b_in, vectors, gains):
    seqs = lens.shape[0]
    rows = x.shape[0]
    per = rows // seqs

    def by_rows(width):
        return pl.BlockSpec((per, width), lambda s, *_: (s, 0))

    def by_columns(height):
        return pl.BlockSpec((height, per), lambda s, *_: (0, s))

    def full(*shape):
        return pl.BlockSpec(shape, lambda s, *_: (0,) * len(shape))

    anywhere = pl.BlockSpec(memory_space=pl.ANY)
    def wide(width, kind=LOW):
        return by_rows(width), jax.ShapeDtypeStruct((rows, width), kind)

    tall = by_columns(768), jax.ShapeDtypeStruct((768, rows), LOW)
    kept = [
        wide(3072), wide(3072), wide(768), wide(768), wide(128, F32), tall,
        wide(768), tall, wide(768), wide(3072), tall, tall,
    ]
    return pl.pallas_call(
        encoder_kernel,
        grid_spec=pltpu.PrefetchScalarGridSpec(
            num_scalar_prefetch=1,
            grid=(seqs,),
            in_specs=[by_rows(768)] + [anywhere] * 4 + [full(1, 3072), full(6, 1, 768), full(1, 2, 768)],
            out_specs=[full(seqs, 768)] + [spec for spec, _ in kept],
            scratch_shapes=[
                pltpu.VMEM((768, 2304), LOW), pltpu.VMEM((768, 768), LOW),
                pltpu.VMEM((768, 3072), LOW), pltpu.VMEM((3072, 768), LOW),
                pltpu.SemaphoreType.DMA((4,)),
            ],
        ),
        out_shape=[jax.ShapeDtypeStruct((seqs, 768), F32)] + [shape for _, shape in kept],
        compiler_params=pltpu.CompilerParams(vmem_limit_bytes=56 * MIB),
        name="encoder",
    )(lens, x, w_qkv, w_attn, w_in, w_out, b_in, vectors, gains)


def second_norm_backward(grad_row, length, first_row, n2, inv2, gain):
    scaled = grad_row * gain
    mean = jnp.mean(scaled, axis=1, keepdims=True)
    along = jnp.mean(scaled * n2, axis=1, keepdims=True)
    keep = first_row + lax.broadcasted_iota(jnp.int32, (n2.shape[0], 1), 0) < length
    return jnp.where(keep, inv2 * (scaled - mean - n2 * along), 0.0), keep


def select(condition):
    return jnp.where(condition, 1.0, 0.0)


def aligned(start, size, multiple):
    return pl.ds(pl.multiple_of(start, multiple), size)


class Sums:
    def __init__(self, n, scratch):
        (self.grads, self.paired, self.crossed, self.rows_got, self.relayed, self.got, self.z_first, self.pair_send, self.pair_recv,
         self.cross_send, self.cross_recv, self.z_send, self.z_recv) = scratch
        self.tower, self.me = lax.axis_index("tower"), lax.axis_index("batch")
        self.depth = n // 4
        self.z, self.y, self.core = self.me // 4, lax.rem(self.me // 2, 2), lax.rem(self.me, 2)
        self.inner = (self.z == 1) | (self.z == 2)
        self.beside = jnp.where(self.z < 2, 1 - self.z, 5 - self.z)
        self.first = jnp.where(self.z < 2, 1, 0)

    def z_at(self, offset):
        return lax.rem(self.z + offset, self.depth)

    def device(self, z, y, core):
        return (self.tower, z * 4 + y * 2 + core)

    def pair_copy(self, chunk):
        return pltpu.make_async_remote_copy(
            src_ref=self.grads.at[chunk, :, 1 - self.core], dst_ref=self.paired.at[chunk],
            send_sem=self.pair_send.at[chunk], recv_sem=self.pair_recv.at[chunk],
            device_id=self.device(self.z, self.y, 1 - self.core), device_id_type=MESH,
        )

    def cross_copy(self, chunk):
        return pltpu.make_async_remote_copy(
            src_ref=self.grads.at[chunk, 1 - self.y, self.core], dst_ref=self.crossed.at[chunk],
            send_sem=self.cross_send.at[chunk], recv_sem=self.cross_recv.at[chunk],
            device_id=self.device(self.z, 1 - self.y, self.core), device_id_type=MESH,
        )

    def rows_copy(self, chunk):
        return pltpu.make_async_remote_copy(
            src_ref=self.grads.at[chunk, self.y, self.core], dst_ref=self.rows_got.at[chunk],
            send_sem=self.z_send.at[chunk, 0], recv_sem=self.z_recv.at[chunk, 0],
            device_id=self.device(self.z_at(chunk + 1), self.y, self.core), device_id_type=MESH,
        )

    def z_copy(self, chunk, part, target, slot):
        return pltpu.make_async_remote_copy(
            src_ref=self.grads.at[chunk, self.y, self.core, part], dst_ref=self.got.at[chunk - 4, slot],
            send_sem=self.z_send.at[chunk, slot], recv_sem=self.z_recv.at[chunk, slot],
            device_id=self.device(target, self.y, self.core), device_id_type=MESH,
        )

    def relay_copy(self, chunk):
        return pltpu.make_async_remote_copy(
            src_ref=self.grads.at[chunk, self.y, self.core, pl.ds(self.first, 3)], dst_ref=self.relayed.at[chunk - 4],
            send_sem=self.z_send.at[chunk, 2], recv_sem=self.z_recv.at[chunk, 2],
            device_id=self.device(self.beside, self.y, self.core), device_id_type=MESH,
        )

    def near_copy(self, chunk):
        return pltpu.make_async_remote_copy(
            src_ref=self.grads.at[chunk, self.y, self.core, self.beside], dst_ref=self.got.at[chunk - 4, 0],
            send_sem=self.z_send.at[chunk, 2], recv_sem=self.z_recv.at[chunk, 0],
            device_id=self.device(self.beside, self.y, self.core), device_id_type=MESH,
        )

    def mate_copy(self, chunk):
        return self.z_copy(chunk, 3 - self.z, 3 - self.z, 0)

    def far_copy(self, chunk):
        far = 3 - self.beside
        return self.z_copy(chunk, far, far, 1)

    def straight_copy(self, chunk, offset):
        return self.z_copy(chunk, self.z_at(offset), self.z_at(offset), offset - 1)

    def z_first_copy(self, chunk, offset):
        return pltpu.make_async_remote_copy(
            src_ref=self.grads.at[chunk, :, self.core, self.z_at(offset)], dst_ref=self.z_first.at[offset - 1],
            send_sem=self.z_send.at[chunk, offset - 1], recv_sem=self.z_recv.at[chunk, offset - 1],
            device_id=self.device(self.z_at(offset), self.y, self.core), device_id_type=MESH,
        )

    def y_last_copy(self, chunk):
        return pltpu.make_async_remote_copy(
            src_ref=self.grads.at[chunk, 1 - self.y, self.core, self.z], dst_ref=self.crossed.at[chunk, 0],
            send_sem=self.cross_send.at[chunk], recv_sem=self.cross_recv.at[chunk],
            device_id=self.device(self.z, 1 - self.y, self.core), device_id_type=MESH,
        )

    def z_first_spread(self, chunk):
        self.pair_copy(chunk).wait_recv()
        for y in range(2):
            for z in range(self.depth):
                place = (chunk, y, self.core, z)
                self.grads[place] = (self.grads[place].astype(F32) + self.paired[chunk, y, z].astype(F32)).astype(LOW)
        for offset in range(1, self.depth):
            self.z_first_copy(chunk, offset).start()

    def z_first_sum(self, chunk, y):
        total = self.grads[chunk, y, self.core, self.z].astype(F32)
        for slot in range(self.depth - 1):
            total = total + self.z_first[slot, y].astype(F32)
        return total

    def z_first_cross(self, chunk):
        for offset in range(1, self.depth):
            self.z_first_copy(chunk, offset).wait_recv()
        self.grads[chunk, 1 - self.y, self.core, self.z] = self.z_first_sum(chunk, 1 - self.y).astype(LOW)
        self.y_last_copy(chunk).start()

    def z_first_total(self, chunk):
        self.y_last_copy(chunk).wait_recv()
        return self.z_first_sum(chunk, self.y) + self.crossed[chunk, 0].astype(F32)

    def pair(self, chunk):
        self.pair_copy(chunk).start()

    def cross(self, chunk):
        self.pair_copy(chunk).wait_recv()
        for part in range(4):
            place = (chunk, 1 - self.y, self.core, part)
            self.grads[place] = (
                self.grads[place].astype(F32) + self.paired[chunk, 1 - self.y, part].astype(F32)
            ).astype(LOW)
        self.cross_copy(chunk).start()

    def spread(self, chunk, by_rows=False, last=False, straight=False):
        self.cross_copy(chunk).wait_recv()
        for part in range(4):
            place = (chunk, self.y, self.core, part)
            self.grads[place] = (
                self.grads[place].astype(F32) + self.paired[chunk, self.y, part].astype(F32)
                + self.crossed[chunk, part].astype(F32)
            ).astype(LOW)
        if by_rows:
            if not last:
                self.rows_copy(chunk).start()
        elif straight:
            for offset in range(1, self.depth):
                self.straight_copy(chunk, offset).start()
        else:
            @pl.when(self.inner)
            def _():
                self.near_copy(chunk).start()

            @pl.when(jnp.logical_not(self.inner))
            def _():
                self.relay_copy(chunk).start()

    def relay(self, chunk):
        @pl.when(self.inner)
        def _():
            self.relay_copy(chunk).wait_recv()
            for part in range(3):
                place = (chunk, self.y, self.core, self.first + part)
                self.grads[place] = (
                    self.grads[place].astype(F32) + self.relayed[chunk - 4, part].astype(F32)
                ).astype(LOW)
            self.mate_copy(chunk).start()
            self.far_copy(chunk).start()

    def rows_total(self, part):
        total = self.grads[3, self.y, self.core, part].astype(F32)
        for chunk in range(3):
            total = total + self.rows_got[chunk, part].astype(F32)
        return total

    def total(self, chunk):
        self.mate_copy(chunk).wait_recv()

        @pl.when(jnp.logical_not(self.inner))
        def _():
            self.far_copy(chunk).wait_recv()

        total = self.grads[chunk, self.y, self.core, self.z].astype(F32) + self.got[chunk - 4, 0].astype(F32)
        return total + jnp.where(self.inner, 0.0, self.got[chunk - 4, 1].astype(F32))

    def straight_total(self, chunk):
        total = self.grads[chunk, self.y, self.core, self.z].astype(F32)
        for offset in range(1, self.depth):
            self.straight_copy(chunk, offset).wait_recv()
            total = total + self.got[chunk - 4, offset - 1].astype(F32)
        return total

    def close(self):
        for chunk in range(CHUNKS):
            self.pair_copy(chunk).wait_send()
            (self.y_last_copy(chunk) if chunk == 8 else self.cross_copy(chunk)).wait_send()

        for offset in range(1, self.depth):
            self.z_first_copy(8, offset).wait_send()
            for chunk in range(9, CHUNKS):
                self.straight_copy(chunk, offset).wait_send()

        for chunk in range(3):
            self.rows_copy(chunk).wait_send()

        @pl.loop(4, 8)
        def _(chunk):
            @pl.when(self.inner)
            def _():
                self.near_copy(chunk).wait_send()
                self.mate_copy(chunk).wait_send()
                self.far_copy(chunk).wait_send()

            @pl.when(jnp.logical_not(self.inner))
            def _():
                self.relay_copy(chunk).wait_send()


def d_pooled_of(n, tower, me, everyone):
    seqs = 4 * n
    packed = everyone[...]
    questions, passages = (
        jnp.concatenate([packed[core, side].reshape(8 * n, 256) for core in range(2)], axis=0) for side in range(2)
    )
    rows = lax.broadcasted_iota(jnp.int32, (seqs, 16 * n), 0)
    places = lax.broadcasted_iota(jnp.int32, (seqs, 16 * n), 1)
    owner, lane = lax.rem(rows // 4, 2) * (n // 2) + rows // 8, lax.rem(rows, 4)

    def picked(values, row):
        return product(select(places == owner * 16 + row).astype(LOW), values)

    def whole(values):
        parts = [product(select(places == owner * 16 + 4 * part + lane).astype(LOW), values) for part in range(3)]
        return jnp.concatenate(parts, axis=1)

    column_lane = lax.broadcasted_iota(jnp.int32, (seqs, 256), 1)
    column_want = lax.rem(lax.broadcasted_iota(jnp.int32, (seqs, 256), 0), 4)

    def column(row):
        return jnp.sum(
            jnp.where(column_lane == column_want, picked(passages, row), 0.0), axis=1, keepdims=True
        )

    question_float, passage_float = whole(questions), whole(passages)
    positives, sets = column(12), column(13)
    first = lax.broadcasted_iota(jnp.int32, (seqs, seqs), 0)
    second = lax.broadcasted_iota(jnp.int32, (seqs, seqs), 1)
    set_row = jnp.sum(jnp.where(first == second, sets, 0.0), axis=0, keepdims=True)
    chosen = second.astype(F32) == positives
    query_set = jnp.sum(jnp.where(chosen, set_row, 0.0), axis=1, keepdims=True)
    logits = transposed_right(question_float.astype(LOW), passage_float.astype(LOW)) * SCALE
    masked = jnp.where(set_row == query_set, logits, NEG)
    weights = jnp.exp(masked - jnp.max(masked, axis=1, keepdims=True))
    softmax = weights / jnp.sum(weights, axis=1, keepdims=True)
    d_logits = (softmax - select(chosen)) * SCALE
    mine_row = lax.broadcasted_iota(jnp.int32, (8, seqs), 0)
    mine_column = lax.broadcasted_iota(jnp.int32, (8, seqs), 1)
    own = select((mine_column == me * 4 + mine_row) & (mine_row < 4))
    by_question = jnp.dot(own, d_logits, precision=HIGH, preferred_element_type=F32)
    by_passage = lax.dot_general(
        own, d_logits, (((1,), (1,)), ((), ())), precision=HIGH, preferred_element_type=F32
    )
    is_passage = tower == 1
    terms = jnp.where(is_passage, by_passage, by_question)
    others = jnp.where(is_passage, question_float, passage_float)
    grad = jnp.dot(terms, others, precision=HIGH, preferred_element_type=F32)
    return jnp.where(is_passage, grad, grad.astype(LOW).astype(F32))


def backward_kernel(
    n, lens, positives, datasets, pooled_ref, gain_ref, wqkv_hbm, wattn_hbm, win_hbm, wout_hbm,
    hidden_hbm, slope_hbm, n1_hbm, n2_hbm, inv_hbm, low_t_hbm, query_hbm, key_t_hbm, value_hbm, probs_hbm,
    context_t_hbm, x_t_hbm,
    out_ref, in_ref, attn_ref, qkv_ref, summed_small_ref, tokens_out,
    grads, paired, crossed, rows_got, relayed, got, z_first, pair_send, pair_recv, cross_send, cross_recv, z_send, z_recv,
    first_weights, second_weights, wide, tall, rows_a, rows_b, rows_c, key_t, context_t, inv, stage,
    rows_small, bias_in, small, small_got, mine, everyone, d_pooled,
    sems, stage_sems, small_send, small_recv, pool_send, pool_recv,
):
    tower, me = lax.axis_index("tower"), lax.axis_index("batch")
    chips = n // 2
    chip, core = me // 2, lax.rem(me, 2)
    sums = Sums(
        n, (grads, paired, crossed, rows_got, relayed, got, z_first, pair_send, pair_recv, cross_send, cross_recv, z_send, z_recv)
    )
    barrier = pltpu.get_barrier_semaphore()

    @pl.loop(1, n)
    def _(step):
        pl.semaphore_signal(
            barrier, inc=1, device_id=(tower, lax.rem(me + step, n)), device_id_type=MESH
        )

    @pl.loop(0, chips)
    def _(other):
        pl.semaphore_signal(
            barrier, inc=1, device_id=(1 - tower, 2 * other + core), device_id_type=MESH
        )

    def load(place, source, target):
        return pltpu.make_async_copy(source, target, sems.at[place])

    def seq_rows(seq):
        return aligned(seq * 256, 256, 256)

    def block(part):
        return slice(768 * part, 768 * (part + 1))

    n2_load, inv_load = load(0, n2_hbm, rows_a), load(1, inv_hbm, inv)
    hidden_loads = [
        load(2 + part, hidden_hbm.at[:, aligned(sums.z_at(part + 1) * 768, 768, 128)], wide.at[:, block(part)])
        for part in range(4)
    ]
    slope_loads = [load(10 + part, slope_hbm.at[:, block(part)], wide.at[:, block(part)]) for part in range(4)]
    out_load = load(14, wout_hbm.at[0], first_weights)
    in_loads = [load(15 + part, win_hbm.at[0, :, block(part)], second_weights.at[block(part)]) for part in range(4)]
    n1_load, low_load = load(19, n1_hbm, rows_b), load(20, low_t_hbm, tall)
    key_load, context_load = load(21, key_t_hbm, key_t), load(22, context_t_hbm, context_t)
    attn_load = load(23, wattn_hbm.at[0], first_weights.at[block(0)])
    qkv_loads = [
        load(24 + part, wqkv_hbm.at[0, :, block(part)], first_weights.at[block(part + 1)]) for part in range(3)
    ]
    query_load, value_load, x_load = load(27, query_hbm, rows_a), load(28, value_hbm, rows_b), load(29, x_t_hbm, tall)

    def probs_load(seq):
        return load(30 + seq, probs_hbm.at[seq_rows(seq)], wide.at[seq_rows(seq)])

    for copy in [n2_load, inv_load] + hidden_loads + [out_load] + in_loads + [n1_load, low_load, key_load, context_load]:
        copy.start()

    row = lax.broadcasted_iota(jnp.int32, (4, 256), 0)
    lane = lax.broadcasted_iota(jnp.int32, (4, 256), 1)
    extra = jnp.zeros((4, 256), F32)
    for seq in range(4):
        for place, numbers in enumerate((positives, datasets)):
            extra = jnp.where((row == place) & (lane == seq), numbers[seq].astype(F32), extra)
    pooled = pooled_ref[...]
    pooled_block = jnp.concatenate(
        [pooled[:, 0:256], pooled[:, 256:512], pooled[:, 512:768], extra], axis=0
    ).astype(LOW)
    mine[...] = pooled_block

    @pl.when(tower == 0)
    def _():
        everyone[core, 0] = jnp.zeros((chips, 16, 256), LOW)

    everyone[core, tower, chip] = pooled_block
    rows_small[...] = jnp.zeros_like(rows_small)
    bias_in[...] = jnp.zeros_like(bias_in)
    pl.semaphore_wait(barrier, n - 1 + chips)

    def pool_copy(side, step, slot):
        return pltpu.make_async_remote_copy(
            src_ref=mine, dst_ref=everyone.at[core, tower, chip],
            send_sem=pool_send.at[slot], recv_sem=pool_recv.at[slot],
            device_id=(side, 2 * lax.rem(chip + step, chips) + core), device_id_type=MESH,
        )

    pool_forward = pltpu.make_async_remote_copy(
        src_ref=everyone.at[core], dst_ref=everyone.at[core],
        send_sem=pool_send.at[n], recv_sem=pool_recv.at[n],
        device_id=(tower, me + 1 - 2 * core), device_id_type=MESH,
    )

    @pl.loop(0, chips)
    def _(step):
        pool_copy(1 - tower, step, chips + step).start()

    @pl.when(tower == 1)
    def _():
        @pl.loop(1, chips)
        def _(step):
            pool_copy(1, step, step).start()

        @pl.loop(1, chips)
        def _(step):
            pool_copy(1, step, step).wait_recv()

    @pl.loop(0, chips)
    def _(step):
        pool_copy(1 - tower, step, chips + step).wait_recv()

    pool_forward.start()
    pool_forward.wait_recv()
    d_pooled[...] = d_pooled_of(n, tower, me, everyone)

    n2_load.wait()
    inv_load.wait()

    def second_backward(seq):
        length = lens[seq]
        grad_row = d_pooled[pl.ds(seq, 1)] / length.astype(F32)
        normal = rows_a[seq_rows(seq)].astype(F32)
        d_second, keep = second_norm_backward(
            grad_row, length, 0, normal, inv[seq_rows(seq), 64:65], gain_ref[0, 1:2]
        )
        return d_second, keep, normal, grad_row

    @pl.loop(0, 4)
    def _(seq):
        d_second, keep, normal, grad_row = second_backward(seq)
        low = d_second.astype(LOW)
        rows_c[seq_rows(seq)] = low
        rows_small[4:5] += jnp.sum(low.astype(F32), axis=0, keepdims=True)
        rows_small[5:6] += d_pooled[pl.ds(seq, 1)]
        rows_small[7:8] += grad_row * jnp.sum(jnp.where(keep, normal, 0.0), axis=0, keepdims=True)

    for part in range(4):
        hidden_loads[part].wait()
        for y in range(2):
            columns = slice(768 * part + 384 * y, 768 * part + 384 * (y + 1))
            grads[part, y] = transposed_left(wide[:, columns], rows_c[...]).astype(LOW).reshape(2, 4, 48, 768)
        slope_loads[part].start()
        sums.pair(part)
        if part > 0:
            sums.cross(part - 1)

    @pl.loop(0, chips)
    def _(step):
        pool_copy(1 - tower, step, chips + step).wait_send()

    @pl.when(tower == 1)
    def _():
        @pl.loop(1, chips)
        def _(step):
            pool_copy(1, step, step).wait_send()

    pool_forward.wait_send()

    for copy in [out_load] + in_loads + [n1_load] + slope_loads:
        copy.wait()

    def stage_copy(seq, kind):
        slot, rows = stage.at[lax.rem(seq, 2)], tokens_out.at[seq_rows(seq)]
        source, target = (rows, slot) if kind == 1 else (slot, rows)
        return pltpu.make_async_copy(source, target, stage_sems.at[kind, seq])

    @pl.loop(0, 4)
    def _(seq):
        @pl.when(seq >= 2)
        def _():
            sums.spread(lax.max(seq - 2, 0), by_rows=True)

        @pl.when(seq == 1)
        def _():
            sums.cross(3)

        rows = seq_rows(seq)
        d_second = second_backward(seq)[0]
        d_branch = rows_c[rows]
        d_first = d_second
        ahead, late = transposed_right(d_branch, first_weights[block(0), :]), None
        for part in range(4):
            d_hidden = ahead
            if part < 3:
                ahead = transposed_right(d_branch, first_weights[block(part + 1), :])
            d_pre = (d_hidden * wide[rows, block(part)].astype(F32)).astype(LOW)
            wide[rows, block(part)] = d_pre
            bias_in[:, block(part)] += jnp.sum(d_pre.astype(F32), axis=0, keepdims=True)
            if late is not None:
                d_first = d_first + transposed_right(late, second_weights[block(part - 1), :])
            late = d_pre
        d_first = d_first + transposed_right(late, second_weights[block(3), :])
        normal = rows_b[rows].astype(F32)
        scaled = d_first * gain_ref[0, 0:1]
        mean = jnp.mean(scaled, axis=1, keepdims=True)
        along = jnp.mean(scaled * normal, axis=1, keepdims=True)
        d_sum_one = inv[rows, 0:1] * (scaled - mean - normal * along)

        @pl.when(seq >= 2)
        def _():
            stage_copy(lax.max(seq - 2, 0), 0).wait()

        stage[lax.rem(seq, 2)] = d_sum_one
        stage_copy(seq, 0).start()
        d_attended = d_sum_one.astype(LOW)
        rows_c[rows] = d_attended
        rows_small[2:3] += jnp.sum(d_attended.astype(F32), axis=0, keepdims=True)
        rows_small[3:4] += jnp.sum(d_first, axis=0, keepdims=True)
        rows_small[6:7] += jnp.sum(d_first * normal, axis=0, keepdims=True)

    for copy in [attn_load] + qkv_loads + [query_load, value_load]:
        copy.start()
    low_load.wait()

    def store(chunk, rows_ref, columns):
        for half in range(2):
            grad = product(rows_ref[384 * half:384 * (half + 1)], columns).astype(LOW)
            for z in range(2):
                grads[chunk, :, :, 2 * half + z] = grad[192 * z:192 * (z + 1)].reshape(2, 2, 48, 768)
        sums.pair(chunk)

    for part in range(4):
        store(4 + part, tall, wide[:, block(part)])
        if part in (1, 2):
            sums.cross(3 + part)
        if part in (0, 2):
            sums.spread(2 + part // 2, by_rows=True, last=part == 2)
    for seq in range(4):
        probs_load(seq).start()
    x_load.start()

    context_load.wait()
    store(8, context_t, rows_c[...])
    for copy in [attn_load] + qkv_loads + [query_load, value_load, key_load]:
        copy.wait()
    lane = lax.broadcasted_iota(jnp.int32, (256, 128), 1)
    none = jnp.zeros((), LOW)

    @pl.loop(0, 4)
    def _(seq):
        rows = seq_rows(seq)

        @pl.when(seq >= 1)
        def _():
            sums.spread(3 + lax.max(seq, 1))

        @pl.when((seq == 1) | (seq == 2))
        def _():
            sums.cross(5 + lax.min(lax.max(seq, 1), 2))

        @pl.when(seq == 3)
        def _():
            sums.relay(4)

        @pl.when(seq == 0)
        def _():
            sums.z_first_spread(8)

        probs_load(seq).wait()
        d_attended = rows_c[rows]
        weight = first_weights[block(0), :]
        d_context = transposed_right(d_attended, weight).astype(LOW)
        d_context_t = transposed_right(weight, d_attended).astype(LOW)

        def d_probs_of(pair):
            lanes = slice(128 * pair, 128 * (pair + 1))
            value_pair = rows_b[rows, lanes]
            return [
                product(jnp.where(mask, value_pair, none), d_context_t[lanes]) for mask in (lane < 64, lane >= 64)
            ]

        ahead, late = d_probs_of(0), None

        def d_projected_of(pair, probs, d_scores):
            lanes = slice(128 * pair, 128 * (pair + 1))
            key_pair, query_pair, d_context_pair = key_t[lanes, rows], rows_a[rows, lanes], d_context[:, lanes]
            d_values = [product(prob, d_context_pair) for prob in probs]
            d_keys = [product(d_score, query_pair) for d_score in d_scores]
            d_queries = [product(key_pair[64 * one:64 * (one + 1)], d_scores[one]) for one in range(2)]
            d_query = (jnp.concatenate(d_queries, axis=0).T * 0.125).astype(LOW)
            d_key = jnp.where(lane < 64, d_keys[0], d_keys[1]).astype(LOW)
            d_value = jnp.where(lane < 64, d_values[0], d_values[1]).astype(LOW)
            for part, value in enumerate((d_query, d_key, d_value)):
                second_weights[aligned(1024 * part + seq * 256, 256, 256), lanes] = value
            rows_small[0:1, lanes] += jnp.sum(d_query.astype(F32), axis=0, keepdims=True)
            rows_small[1:2, lanes] += jnp.sum(d_value.astype(F32), axis=0, keepdims=True)

        for pair in range(6):
            d_probs = ahead
            if pair < 5:
                ahead = d_probs_of(pair + 1)
            lanes = slice(128 * pair, 128 * (pair + 1))
            weighed = d_context_t[lanes].astype(F32) * context_t[lanes, rows].astype(F32)
            probs, d_scores = [], []
            for one in range(2):
                head = 2 * pair + one
                row_sum = jnp.sum(weighed[64 * one:64 * (one + 1)], axis=0, keepdims=True)
                prob = wide[rows, 256 * head:256 * (head + 1)]
                probs.append(prob)
                d_scores.append((prob.astype(F32) * (d_probs[one] - row_sum)).astype(LOW))
            if late is not None:
                d_projected_of(*late)
            late = pair, probs, d_scores
        d_projected_of(*late)

    for seq in (2, 3):
        stage_copy(seq, 0).wait()
    for seq in (0, 1):
        stage_copy(seq, 1).start()
    x_load.wait()
    for part in range(3):
        store(9 + part, tall, second_weights[1024 * part:1024 * (part + 1), :])
        if part == 0:
            sums.relay(5)
            sums.spread(7)
        else:
            sums.cross(8 + part)

    bundle, bias_row = rows_small[...], bias_in[...]
    small[...] = jnp.zeros_like(small)
    for device in range(n):
        small[device, 0:8, 0:48] = bundle[:, 48 * device:48 * (device + 1)]
        for part in range(4):
            start = 192 * device + 48 * part
            small[device, 8 + part:9 + part, 0:48] = bias_row[:, start:start + 48]

    def small_copy(step):
        other = lax.rem(me + step, n)
        return pltpu.make_async_remote_copy(
            src_ref=small.at[other], dst_ref=small_got.at[step],
            send_sem=small_send.at[step], recv_sem=small_recv.at[step],
            device_id=(tower, other), device_id_type=MESH,
        )


    @pl.loop(1, n)
    def _(step):
        small_copy(step).start()

    def tokens(seq):
        stage_copy(seq, 1).wait()
        slot = seq % 2
        total = stage[slot]
        for part in range(3):
            total = total + transposed_right(
                second_weights[1024 * part + seq * 256:1024 * part + seq * 256 + 256, :],
                first_weights[block(part + 1), :],
            )
        stage[slot] = total
        stage_copy(seq, 2).start()

    tokens(0)
    tokens(1)
    sums.relay(6)
    sums.relay(7)
    sums.z_first_cross(8)
    sums.spread(9, straight=True)
    sums.cross(11)
    for seq in (2, 3):
        stage_copy(seq - 2, 2).wait()
        stage_copy(seq, 1).start()
    tokens(2)
    tokens(3)
    summed_small_ref[...] = small[me]

    @pl.loop(1, n)
    def _(step):
        small_copy(step).wait()
        summed_small_ref[...] += small_got[step]

    for chunk in range(3):
        sums.rows_copy(chunk).wait_recv()
    for part in range(4):
        out_ref[48 * part:48 * (part + 1)] = sums.rows_total(part)
    for chunk in range(4, 8):
        in_ref[:, block(chunk - 4)] = sums.total(chunk)
    attn_ref[...] = sums.z_first_total(8)
    sums.spread(10, straight=True)
    qkv_ref[:, block(0)] = sums.straight_total(9)
    sums.spread(11, straight=True)
    qkv_ref[:, block(1)] = sums.straight_total(10)
    qkv_ref[:, block(2)] = sums.straight_total(11)
    for seq in (2, 3):
        stage_copy(seq, 2).wait()
    sums.close()


def backward(lens, positives, datasets, pooled, gains, weights, activations, n):
    rows = activations[0].shape[0]
    anywhere = pl.BlockSpec(memory_space=pl.ANY)
    vmem = pl.BlockSpec(memory_space=pltpu.VMEM)
    scalars = pl.BlockSpec(memory_space=pltpu.SMEM)
    tile = (48, 768)
    dma = pltpu.SemaphoreType.DMA
    return pl.pallas_call(
        partial(backward_kernel, n),
        in_specs=[scalars] * 3 + [vmem] * 2 + [anywhere] * (4 + len(activations)),
        out_specs=[vmem] * 5 + [anywhere],
        out_shape=[
            jax.ShapeDtypeStruct(shape, F32)
            for shape in ((192, 768), (48, 3072), (48, 768), (48, 2304), (16, 128), (rows, 768))
        ],
        scratch_shapes=[
            pltpu.VMEM((CHUNKS, 2, 2, 4) + tile, LOW), pltpu.VMEM((CHUNKS, 2, 4) + tile, LOW),
            pltpu.VMEM((CHUNKS, 4) + tile, LOW), pltpu.VMEM((3, 4) + tile, LOW),
            pltpu.VMEM((4, 3) + tile, LOW), pltpu.VMEM((CHUNKS - 4, 3) + tile, LOW),
            pltpu.VMEM((3, 2) + tile, LOW),
            dma((CHUNKS,)), dma((CHUNKS,)), dma((CHUNKS,)), dma((CHUNKS,)), dma((CHUNKS, 3)), dma((CHUNKS, 3)),
            pltpu.VMEM((3072, 768), LOW), pltpu.VMEM((3072, 768), LOW), pltpu.VMEM((rows, 3072), LOW),
            pltpu.VMEM((768, rows), LOW), pltpu.VMEM((rows, 768), LOW), pltpu.VMEM((rows, 768), LOW),
            pltpu.VMEM((rows, 768), LOW), pltpu.VMEM((768, rows), LOW), pltpu.VMEM((768, rows), LOW),
            pltpu.VMEM((rows, 128), F32), pltpu.VMEM((2, 256, 768), F32),
            pltpu.VMEM((8, 768), F32), pltpu.VMEM((1, 3072), F32),
            pltpu.VMEM((n, 16, 128), F32), pltpu.VMEM((n, 16, 128), F32),
            pltpu.VMEM((16, 256), LOW), pltpu.VMEM((2, 2, n // 2, 16, 256), LOW), pltpu.VMEM((8, 768), F32),
            dma((34,)), dma((3, 4)), dma((n,)), dma((n,)), dma((2 * n,)), dma((2 * n,)),
        ],
        compiler_params=pltpu.CompilerParams(collective_id=1, has_side_effects=True, vmem_limit_bytes=60 * MIB),
        name="backward",
    )(lens, positives, datasets, pooled, gains, *weights, *activations)


def deliver_kernel(
    out_hbm, in_hbm, attn_hbm, qkv_hbm, small_hbm, tokens_hbm,
    out_to, in_to, attn_to, qkv_to, bias_in_to, vectors_to, gains_to, tokens_to,
    out_held, in_held, attn_held, qkv_held, small_held, held, sems,
):
    parts, rows = held.shape[0], held.shape[1]
    ways = [
        (tokens_hbm.at[pl.ds(rows * part, rows)], held.at[part], tokens_to.at[pl.ds(rows * part, rows)])
        for part in range(parts)
    ] + [
        (out_hbm, out_held, out_to), (in_hbm, in_held, in_to), (attn_hbm, attn_held, attn_to),
        (qkv_hbm, qkv_held, qkv_to),
    ]
    fetches = [
        pltpu.make_async_copy(source, middle, sems.at[0, place]) for place, (source, middle, _) in enumerate(ways)
    ]
    sends = [
        pltpu.make_async_copy(middle, target, sems.at[1, place]) for place, (_, middle, target) in enumerate(ways)
    ]
    small_fetch = pltpu.make_async_copy(small_hbm, small_held, sems.at[0, len(ways)])
    small_fetch.start()
    for fetch in fetches:
        fetch.start()
    for fetch, send in zip(fetches, sends):
        fetch.wait()
        send.start()
    small_fetch.wait()
    small = small_held[...]
    for row in range(6):
        vectors_to[row] = small[row:row + 1, :48]
    gains_to[...] = small[6:8, :48]
    bias_in_to[...] = jnp.concatenate([small[8 + part:9 + part, :48] for part in range(4)], axis=1)
    for send in sends:
        send.wait()


def deliver(*arrays):
    *sums, small, tokens = arrays
    anywhere = pl.BlockSpec(memory_space=pl.ANY)
    vmem = pl.BlockSpec(memory_space=pltpu.VMEM)
    shapes = [array.shape for array in sums] + [(1, 192), (6, 1, 48), (2, 48), tokens.shape]
    rows, width = tokens.shape
    parts = 16
    return pl.pallas_call(
        deliver_kernel,
        in_specs=[anywhere] * 6,
        out_specs=[anywhere] * 4 + [vmem] * 3 + [anywhere],
        out_shape=[jax.ShapeDtypeStruct(shape, F32) for shape in shapes],
        scratch_shapes=[pltpu.VMEM(array.shape, F32) for array in sums]
        + [pltpu.VMEM(small.shape, F32), pltpu.VMEM((parts, rows // parts, width), F32)]
        + [pltpu.SemaphoreType.DMA((2, parts + 5))],
        compiler_params=pltpu.CompilerParams(vmem_limit_bytes=60 * MIB),
        name="deliver",
    )(*arrays)


def per_device(
    n,
    tokens, lengths, positives, datasets, w_qkv, w_attn_out, w_ffn_in, w_ffn_out, b_ffn_in, biases, gains,
):
    seq_count, seq_len, width = (tokens.shape[1], tokens.shape[2], tokens.shape[3])
    lens = lengths[0]
    inputs = tokens[0].reshape(seq_count * seq_len, width)
    weights = (w_qkv, w_attn_out, w_ffn_in, w_ffn_out)
    pooled, *activations = encoder(lens, inputs, *weights, b_ffn_in, biases.transpose(1, 0, 2), gains)
    *sums, grad_tokens = backward(lens, positives, datasets, pooled, gains, weights, activations, n)
    summed_out, summed_in, summed_attn, summed_qkv, bias_in, vectors, scales, grad_tokens = deliver(*sums, grad_tokens)
    return (
        pooled[None],
        grad_tokens.reshape(1, seq_count, seq_len, width),
        summed_qkv[None],
        summed_attn[None],
        summed_in[None],
        summed_out[None],
        bias_in,
        vectors.transpose(1, 0, 2),
        scales[None],
    )


def from_behind(value, axis, steps):
    count = lax.axis_size(axis)
    leading, last = (max(0, -steps), min(count, count - steps))
    return lax.ppermute(value, axis, [(source, source + steps) for source in range(leading, last)])


def loss_gradient_plain(pooled, positives, datasets):
    seq_count = pooled.shape[0]
    mine = pooled.astype(jnp.bfloat16)
    questions = from_behind(mine, "tower", 1)
    everyone, every_set = (
        lax.all_gather(mine, "batch", axis=0, tiled=True),
        lax.all_gather(datasets.astype(jnp.bfloat16), "batch", axis=0, tiled=True),
    )
    total_seqs = everyone.shape[0]
    columns = lax.broadcasted_iota(jnp.int32, (seq_count, total_seqs), 1)
    chosen = columns == positives[:, None]
    set_row = every_set.astype(jnp.float32)[None, :]
    query_set = jnp.sum(jnp.where(chosen, set_row, 0.0), axis=1, keepdims=True)
    allowed = set_row == query_set
    question_float = questions.astype(jnp.float32)
    everyone_float = everyone.astype(jnp.float32)
    logits = jnp.dot(question_float, everyone_float.T, precision=HIGH) * SCALE
    masked = jnp.where(allowed, logits, NEG)
    softmax_rows = jnp.exp(masked - jax.nn.logsumexp(masked, axis=1, keepdims=True))
    d_logits = (softmax_rows - chosen.astype(jnp.float32)) * SCALE
    d_questions = jnp.dot(d_logits, everyone_float, precision=HIGH).astype(jnp.bfloat16)
    passage_terms = jnp.dot(d_logits.T, question_float, precision=HIGH)
    d_passages = lax.psum_scatter(passage_terms, "batch", scatter_dimension=0, tiled=True)
    returned = from_behind(d_questions, "tower", -1)
    is_passage = lax.axis_index("tower") == 1
    return jnp.where(is_passage, d_passages, returned.astype(jnp.float32))


def per_device_plain(

    tokens, lengths, positives, datasets, w_qkv, w_attn_out, w_ffn_in, w_ffn_out, b_ffn_in, biases, gains,
):
    seq_count, seq_len, width = (tokens.shape[1], tokens.shape[2], tokens.shape[3])
    head_size = width // HEADS
    rows = seq_count * seq_len
    inputs = tokens[0].reshape(rows, width)
    lens = lengths[0]
    weight_qkv = w_qkv[0]
    weight_attn = w_attn_out[0]
    weight_in = w_ffn_in[0]
    weight_out = w_ffn_out[0]
    bias_in = b_ffn_in[0]
    vectors = biases[0]
    scales = gains[0]
    positions = lax.broadcasted_iota(jnp.int32, (seq_count, seq_len), 1)
    keep = positions < lens[:, None]
    keep_float = keep.astype(jnp.float32)
    lens_float = lens.astype(jnp.float32)[:, None]
    shape_heads = (seq_count, seq_len, HEADS, head_size)
    projected = product(inputs, weight_qkv)
    query = (projected[:, :width] + vectors[0]).astype(jnp.bfloat16)
    key_rows = projected[:, width : 2 * width].astype(jnp.bfloat16)
    value = (projected[:, 2 * width :] + vectors[1]).astype(jnp.bfloat16)
    query_heads = query.reshape(shape_heads)
    key_heads = key_rows.reshape(shape_heads)
    value_heads = value.reshape(shape_heads)
    scores = scores_of(query_heads, key_heads, keep)
    log_total = jax.nn.logsumexp(scores, axis=-1, keepdims=True)
    probs_low = jnp.exp(scores - log_total).astype(jnp.bfloat16)
    context = jnp.einsum(
        "shqk,skhe->sqhe", probs_low, value_heads, preferred_element_type=jnp.float32
    )
    context = context.reshape(rows, width).astype(jnp.bfloat16)
    attended = product(context, weight_attn) + vectors[2]
    first_norm, normed_one, inverse_one = norm_forward(
        inputs.astype(jnp.float32) + attended, scales[0], vectors[3]
    )
    first_low = first_norm.astype(jnp.bfloat16)
    hidden_pre = product(first_low, weight_in) + bias_in
    hidden = jax.nn.gelu(hidden_pre, approximate=False).astype(jnp.bfloat16)
    branch = product(hidden, weight_out) + vectors[4]
    output, normed_two, inverse_two = norm_forward(first_norm + branch, scales[1], vectors[5])
    pooled = (
        jnp.sum(output.reshape(seq_count, seq_len, width) * keep_float[:, :, None], axis=1)
        / lens_float
    )
    d_pooled = loss_gradient_plain(pooled, positives, datasets)
    d_output = ((d_pooled / lens_float)[:, None, :] * keep_float[:, :, None]).reshape(rows, width)
    d_second, d_gain_two, d_shift_two = norm_backward(d_output, normed_two, inverse_two, scales[1])
    d_branch = d_second.astype(jnp.bfloat16)
    g_weight_out = transposed_left(hidden, d_branch)
    g_bias_out = jnp.sum(d_branch.astype(jnp.float32), axis=0)
    d_hidden = transposed_right(d_branch, weight_out)
    gelu_pull = jax.vjp(partial(jax.nn.gelu, approximate=False), hidden_pre)[1]
    d_pre = gelu_pull(d_hidden)[0].astype(jnp.bfloat16)
    g_weight_in = transposed_left(first_low, d_pre)
    g_bias_in = jnp.sum(d_pre.astype(jnp.float32), axis=0)
    d_first = d_second + transposed_right(d_pre, weight_in)
    d_sum_one, d_gain_one, d_shift_one = norm_backward(d_first, normed_one, inverse_one, scales[0])
    d_attended = d_sum_one.astype(jnp.bfloat16)
    g_weight_attn = transposed_left(context, d_attended)
    g_bias_attn = jnp.sum(d_attended.astype(jnp.float32), axis=0)
    d_context = transposed_right(d_attended, weight_attn).astype(jnp.bfloat16).reshape(shape_heads)
    again = scores_of(query_heads, key_heads, keep)
    probs = jnp.exp(again - log_total)
    d_value = jnp.einsum(
        "shqk,sqhe->skhe", probs.astype(jnp.bfloat16), d_context, preferred_element_type=jnp.float32
    )
    d_probs = jnp.einsum(
        "sqhe,skhe->shqk", d_context, value_heads, preferred_element_type=jnp.float32
    )
    d_scores = (probs * (d_probs - jnp.sum(d_probs * probs, axis=-1, keepdims=True))).astype(
        jnp.bfloat16
    )
    d_query = (
        jnp.einsum("shqk,skhe->sqhe", d_scores, key_heads, preferred_element_type=jnp.float32)
        * 0.125
    )
    d_key = (
        jnp.einsum("shqk,sqhe->skhe", d_scores, query_heads, preferred_element_type=jnp.float32)
        * 0.125
    )
    d_query_low = d_query.reshape(rows, width).astype(jnp.bfloat16)
    d_key_low = d_key.reshape(rows, width).astype(jnp.bfloat16)
    d_value_low = d_value.reshape(rows, width).astype(jnp.bfloat16)
    d_projected = jnp.concatenate([d_query_low, d_key_low, d_value_low], axis=1)
    g_weight_qkv = transposed_left(inputs, d_projected)
    g_bias_query = jnp.sum(d_query_low.astype(jnp.float32), axis=0)
    g_bias_value = jnp.sum(d_value_low.astype(jnp.float32), axis=0)
    d_inputs = d_sum_one + transposed_right(d_projected, weight_qkv)
    g_vectors = jnp.stack(
        [g_bias_query, g_bias_value, g_bias_attn, d_shift_one, g_bias_out, d_shift_two]
    )
    g_scales = jnp.stack([d_gain_one, d_gain_two])

    def scatter(value, dimension):
        return lax.psum_scatter(value, "batch", scatter_dimension=dimension, tiled=True)

    summed_qkv, summed_attn, summed_in, summed_out = (
        scatter(g_weight_qkv, 0), scatter(g_weight_attn, 0), scatter(g_weight_in, 0), scatter(g_weight_out, 0)
    )
    summed_bias_in, summed_vectors, summed_scales = (
        scatter(g_bias_in, 0), scatter(g_vectors, 1), scatter(g_scales, 1)
    )
    return (
        pooled[None],
        d_inputs.reshape(1, seq_count, seq_len, width),
        summed_qkv[None],
        summed_attn[None],
        summed_in[None],
        summed_out[None],
        summed_bias_in[None],
        summed_vectors[None],
        summed_scales[None],
    )


def solution(mesh):
    n = mesh.shape["batch"]
    direct = n == 16
    in_specs = (
        P("tower", "batch", None, None),
        P("tower", "batch"),
        P("batch"),
        P("batch"),
        P("tower", None, None),
        P("tower", None, None),
        P("tower", None, None),
        P("tower", None, None),
        P("tower", None),
        P("tower", None, None),
        P("tower", None, None),
    )
    out_specs = (
        P("tower", "batch", None),
        P("tower", "batch", None, None),
        P("tower", "batch", None),
        P("tower", "batch", None),
        P("tower", "batch", None),
        P("tower", "batch", None),
        P("tower", "batch"),
        P("tower", None, "batch"),
        P("tower", None, "batch"),
    )
    return jax.shard_map(
        partial(per_device, n) if direct else per_device_plain, mesh=mesh, in_specs=in_specs, out_specs=out_specs, check_vma=False
    )
```
